256 devices in a mesh: space: 32 (over z, x_lo, core), inj: 8 (over y, x_hi).
Axes of the slice: x: 4 (x_hi: 2, x_lo: 2; x = x_hi * 2 + x_lo), y: 4, z: 8, core: 2. Of those that a mesh axis runs over, the one named last changes fastest.
Arguments:
- conductivity: float32 [192, 64, 128], P('space'), may hold values from 0.05 to 2
- start_potential: float32 [16, 192, 64, 128], P('inj', 'space'), may hold values from -6 to 6
- start_adjoint: float32 [16, 192, 64, 128], P('inj', 'space'), may hold values from -6 to 6
- inj_cells: int32 [16, 2], P('inj'), may hold values from 0 to 1572863
- dipole_cells: int32 [8, 1024, 2, 128], P('inj', 'space'), may hold values from 0 to 49151
- owner_tile: int32 [8, 1024, 1], P('inj', 'space'), may hold values from 0 to 31; in each aligned block of 32 rows (0 to 31, 32 to 63, ..., all dimensions but the last counted through in order) at most 2 rows name the same one
- live_count: int32 [8, 1024], P('inj', 'space'), may hold values from 1 to 128, 81920 in all within a row
- observed: float32 [8, 1024, 2, 128], P('inj', 'space'), may hold values from -6 to 6
Outputs:
- gradient: float32 [192, 64, 128], P('space', 'inj')
- residual: float32 [8, 1024, 2, 128], P('inj', 'space')
The draws below stay inside these ranges and needn't reach their ends.
Inputs may be any that keep to these rules, and one draw needn't show every extreme that they name: `owner_tile`: of the rows of one device, no more than 2 name the same tile, and on some device some tile is named by exactly 2 rows. The first live_count slots of a block are in use, the rest are padding.
All inputs are finite; a program needn't handle non-finite values.
Results may differ from the reference program's by a relative error of at most 0.0003.
Values sent between devices are 32-bit elements; how exact they have to be, the bound alone decides.
A program may use at most 128 MiB of HBM per device.

```python
import math
import jax
import jax.numpy as jnp
import numpy as np
from jax import lax

CX = 6
NY = 64
NZ = 128
INJ_G = 2
ELEC = 128
BLK_DEV = 32
CAP = 2
NX = 192
GROUPS = 8
INJECTIONS = 16
SBLK = 1024
N_SPACE = 32


def set_ends(drawn, key, low, largest):
    dims = drawn.shape
    spot = [jax.random.randint(jax.random.fold_in(key, axis), (), 0, dims[axis]) for axis in range(len(dims))]
    drawn = drawn.at[tuple(spot)].set(low)
    longest = dims.index(max(dims))
    spot[longest] = (spot[longest] + 1) % dims[longest]
    return drawn.at[tuple(spot)].set(largest)


def shard_levels(stream_key, dims, cuts, low, largest):
    gain, own = 1.0, jax.random.fold_in(stream_key, 6)
    for position, shards_of in cuts:
        draws = jnp.exp(jax.random.uniform(jax.random.fold_in(own, position), (shards_of,), jnp.float32, low / len(cuts), largest / len(cuts)))
        gain = gain * jnp.repeat(draws, dims[position] // shards_of).reshape([-1 if axis == position else 1 for axis in range(len(dims))])
    return gain


def profile(count, total, limit, lean):
    weights = [(1 << 20) // math.isqrt(standing ** lean) + 1 for standing in range(2, count + 1)]
    surplus, holding = total - limit - (count - 1), [1] * (count - 1)
    while surplus > 0:
        free = [i for i in range(count - 1) if holding[i] < limit]
        whole, left = sum([weights[i] for i in free]), surplus
        for i in free:
            more = min(limit - holding[i], max(1, left * weights[i] // whole), surplus)
            holding[i] = holding[i] + more
            surplus = surplus - more
    return np.array([limit] + holding)


def ragged(own_key, count, total, most, slope):
    if count == 2:
        one = jax.random.randint(own_key, (), max(1, total - most), min(most, total - 1) + 1)
        return jnp.stack([one, total - one])
    tallies = jnp.asarray(profile(count, total, most, slope), jnp.int32)
    couples = (count - 1) // 2
    giver, taker = tallies[1:1 + 2 * couples:2], tallies[2:2 + 2 * couples:2]
    room = jnp.minimum(giver - 1, most - taker)
    shifted = jax.random.randint(jax.random.fold_in(own_key, 1), (couples,), 0, 1 << 20) % (room + 1)
    tallies = tallies.at[1:1 + 2 * couples:2].set(giver - shifted).at[2:2 + 2 * couples:2].set(taker + shifted)
    return tallies[jax.random.permutation(jax.random.fold_in(own_key, 2), count)]


def deal_out(rng, own, number, rows, count, top, most, skew):
    ranking = jax.random.permutation(rng, count)
    packed, common = shares(count, rows * top, most, skew, True), shares(count, rows * top, most, skew, False)
    places = jnp.arange(count)

    def named(tallies, rotation):
        used = int((tallies > 0).sum())
        fixed = max(1, used // 4)
        moved = fixed + (places - fixed + rotation * (used - fixed)) % max(1, count - fixed)
        return jnp.zeros((count,), jnp.int32).at[ranking[jnp.where(places < fixed, places, moved)]].set(jnp.asarray(tallies, jnp.int32))

    tallies = jnp.where(number % 4 == 0, named(packed, number // 4), named(common, number - number // 4 - 1))
    mixed = jax.random.permutation(jax.random.fold_in(own, 3), count)
    giver, taker = mixed[0:count // 2 * 2:2], mixed[1:count // 2 * 2:2]
    room = jnp.minimum(tallies[giver] - 1, most - tallies[taker]) // 2
    room = jnp.where((giver == ranking[0]) | (taker == ranking[0]) | (tallies[taker] == 0), 0, jnp.maximum(room, 0))
    moved = jax.random.randint(jax.random.fold_in(own, 4), (count // 2,), 0, 1 << 20) % (room + 1)
    tallies = tallies.at[giver].add(-moved).at[taker].add(moved)
    items = jnp.searchsorted(jnp.cumsum(tallies), jnp.arange(rows * top), side="right").astype(jnp.int32)
    grid = items.reshape(top, rows).T
    grid = grid[jax.random.permutation(jax.random.fold_in(own, 1), rows)]
    rotation = jax.random.randint(jax.random.fold_in(own, 2), (rows, 1), 0, top)
    return jnp.take_along_axis(grid, (jnp.arange(top)[None, :] + rotation) % top, axis=1)


def shares(amount, total, reach, slope, full):
    weights = [(1 << 20) // math.isqrt(standing ** slope) + 1 for standing in range(1, amount + 1)]
    largest = reach if full else min(reach, max(-(-total // amount), total * weights[0] // sum(weights)))
    least = 1 if total - largest >= amount - 1 else 0
    holding, spare = [largest] + [least] * (amount - 1), total - largest - least * (amount - 1)
    while spare > 0:
        movable = [i for i in range(1, amount) if holding[i] < largest] or [i for i in range(1, amount) if holding[i] < reach]
        pool, budget = sum([weights[i] for i in movable]), spare
        for i in movable:
            extra = min(reach - holding[i], max(1, budget * weights[i] // pool), spare)
            holding[i] = holding[i] + extra
            spare = spare - extra
    return np.array(holding)


def scatter_about(own_key, extent, spread, limit, split=(), kind=jnp.bfloat16):
    entries = jax.random.normal(own_key, extent, jnp.float32) * spread
    if len(split) > 0:
        entries = shard_levels(own_key, extent, split, -0.22, 0.18) * entries
    return jnp.clip(entries, min=-limit, max=limit).astype(kind)


def setup_inputs(seed: int = 0) -> dict:
    arg_keys = jax.random.split(jax.random.key(seed), 9)
    conductivity = jnp.clip(jnp.exp(math.log(2.0) - 3.6888794 * jax.random.uniform(arg_keys[0], (NX, NY, NZ), jnp.float32) ** shard_levels(arg_keys[0], (NX, NY, NZ), ((0, 32),), -0.2, 0.2)), 0.05, 2.0)
    start_potential = scatter_about(arg_keys[1], (INJECTIONS, NX, NY, NZ), 1.0, 6.0, ((0, 8), (1, 32)), jnp.float32)
    start_adjoint = scatter_about(arg_keys[2], (INJECTIONS, NX, NY, NZ), 1.0, 6.0, ((0, 8), (1, 32)), jnp.float32)
    inj_cells = set_ends(jax.random.randint(arg_keys[3], (INJECTIONS, 2), 0, NX * NY * NZ), jax.random.fold_in(arg_keys[3], 1), 0, (NX * NY * NZ) - 1).astype(jnp.int32)
    dipole_cells = set_ends(jax.random.randint(arg_keys[4], (GROUPS, SBLK, 2, ELEC), 0, CX * NY * NZ), jax.random.fold_in(arg_keys[4], 1), 0, (CX * NY * NZ) - 1).astype(jnp.int32)
    owner_tile_keys = jax.random.split(jax.random.fold_in(arg_keys[5], 1), GROUPS * SBLK // BLK_DEV)
    owner_tile_turns = jax.random.permutation(jax.random.fold_in(arg_keys[5], 3), GROUPS * SBLK // BLK_DEV)
    owner_tile = jax.vmap(lambda own, number: deal_out(jax.random.fold_in(arg_keys[5], 2), own, number, BLK_DEV, N_SPACE, 1, CAP, 2))(owner_tile_keys, owner_tile_turns).reshape((GROUPS, SBLK, 1))
    live_count = jax.vmap(lambda own: ragged(own, SBLK, SBLK * ELEC * 5 // 8, ELEC, 1))(jax.random.split(arg_keys[6], GROUPS)).reshape((GROUPS, SBLK)).astype(jnp.int32)
    observed = scatter_about(arg_keys[7], (GROUPS, SBLK, INJ_G, ELEC), 1.0, 6.0, ((0, 8), (1, 32)), jnp.float32)
    return {"conductivity": conductivity, "start_potential": start_potential, "start_adjoint": start_adjoint, "inj_cells": inj_cells, "dipole_cells": dipole_cells, "owner_tile": owner_tile, "live_count": live_count, "observed": observed}


current_amp = 4.0
sweep_weights = [1.0 / (1.0 + 0.9 * math.cos((2 * step_k + 1) * math.pi / 6.0)) for step_k in range(3)]


def forward_cell(values, which_axis):
    length = values.shape[which_axis]
    interior = lax.slice_in_dim(values, 1, length, axis=which_axis)
    border = jnp.zeros_like(lax.slice_in_dim(values, 0, 1, axis=which_axis))
    return jnp.concatenate([interior, border], axis=which_axis)


def backward_cell(values, which_axis):
    length = values.shape[which_axis]
    interior = lax.slice_in_dim(values, 0, length - 1, axis=which_axis)
    border = jnp.zeros_like(lax.slice_in_dim(values, 0, 1, axis=which_axis))
    return jnp.concatenate([border, interior], axis=which_axis)


def conductances(sigma):
    face_xp = 0.5 * (sigma + forward_cell(sigma, 0))
    face_xm = 0.5 * (sigma + backward_cell(sigma, 0))
    face_yp = 0.5 * (sigma + forward_cell(sigma, 1))
    face_ym = 0.5 * (sigma + backward_cell(sigma, 1))
    face_zp = 0.5 * (sigma + forward_cell(sigma, 2))
    face_zm = 0.5 * (sigma + backward_cell(sigma, 2))
    diagonal = face_xp + face_xm + face_yp + face_ym + face_zp + face_zm
    return (face_xp, face_xm, face_yp, face_ym, face_zp, face_zm, diagonal)


def operate(values, faces, leading):
    beside_all = faces[0] * forward_cell(values, leading) + faces[1] * backward_cell(values, leading)
    beside_all = beside_all + faces[2] * forward_cell(values, leading + 1) + faces[3] * backward_cell(values, leading + 1)
    beside_all = beside_all + faces[4] * forward_cell(values, leading + 2) + faces[5] * backward_cell(values, leading + 2)
    return faces[6] * values - beside_all


def relax(potential, source, faces):
    for weight in sweep_weights:
        potential = potential + weight * ((source - operate(potential, faces, 0)) / faces[6])
    return potential


def adjoint_term(potential, adjoint):
    total = jnp.zeros_like(potential)
    for leading in range(3):
        for mover in (forward_cell, backward_cell):
            total = total + (potential - mover(potential, leading)) * (adjoint - mover(adjoint, leading))
    return -0.5 * total


def reference(conductivity, start_potential, start_adjoint, inj_cells, dipole_cells, owner_tile, live_count, observed):
    faces = conductances(conductivity)
    cell_total = NX * NY * NZ
    base = owner_tile[:, :, 0] * (CX * NY * NZ)
    pos_plus = (base[:, :, None] + dipole_cells[:, :, 0, :]).astype(jnp.int32)
    pos_minus = (base[:, :, None] + dipole_cells[:, :, 1, :]).astype(jnp.int32)
    live_mask = jnp.arange(ELEC, dtype=jnp.int32)[None, None, :] < live_count[:, :, None]

    def one_injection(gradient, index):
        group = index // INJ_G
        local = index % INJ_G
        source = jnp.zeros((cell_total,), jnp.float32)
        source = source.at[inj_cells[index, 0]].add(current_amp).at[inj_cells[index, 1]].add(-current_amp)
        potential = relax(start_potential[index], source.reshape(NX, NY, NZ), faces)
        flat_potential = potential.reshape(-1)
        plus_ids = pos_plus[group]
        minus_ids = pos_minus[group]
        measured = observed[group][:, local, :]
        misfit = jnp.where(live_mask[group], flat_potential[plus_ids] - flat_potential[minus_ids] - measured, 0.0)
        adjoint_source = jnp.zeros((cell_total,), jnp.float32)
        adjoint_source = adjoint_source.at[plus_ids.reshape(-1)].add(misfit.reshape(-1))
        adjoint_source = adjoint_source.at[minus_ids.reshape(-1)].add(-misfit.reshape(-1))
        adjoint = relax(start_adjoint[index], adjoint_source.reshape(NX, NY, NZ), faces)
        return gradient + adjoint_term(potential, adjoint), misfit

    gradient, misfits = lax.scan(one_injection, jnp.zeros((NX, NY, NZ), jnp.float32), jnp.arange(INJECTIONS, dtype=jnp.int32))
    residual = misfits.reshape(GROUPS, INJ_G, SBLK, ELEC).transpose(0, 2, 1, 3)
    return gradient, residual
```

```python
import functools
import math

import jax
import jax.numpy as jnp
from jax import lax
from jax.experimental import pallas as pl
from jax.experimental.pallas import tpu as pltpu
from jax.sharding import PartitionSpec as P

MESH = pl.DeviceIdType.MESH
F32 = jnp.float32
BF16 = jnp.bfloat16
HIGHEST = lax.Precision.HIGHEST

current_amp = 4.0
sweep_weights = [
    1.0 / (1.0 + 0.9 * math.cos((2 * step_k + 1) * math.pi / 6.0)) for step_k in range(3)
]

H = 4
PAD = 8


def iota(shape, dim):
    return lax.broadcasted_iota(jnp.int32, shape, dim)


def rows_sum(values):
    return jnp.sum(values, axis=0, keepdims=True)


def kernel(
    n_space, n_inj, nx, ny, nz, blocks,
    sig_in, pot_in, adj_in, inj_cells, owner, live, cells, observed,
    grad_out, res_out,
    sigma, pa, pb, aa, ab, coef, src, asrc, send, recv, ret_send, ret_recv,
    rim, onehot, table, scat, partial, shares,
    local_sem, halo_send, halo_recv, far_send, far_recv, block_send, block_recv,
    ret_send_sem, ret_recv_sem, rim_send, rim_recv, asrc_send, asrc_recv, share_send, share_recv,
):
    me = lax.axis_index("space")
    my_inj = lax.axis_index("inj")
    left = lax.rem(me + n_space - 1, n_space)
    right = lax.rem(me + 1, n_space)
    planes = nx + 2 * H
    rows = pl.ds(PAD, ny)
    half = nx // 2
    tall = half * ny
    wide = 2 * nz
    half_cells = float(half * ny * nz)

    barrier = pltpu.get_barrier_semaphore()

    def greet(d, carry):
        pl.semaphore_signal(barrier, inc=1, device_id=(lax.rem(me + d, n_space), my_inj), device_id_type=MESH)
        return carry

    def greet_inj(d, carry):
        pl.semaphore_signal(barrier, inc=1, device_id=(me, lax.rem(my_inj + d, n_inj)), device_id_type=MESH)
        return carry

    lax.fori_loop(1, n_space, greet, 0)
    lax.fori_loop(1, n_inj, greet_inj, 0)

    locals_ = [
        pltpu.make_async_copy(sig_in, sigma.at[pl.ds(H, nx), rows], local_sem.at[0]),
        pltpu.make_async_copy(pot_in, pa.at[:, pl.ds(H, nx), rows], local_sem.at[1]),
        pltpu.make_async_copy(adj_in, aa.at[:, pl.ds(H, nx), rows], local_sem.at[2]),
    ]
    for copy in locals_:
        copy.start()

    edge = jnp.zeros((PAD, nz), F32)

    def clear(p, carry):
        for low in (0, PAD + ny):
            sigma[p, pl.ds(low, PAD), :] = edge
            for i in range(2):
                for buf in (pa, pb, aa, ab):
                    buf[i, p, pl.ds(low, PAD), :] = edge
        return carry

    lax.fori_loop(0, planes, clear, 0)

    lanes = 4 * blocks
    lane_c = iota((blocks, lanes), 1)
    block_c = lax.rem(lane_c, 2 * blocks) // 2
    field_c = lax.rem(lane_c, 2) + 2 * (lane_c // (2 * blocks))
    row_b = iota((blocks, lanes), 0)
    owners = jnp.broadcast_to(owner[...].astype(F32), (blocks, lanes))
    owner_c = rows_sum(jnp.where(row_b == block_c, owners, 0.0))
    earlier = (owners == owner_c) & (row_b < block_c)
    rank_c = rows_sum(jnp.where(earlier, 1.0, 0.0))
    slot_c = owner_c * 2.0 + rank_c
    target = slot_c * 4.0 + field_c[:1].astype(F32)
    place = jnp.where(iota((n_space * 8, lanes), 0).astype(F32) == target, 1.0, 0.0)

    row_r = iota((lanes, blocks), 0)
    block_r = lax.rem(row_r, 2 * blocks) // 2
    lives = jnp.broadcast_to(live[...].astype(F32), (lanes, blocks))
    live_r = jnp.sum(jnp.where(block_r == iota((lanes, blocks), 1), lives, 0.0), axis=1, keepdims=True)
    data = jnp.concatenate([cells[...].astype(F32) + 1.0, observed[...]], axis=0)
    elec = data.shape[1]
    data = jnp.where(iota((lanes, elec), 1).astype(F32) < live_r, data, 0.0)
    packed = jnp.dot(place, data, precision=HIGHEST, preferred_element_type=F32)
    for t in range(n_space):
        send[t] = packed[8 * t : 8 * t + 8]

    pl.semaphore_wait(barrier, n_space - 1 + n_inj - 1)

    def remote(source, target, send_sem, recv_sem, space, inj):
        return pltpu.make_async_remote_copy(
            src_ref=source, dst_ref=target, send_sem=send_sem, recv_sem=recv_sem,
            device_id=(space, inj), device_id_type=MESH,
        )

    early = [
        remote(sig_in.at[pl.ds(nx - H, H)], sigma.at[pl.ds(0, H), rows], halo_send.at[0], halo_recv.at[0], right, my_inj),
        remote(sig_in.at[pl.ds(0, H)], sigma.at[pl.ds(nx + H, H), rows], halo_send.at[1], halo_recv.at[1], left, my_inj),
        remote(pot_in.at[:, pl.ds(nx - 3, 3)], pa.at[:, pl.ds(H - 3, 3), rows], halo_send.at[2], halo_recv.at[2], right, my_inj),
        remote(pot_in.at[:, pl.ds(0, 3)], pa.at[:, pl.ds(nx + H, 3), rows], halo_send.at[3], halo_recv.at[3], left, my_inj),
    ]
    late = [
        remote(adj_in.at[:, pl.ds(nx - H, H)], aa.at[:, pl.ds(0, H), rows], far_send.at[0], far_recv.at[0], right, my_inj),
        remote(adj_in.at[:, pl.ds(0, H)], aa.at[:, pl.ds(nx + H, H), rows], far_send.at[1], far_recv.at[1], left, my_inj),
    ]
    for copy in early:
        copy.start()

    def send_block(d, carry):
        to = lax.rem(me + d, n_space)
        remote(send.at[to], recv.at[me], block_send, block_recv, to, my_inj).start()
        return carry

    lax.fori_loop(1, n_space, send_block, 0)
    for copy in late:
        copy.start()
    recv[me] = send[me]

    cell_ids = iota((ny, nz), 0) * nz + iota((ny, nz), 1)

    def own_source(p, carry):
        first = (me * nx - H + p) * (ny * nz)
        for i in range(2):
            plus = jnp.where(cell_ids == inj_cells[i, 0] - first, current_amp, 0.0)
            minus = jnp.where(cell_ids == inj_cells[i, 1] - first, current_amp, 0.0)
            src[i, p] = plus - minus
        return carry

    lax.fori_loop(0, planes, own_source, 0)

    def no_halo(buf, lead):
        nothing = jnp.zeros((ny, nz), F32)

        @pl.when(me == 0)
        def _():
            for p in range(H):
                for i in range(lead):
                    if lead == 1:
                        buf[p, rows, :] = nothing
                    else:
                        buf[i, p, rows, :] = nothing

        @pl.when(me == n_space - 1)
        def _():
            for p in range(nx + H, planes):
                for i in range(lead):
                    if lead == 1:
                        buf[p, rows, :] = nothing
                    else:
                        buf[i, p, rows, :] = nothing

    first_lane = iota((ny, nz), 1) == 0
    last_lane = iota((ny, nz), 1) == nz - 1

    locals_[0].wait()
    early[0].wait()
    early[1].wait()
    no_halo(sigma, 1)

    def faces(p, carry):
        here = sigma[p, rows, :]
        zp = jnp.where(last_lane, 0.0, pltpu.roll(here, nz - 1, 1))
        zm = jnp.where(first_lane, 0.0, pltpu.roll(here, 1, 1))
        around = [
            sigma[p + 1, rows, :], sigma[p - 1, rows, :],
            sigma[p, pl.ds(PAD + 1, ny), :], sigma[p, pl.ds(PAD - 1, ny), :], zp, zm,
        ]
        around = [0.5 * (here + value) for value in around]
        diag = around[0] + around[1] + around[2] + around[3] + around[4] + around[5]
        plane = me * nx - H + p
        inside = jnp.where((plane >= 0) & (plane < n_space * nx), 1.0, 0.0)
        inverse = inside / jnp.where(diag > 0.0, diag, 1.0)
        around[4] = jnp.where(last_lane, 0.0, around[4])
        around[5] = jnp.where(first_lane, 0.0, around[5])
        for k in range(6):
            coef[k, p] = around[k] * inverse
        coef[6, p] = inverse
        return carry

    lax.fori_loop(1, planes - 1, faces, 0)

    def sweep(source, old, new, low, high, weight):
        def plane(p, carry):
            c = [coef[k, p] for k in range(7)]
            for i in range(2):
                here = old[i, p, rows, :]
                beside = c[0] * old[i, p + 1, rows, :] + c[1] * old[i, p - 1, rows, :]
                beside = beside + (
                    c[2] * old[i, p, pl.ds(PAD + 1, ny), :] + c[3] * old[i, p, pl.ds(PAD - 1, ny), :]
                )
                beside = beside + (c[4] * pltpu.roll(here, nz - 1, 1) + c[5] * pltpu.roll(here, 1, 1))
                beside = beside + c[6] * source[i, p]
                new[i, p, rows, :] = here + weight * (beside - here)
            return carry

        lax.fori_loop(low, high, plane, 0)

    locals_[1].wait()
    early[2].wait()
    early[3].wait()
    no_halo(pa, 2)
    sweep(src, pa, pb, 2, planes - 2, sweep_weights[0])
    sweep(src, pb, pa, 3, planes - 3, sweep_weights[1])
    sweep(src, pa, pb, H, planes - H, sweep_weights[2])

    rims = [
        remote(pb.at[:, H + nx - 1, rows], rim.at[0], rim_send.at[0], rim_recv.at[0], right, my_inj),
        remote(pb.at[:, H, rows], rim.at[1], rim_send.at[1], rim_recv.at[1], left, my_inj),
    ]
    for copy in rims:
        copy.start()

    for i in range(2):
        for x in range(nx):
            value = pb[i, H + x, rows, :]
            high = value.astype(BF16)
            low = (value - high.astype(F32)).astype(BF16)
            at = (pl.ds(i * tall + (x % half) * ny, ny))
            table[at, pl.ds((x // half) * nz, nz)] = high
            table[at, pl.ds(wide + (x // half) * nz, nz)] = low

    got = pltpu.make_async_copy(recv.at[pl.ds(0, n_space - 1)], recv.at[pl.ds(0, n_space - 1)], block_recv)
    got.wait()

    wide_iota = iota((wide, elec), 0).astype(F32).astype(BF16)
    tall_iota = iota((tall, elec), 0).astype(F32)
    tall_iota16 = tall_iota.astype(BF16)
    one = jnp.ones((wide, elec), BF16)
    none = jnp.zeros((wide, elec), BF16)

    def split_cells(t):
        cell = recv[t] - 1.0
        upper = cell >= half_cells
        within = jnp.where(upper, cell - half_cells, cell)
        tall_at = jnp.floor(within * (1.0 / nz))
        wide_at = within - tall_at * nz + jnp.where(upper, float(nz), 0.0)
        return tall_at, jnp.where(cell < 0.0, -1.0, wide_at)

    def fetch(t, carry):
        tall_at, wide_at = split_cells(t)
        for s in range(2):
            for f in range(2):
                row = jnp.broadcast_to(wide_at[4 * s + f : 4 * s + f + 1], (wide, elec)).astype(BF16)
                onehot[t, :, pl.ds((2 * s + f) * elec, elec)] = jnp.where(wide_iota == row, one, none)
        hot = onehot[t]
        found = jnp.dot(table[:, :wide], hot, preferred_element_type=F32)
        found = found + jnp.dot(table[:, wide:], hot, preferred_element_type=F32)
        out = []
        for s in range(2):
            ends = [[], []]
            for f in range(2):
                row = tall_at[4 * s + f : 4 * s + f + 1]
                here = tall_iota == row
                for i in range(2):
                    piece = found[i * tall : (i + 1) * tall, (2 * s + f) * elec : (2 * s + f + 1) * elec]
                    ends[i].append(rows_sum(jnp.where(here, piece, 0.0)))
            for i in range(2):
                out.append(ends[i][0] - ends[i][1] - recv[t, pl.ds(4 * s + 2 + i, 1), :])
        ret_send[t] = jnp.concatenate(out, axis=0)
        return carry

    lax.fori_loop(0, n_space, fetch, 0)

    def send_ret(d, carry):
        to = lax.rem(me + d, n_space)
        remote(ret_send.at[to], ret_recv.at[me], ret_send_sem, ret_recv_sem, to, my_inj).start()
        return carry

    lax.fori_loop(1, n_space, send_ret, 0)
    ret_recv[me] = ret_send[me]

    scat[...] = jnp.zeros_like(scat)

    def spread(t, carry):
        tall_at, _ = split_cells(t)
        misfit = ret_send[t]
        high = misfit.astype(BF16).astype(F32)
        low = misfit - high
        columns = [[], []]
        for s in range(2):
            for f in range(2):
                sign = 1.0 if f == 0 else -1.0
                row = jnp.broadcast_to(tall_at[4 * s + f : 4 * s + f + 1], (tall, elec)).astype(BF16)
                here = tall_iota16 == row
                for part, value in enumerate((high, low)):
                    pieces = []
                    for i in range(2):
                        amount = jnp.broadcast_to(sign * value[2 * s + i : 2 * s + i + 1], (tall, elec)).astype(BF16)
                        pieces.append(jnp.where(here, amount, jnp.zeros((tall, elec), BF16)))
                    columns[part].append(jnp.concatenate(pieces, axis=0))
        hot = onehot[t]
        total = scat[...]
        for part in range(2):
            total = total + lax.dot_general(
                jnp.concatenate(columns[part], axis=1), hot, (((1,), (1,)), ((), ())),
                preferred_element_type=F32,
            )
        scat[...] = total
        return carry

    lax.fori_loop(0, n_space, spread, 0)
    for i in range(2):
        for x in range(nx):
            asrc[i, H + x] = scat[pl.ds(i * tall + (x % half) * ny, ny), pl.ds((x // half) * nz, nz)]
    around = [
        remote(asrc.at[:, pl.ds(H + nx - 3, 3)], asrc.at[:, pl.ds(1, 3)], asrc_send.at[0], asrc_recv.at[0], right, my_inj),
        remote(asrc.at[:, pl.ds(H, 3)], asrc.at[:, pl.ds(H + nx, 3)], asrc_send.at[1], asrc_recv.at[1], left, my_inj),
    ]
    for copy in around:
        copy.start()

    locals_[2].wait()
    late[0].wait()
    late[1].wait()
    no_halo(aa, 2)
    for copy in rims:
        copy.wait()
    for i in range(2):
        pb[i, H - 1, rows, :] = jnp.where(me == 0, 0.0, rim[0, i])
        pb[i, H + nx, rows, :] = jnp.where(me == n_space - 1, 0.0, rim[1, i])

    for copy in around:
        copy.wait()
    sweep(asrc, aa, ab, 1, planes - 1, sweep_weights[0])
    sweep(asrc, ab, aa, 2, planes - 2, sweep_weights[1])
    sweep(asrc, aa, ab, 3, planes - 3, sweep_weights[2])

    def term(x, carry):
        p = x + H
        total = jnp.zeros((ny, nz), F32)
        for i in range(2):
            here, there = pb[i, p, rows, :], ab[i, p, rows, :]
            pairs = [
                (pb[i, p + 1, rows, :], ab[i, p + 1, rows, :]),
                (pb[i, p - 1, rows, :], ab[i, p - 1, rows, :]),
                (pb[i, p, pl.ds(PAD + 1, ny), :], ab[i, p, pl.ds(PAD + 1, ny), :]),
                (pb[i, p, pl.ds(PAD - 1, ny), :], ab[i, p, pl.ds(PAD - 1, ny), :]),
                tuple(jnp.where(last_lane, 0.0, pltpu.roll(v, nz - 1, 1)) for v in (here, there)),
                tuple(jnp.where(first_lane, 0.0, pltpu.roll(v, 1, 1)) for v in (here, there)),
            ]
            for u, v in pairs:
                total = total + (here - u) * (there - v)
        partial[:, x] = (-0.5 * total).reshape(n_inj, ny // n_inj, nz)
        return carry

    lax.fori_loop(0, nx, term, 0)

    def send_share(d, carry):
        to = lax.rem(my_inj + d, n_inj)
        remote(partial.at[to], shares.at[my_inj], share_send, share_recv, me, to).start()
        return carry

    lax.fori_loop(1, n_inj, send_share, 0)
    shares[my_inj] = partial[my_inj]

    ret_got = pltpu.make_async_copy(ret_recv.at[pl.ds(0, n_space - 1)], ret_recv.at[pl.ds(0, n_space - 1)], ret_recv_sem)
    ret_got.wait()
    lane_j = lax.rem(iota((1, lanes), 1), 2).astype(F32)
    back = jnp.where(iota((n_space * 4, lanes), 0).astype(F32) == slot_c * 2.0 + lane_j, 1.0, 0.0)
    back = jnp.transpose(back)[: 2 * blocks]
    returned = jnp.concatenate([ret_recv[t] for t in range(n_space)], axis=0)
    res_out[...] = jnp.dot(back, returned, precision=HIGHEST, preferred_element_type=F32)

    share_got = pltpu.make_async_copy(shares.at[pl.ds(0, n_inj - 1)], shares.at[pl.ds(0, n_inj - 1)], share_recv)
    share_got.wait()
    total = shares[0]
    for k in range(1, n_inj):
        total = total + shares[k]
    grad_out[...] = total

    pltpu.make_async_copy(send.at[pl.ds(0, n_space - 1)], send.at[pl.ds(0, n_space - 1)], block_send).wait()
    pltpu.make_async_copy(ret_send.at[pl.ds(0, n_space - 1)], ret_send.at[pl.ds(0, n_space - 1)], ret_send_sem).wait()
    pltpu.make_async_copy(partial.at[pl.ds(0, n_inj - 1)], partial.at[pl.ds(0, n_inj - 1)], share_send).wait()


def body(
    conductivity, start_potential, start_adjoint, inj_cells, dipole_cells, owner_tile, live_count, observed,
):
    n_space, n_inj = lax.axis_size("space"), lax.axis_size("inj")
    nx, ny, nz = conductivity.shape
    blocks, elec = observed.shape[1], observed.shape[3]
    planes, tall_rows = nx + 2 * H, ny + 2 * PAD
    wide, tall = 2 * nz, nx // 2 * ny
    anywhere = pl.BlockSpec(memory_space=pl.ANY)
    vmem = pl.BlockSpec(memory_space=pltpu.VMEM)
    smem = pl.BlockSpec(memory_space=pltpu.SMEM)
    field = pltpu.VMEM((2, planes, tall_rows, nz), F32)
    dma = pltpu.SemaphoreType.DMA
    gradient, residual = pl.pallas_call(
        functools.partial(kernel, n_space, n_inj, nx, ny, nz, blocks),
        out_shape=(
            jax.ShapeDtypeStruct((nx, ny // n_inj, nz), F32),
            jax.ShapeDtypeStruct((2 * blocks, elec), F32),
        ),
        in_specs=[anywhere, anywhere, anywhere, smem, vmem, vmem, vmem, vmem],
        out_specs=(vmem, vmem),
        scratch_shapes=[
            pltpu.VMEM((planes, tall_rows, nz), F32),
            field, field, field, field,
            pltpu.VMEM((7, planes, ny, nz), F32),
            pltpu.VMEM((2, planes, ny, nz), F32),
            pltpu.VMEM((2, planes, ny, nz), F32),
            pltpu.VMEM((n_space, 8, elec), F32),
            pltpu.VMEM((n_space, 8, elec), F32),
            pltpu.VMEM((n_space, 4, elec), F32),
            pltpu.VMEM((n_space, 4, elec), F32),
            pltpu.VMEM((2, 2, ny, nz), F32),
            pltpu.VMEM((n_space, wide, 4 * elec), BF16),
            pltpu.VMEM((2 * tall, 2 * wide), BF16),
            pltpu.VMEM((2 * tall, wide), F32),
            pltpu.VMEM((n_inj, nx, ny // n_inj, nz), F32),
            pltpu.VMEM((n_inj, nx, ny // n_inj, nz), F32),
            dma((3,)), dma((4,)), dma((4,)), dma((2,)), dma((2,)), dma, dma,
            dma, dma, dma((2,)), dma((2,)), dma((2,)), dma((2,)), dma, dma,
        ],
        compiler_params=pltpu.CompilerParams(
            collective_id=0, has_side_effects=True, vmem_limit_bytes=48 * 1024 * 1024
        ),
    )(
        conductivity, start_potential, start_adjoint, inj_cells,
        owner_tile.reshape(blocks, 1), live_count,
        dipole_cells.reshape(2 * blocks, elec), observed.reshape(2 * blocks, elec),
    )
    return gradient, residual.reshape(1, blocks, 2, elec)


def solution(mesh):
    return jax.shard_map(
        body,
        mesh=mesh,
        in_specs=(
            P("space", None, None),
            P("inj", "space", None, None),
            P("inj", "space", None, None),
            P("inj", None),
            P("inj", "space", None, None),
            P("inj", "space", None),
            P("inj", "space"),
            P("inj", "space", None, None),
        ),
        out_specs=(P("space", "inj", None), P("inj", "space", None, None)),
        check_vma=False,
    )
```

```python
import functools
import math

import jax
import jax.numpy as jnp
from jax import lax
from jax.experimental import pallas as pl
from jax.experimental.pallas import tpu as pltpu
from jax.sharding import PartitionSpec as P

MESH = pl.DeviceIdType.MESH
F32 = jnp.float32
BF16 = jnp.bfloat16
HIGHEST = lax.Precision.HIGHEST

current_amp = 4.0
sweep_weights = [
    1.0 / (1.0 + 0.9 * math.cos((2 * step_k + 1) * math.pi / 6.0)) for step_k in range(3)
]

H = 4
PAD = 8


def iota(shape, dim):
    return lax.broadcasted_iota(jnp.int32, shape, dim)


def rows_sum(values):
    return jnp.sum(values, axis=0, keepdims=True)


def kernel(
    n_space, n_inj, nx, ny, nz, blocks,
    sig_in, pot_in, adj_in, inj_in, owner_in, live_in, cells_in, observed_in,
    grad_out, res_out,
    inj_cells, owner, live, cells, observed, sigma, pa, pb, aa, ab, coef, src, asrc, send, recv, ret_send, ret_recv,
    rim, onehot, table, scat, partial, shares,
    local_sem, halo_send, halo_recv, far_send, far_recv, block_send, block_recv,
    ret_send_sem, ret_recv_sem, rim_send, rim_recv, asrc_send, asrc_recv, share_send, share_recv,
):
    me = lax.axis_index("space")
    my_inj = lax.axis_index("inj")
    left = lax.rem(me + n_space - 1, n_space)
    right = lax.rem(me + 1, n_space)
    planes = nx + 2 * H
    rows = pl.ds(PAD, ny)
    half = nx // 2
    tall = half * ny
    wide = 2 * nz
    half_cells = float(half * ny * nz)
    group = math.gcd(n_space, 8)

    barrier = pltpu.get_barrier_semaphore()

    def greet(d, carry):
        pl.semaphore_signal(barrier, inc=1, device_id=(lax.rem(me + d, n_space), my_inj), device_id_type=MESH)
        return carry

    def greet_inj(d, carry):
        pl.semaphore_signal(barrier, inc=1, device_id=(me, lax.rem(my_inj + d, n_inj)), device_id_type=MESH)
        return carry

    lax.fori_loop(1, n_space, greet, 0)
    lax.fori_loop(1, n_inj, greet_inj, 0)

    small = [
        pltpu.make_async_copy(source, target, local_sem.at[3 + k])
        for k, (source, target) in enumerate(
            ((inj_in, inj_cells), (owner_in, owner), (live_in, live), (cells_in, cells), (observed_in, observed))
        )
    ]
    locals_ = [
        pltpu.make_async_copy(sig_in, sigma.at[pl.ds(H, nx), rows], local_sem.at[0]),
        pltpu.make_async_copy(pot_in, pa.at[:, pl.ds(H, nx), rows], local_sem.at[1]),
        pltpu.make_async_copy(adj_in, aa.at[:, pl.ds(H, nx), rows], local_sem.at[2]),
    ]
    for copy in small + locals_:
        copy.start()

    edge = jnp.zeros((PAD, nz), F32)

    def clear(p, carry):
        for low in (0, PAD + ny):
            sigma[p, pl.ds(low, PAD), :] = edge
            for i in range(2):
                for buf in (pa, pb, aa, ab):
                    buf[i, p, pl.ds(low, PAD), :] = edge
        return carry

    lax.fori_loop(0, planes, clear, 0)

    pl.semaphore_wait(barrier, n_space - 1 + n_inj - 1)

    def remote(source, target, send_sem, recv_sem, space, inj):
        return pltpu.make_async_remote_copy(
            src_ref=source, dst_ref=target, send_sem=send_sem, recv_sem=recv_sem,
            device_id=(space, inj), device_id_type=MESH,
        )

    early = [
        remote(sig_in.at[pl.ds(nx - H, H)], sigma.at[pl.ds(0, H), rows], halo_send.at[0], halo_recv.at[0], right, my_inj),
        remote(sig_in.at[pl.ds(0, H)], sigma.at[pl.ds(nx + H, H), rows], halo_send.at[1], halo_recv.at[1], left, my_inj),
        remote(pot_in.at[:, pl.ds(nx - 3, 3)], pa.at[:, pl.ds(H - 3, 3), rows], halo_send.at[2], halo_recv.at[2], right, my_inj),
        remote(pot_in.at[:, pl.ds(0, 3)], pa.at[:, pl.ds(nx + H, 3), rows], halo_send.at[3], halo_recv.at[3], left, my_inj),
    ]
    late = [
        remote(adj_in.at[:, pl.ds(nx - H, H)], aa.at[:, pl.ds(0, H), rows], far_send.at[0], far_recv.at[0], right, my_inj),
        remote(adj_in.at[:, pl.ds(0, H)], aa.at[:, pl.ds(nx + H, H), rows], far_send.at[1], far_recv.at[1], left, my_inj),
    ]
    for copy in early:
        copy.start()

    for copy in small:
        copy.wait()
    lanes = 4 * blocks
    lane_c = iota((blocks, lanes), 1)
    block_c = lax.rem(lane_c, 2 * blocks) // 2
    field_c = lax.rem(lane_c, 2) + 2 * (lane_c // (2 * blocks))
    row_b = iota((blocks, lanes), 0)
    owners = jnp.broadcast_to(owner[...].astype(F32), (blocks, blocks))
    owners = jnp.where(iota((blocks, blocks), 0) == iota((blocks, blocks), 1), owners, 0.0)
    owners = jnp.broadcast_to(jnp.sum(owners, axis=1, keepdims=True), (blocks, lanes))
    owner_c = rows_sum(jnp.where(row_b == block_c, owners, 0.0))
    earlier = (owners == owner_c) & (row_b < block_c)
    rank_c = rows_sum(jnp.where(earlier, 1.0, 0.0))
    slot_c = owner_c * 2.0 + rank_c
    target = slot_c * 4.0 + field_c[:1].astype(F32)
    place = jnp.where(iota((n_space * 8, lanes), 0).astype(F32) == target, 1.0, 0.0)

    row_r = iota((lanes, blocks), 0)
    block_r = lax.rem(row_r, 2 * blocks) // 2
    lives = jnp.broadcast_to(live[...].astype(F32), (lanes, blocks))
    live_r = jnp.sum(jnp.where(block_r == iota((lanes, blocks), 1), lives, 0.0), axis=1, keepdims=True)
    data = jnp.concatenate([cells[...].astype(F32) + 1.0, observed[...]], axis=0)
    elec = data.shape[1]
    data = jnp.where(iota((lanes, elec), 1).astype(F32) < live_r, data, 0.0)
    packed = jnp.dot(place, data, precision=HIGHEST, preferred_element_type=F32)
    for t in range(n_space):
        send[t] = packed[8 * t : 8 * t + 8]

    def send_block(d, carry):
        to = lax.rem(me + d, n_space)
        remote(send.at[to], recv.at[me], block_send, block_recv, to, my_inj).start()
        return carry

    lax.fori_loop(1, n_space, send_block, 0)
    for copy in late:
        copy.start()
    recv[me] = send[me]

    cell_ids = iota((ny, nz), 0) * nz + iota((ny, nz), 1)

    def own_source(p, carry):
        first = (me * nx - H + p) * (ny * nz)
        for i in range(2):
            plus = jnp.where(cell_ids == inj_cells[i, 0] - first, current_amp, 0.0)
            minus = jnp.where(cell_ids == inj_cells[i, 1] - first, current_amp, 0.0)
            src[i, p] = plus - minus
        return carry

    lax.fori_loop(0, planes, own_source, 0)

    def no_halo(buf, lead):
        nothing = jnp.zeros((ny, nz), F32)

        @pl.when(me == 0)
        def _():
            for p in range(H):
                for i in range(lead):
                    if lead == 1:
                        buf[p, rows, :] = nothing
                    else:
                        buf[i, p, rows, :] = nothing

        @pl.when(me == n_space - 1)
        def _():
            for p in range(nx + H, planes):
                for i in range(lead):
                    if lead == 1:
                        buf[p, rows, :] = nothing
                    else:
                        buf[i, p, rows, :] = nothing

    first_lane = iota((ny, nz), 1) == 0
    last_lane = iota((ny, nz), 1) == nz - 1

    locals_[0].wait()
    early[0].wait()
    early[1].wait()
    no_halo(sigma, 1)

    def faces(p, carry):
        here = sigma[p, rows, :]
        zp = jnp.where(last_lane, 0.0, pltpu.roll(here, nz - 1, 1))
        zm = jnp.where(first_lane, 0.0, pltpu.roll(here, 1, 1))
        around = [
            sigma[p + 1, rows, :], sigma[p - 1, rows, :],
            sigma[p, pl.ds(PAD + 1, ny), :], sigma[p, pl.ds(PAD - 1, ny), :], zp, zm,
        ]
        around = [0.5 * (here + value) for value in around]
        diag = around[0] + around[1] + around[2] + around[3] + around[4] + around[5]
        plane = me * nx - H + p
        inside = jnp.where((plane >= 0) & (plane < n_space * nx), 1.0, 0.0)
        inverse = inside / jnp.where(diag > 0.0, diag, 1.0)
        around[4] = jnp.where(last_lane, 0.0, around[4])
        around[5] = jnp.where(first_lane, 0.0, around[5])
        for k in range(6):
            coef[k, p] = around[k] * inverse
        coef[6, p] = inverse
        return carry

    lax.fori_loop(1, planes - 1, faces, 0)

    def sweep(source, old, new, low, high, weight):
        def plane(p, carry):
            c = [coef[k, p] for k in range(7)]
            for i in range(2):
                here = old[i, p, rows, :]
                beside = c[0] * old[i, p + 1, rows, :] + c[1] * old[i, p - 1, rows, :]
                beside = beside + (
                    c[2] * old[i, p, pl.ds(PAD + 1, ny), :] + c[3] * old[i, p, pl.ds(PAD - 1, ny), :]
                )
                beside = beside + (c[4] * pltpu.roll(here, nz - 1, 1) + c[5] * pltpu.roll(here, 1, 1))
                beside = beside + c[6] * source[i, p]
                new[i, p, rows, :] = here + weight * (beside - here)
            return carry

        lax.fori_loop(low, high, plane, 0)

    locals_[1].wait()
    early[2].wait()
    early[3].wait()
    no_halo(pa, 2)
    sweep(src, pa, pb, 2, planes - 2, sweep_weights[0])
    sweep(src, pb, pa, 3, planes - 3, sweep_weights[1])
    sweep(src, pa, pb, H, planes - H, sweep_weights[2])

    rims = [
        remote(pb.at[:, H + nx - 1, rows], rim.at[0], rim_send.at[0], rim_recv.at[0], right, my_inj),
        remote(pb.at[:, H, rows], rim.at[1], rim_send.at[1], rim_recv.at[1], left, my_inj),
    ]
    for copy in rims:
        copy.start()

    for i in range(2):
        for x in range(nx):
            value = pb[i, H + x, rows, :]
            high = value.astype(BF16)
            low = (value - high.astype(F32)).astype(BF16)
            at = (pl.ds(i * tall + (x % half) * ny, ny))
            table[at, pl.ds((x // half) * nz, nz)] = high
            table[at, pl.ds(wide + (x // half) * nz, nz)] = low

    got = pltpu.make_async_copy(recv.at[pl.ds(0, n_space - 1)], recv.at[pl.ds(0, n_space - 1)], block_recv)
    got.wait()

    wide_iota = iota((wide, elec), 0).astype(F32).astype(BF16)
    tall_iota = iota((tall, elec), 0).astype(F32)
    tall_iota16 = tall_iota.astype(BF16)
    one = jnp.ones((wide, elec), BF16)
    none = jnp.zeros((wide, elec), BF16)

    def split_cells(t):
        cell = recv[t] - 1.0
        upper = cell >= half_cells
        within = jnp.where(upper, cell - half_cells, cell)
        tall_at = jnp.floor(within * (1.0 / nz))
        wide_at = within - tall_at * nz + jnp.where(upper, float(nz), 0.0)
        return tall_at, jnp.where(cell < 0.0, -1.0, wide_at)

    def mark(t, carry):
        _, wide_at = split_cells(t)
        for s in range(2):
            for f in range(2):
                row = jnp.broadcast_to(wide_at[4 * s + f : 4 * s + f + 1], (wide, elec)).astype(BF16)
                onehot[t, :, pl.ds((2 * s + f) * elec, elec)] = jnp.where(wide_iota == row, one, none)
        return carry

    lax.fori_loop(0, n_space, mark, 0)

    def fetch(u, carry):
        for k in range(group):
            t = u * group + k
            tall_at, _ = split_cells(t)
            hot = onehot[t]
            found = jnp.dot(table[...], jnp.concatenate([hot, hot], axis=0), preferred_element_type=F32)
            out = []
            for s in range(2):
                ends = [[], []]
                for f in range(2):
                    here = tall_iota == tall_at[4 * s + f : 4 * s + f + 1]
                    for i in range(2):
                        piece = found[i * tall : (i + 1) * tall, (2 * s + f) * elec : (2 * s + f + 1) * elec]
                        ends[i].append(rows_sum(jnp.where(here, piece, 0.0)))
                for i in range(2):
                    out.append(ends[i][0] - ends[i][1] - recv[t, pl.ds(4 * s + 2 + i, 1), :])
            ret_send[t] = jnp.concatenate(out, axis=0)
        return carry

    lax.fori_loop(0, n_space // group, fetch, 0)

    def send_ret(d, carry):
        to = lax.rem(me + d, n_space)
        remote(ret_send.at[to], ret_recv.at[me], ret_send_sem, ret_recv_sem, to, my_inj).start()
        return carry

    lax.fori_loop(1, n_space, send_ret, 0)
    ret_recv[me] = ret_send[me]

    scat[...] = jnp.zeros_like(scat)

    def spread(u, carry):
        amounts, hots = [], []
        for k in range(group):
            t = u * group + k
            tall_at, _ = split_cells(t)
            misfit = ret_send[t]
            high = misfit.astype(BF16).astype(F32)
            low = misfit - high
            columns = [[], []]
            for s in range(2):
                for f in range(2):
                    sign = 1.0 if f == 0 else -1.0
                    row = jnp.broadcast_to(tall_at[4 * s + f : 4 * s + f + 1], (tall, elec)).astype(BF16)
                    here = tall_iota16 == row
                    for part, value in enumerate((high, low)):
                        pieces = []
                        for i in range(2):
                            amount = jnp.broadcast_to(sign * value[2 * s + i : 2 * s + i + 1], (tall, elec)).astype(BF16)
                            pieces.append(jnp.where(here, amount, jnp.zeros((tall, elec), BF16)))
                        columns[part].append(jnp.concatenate(pieces, axis=0))
            hot = onehot[t]
            amounts += columns[0] + columns[1]
            hots += [hot, hot]
        scat[...] += lax.dot_general(
            jnp.concatenate(amounts, axis=1), jnp.concatenate(hots, axis=1), (((1,), (1,)), ((), ())),
            preferred_element_type=F32,
        )
        return carry

    lax.fori_loop(0, n_space // group, spread, 0)
    for i in range(2):
        for x in range(nx):
            asrc[i, H + x] = scat[pl.ds(i * tall + (x % half) * ny, ny), pl.ds((x // half) * nz, nz)]
    around = [
        remote(asrc.at[:, pl.ds(H + nx - 3, 3)], asrc.at[:, pl.ds(1, 3)], asrc_send.at[0], asrc_recv.at[0], right, my_inj),
        remote(asrc.at[:, pl.ds(H, 3)], asrc.at[:, pl.ds(H + nx, 3)], asrc_send.at[1], asrc_recv.at[1], left, my_inj),
    ]
    for copy in around:
        copy.start()

    locals_[2].wait()
    late[0].wait()
    late[1].wait()
    no_halo(aa, 2)
    for copy in rims:
        copy.wait()
    for i in range(2):
        pb[i, H - 1, rows, :] = jnp.where(me == 0, 0.0, rim[0, i])
        pb[i, H + nx, rows, :] = jnp.where(me == n_space - 1, 0.0, rim[1, i])

    for copy in around:
        copy.wait()
    sweep(asrc, aa, ab, 1, planes - 1, sweep_weights[0])
    sweep(asrc, ab, aa, 2, planes - 2, sweep_weights[1])
    sweep(asrc, aa, ab, 3, planes - 3, sweep_weights[2])

    def term(x, carry):
        p = x + H
        total = jnp.zeros((ny, nz), F32)
        for i in range(2):
            here, there = pb[i, p, rows, :], ab[i, p, rows, :]
            pairs = [
                (pb[i, p + 1, rows, :], ab[i, p + 1, rows, :]),
                (pb[i, p - 1, rows, :], ab[i, p - 1, rows, :]),
                (pb[i, p, pl.ds(PAD + 1, ny), :], ab[i, p, pl.ds(PAD + 1, ny), :]),
                (pb[i, p, pl.ds(PAD - 1, ny), :], ab[i, p, pl.ds(PAD - 1, ny), :]),
                tuple(jnp.where(last_lane, 0.0, pltpu.roll(v, nz - 1, 1)) for v in (here, there)),
                tuple(jnp.where(first_lane, 0.0, pltpu.roll(v, 1, 1)) for v in (here, there)),
            ]
            for u, v in pairs:
                total = total + (here - u) * (there - v)
        partial[:, x] = (-0.5 * total).reshape(n_inj, ny // n_inj, nz)
        return carry

    lax.fori_loop(0, nx, term, 0)

    def send_share(d, carry):
        to = lax.rem(my_inj + d, n_inj)
        remote(partial.at[to], shares.at[my_inj], share_send, share_recv, me, to).start()
        return carry

    lax.fori_loop(1, n_inj, send_share, 0)
    shares[my_inj] = partial[my_inj]

    ret_got = pltpu.make_async_copy(ret_recv.at[pl.ds(0, n_space - 1)], ret_recv.at[pl.ds(0, n_space - 1)], ret_recv_sem)
    ret_got.wait()
    lane_j = lax.rem(iota((1, lanes), 1), 2).astype(F32)
    back = jnp.where(iota((n_space * 4, lanes), 0).astype(F32) == slot_c * 2.0 + lane_j, 1.0, 0.0)
    back = jnp.transpose(back)[: 2 * blocks]
    returned = jnp.concatenate([ret_recv[t] for t in range(n_space)], axis=0)
    res_out[...] = jnp.dot(back, returned, precision=HIGHEST, preferred_element_type=F32)

    share_got = pltpu.make_async_copy(shares.at[pl.ds(0, n_inj - 1)], shares.at[pl.ds(0, n_inj - 1)], share_recv)
    share_got.wait()
    total = shares[0]
    for k in range(1, n_inj):
        total = total + shares[k]
    grad_out[...] = total

    pltpu.make_async_copy(send.at[pl.ds(0, n_space - 1)], send.at[pl.ds(0, n_space - 1)], block_send).wait()
    pltpu.make_async_copy(ret_send.at[pl.ds(0, n_space - 1)], ret_send.at[pl.ds(0, n_space - 1)], ret_send_sem).wait()
    pltpu.make_async_copy(partial.at[pl.ds(0, n_inj - 1)], partial.at[pl.ds(0, n_inj - 1)], share_send).wait()


def body(
    conductivity, start_potential, start_adjoint, inj_cells, dipole_cells, owner_tile, live_count, observed,
):
    n_space, n_inj = lax.axis_size("space"), lax.axis_size("inj")
    nx, ny, nz = conductivity.shape
    blocks, elec = observed.shape[1], observed.shape[3]
    planes, tall_rows = nx + 2 * H, ny + 2 * PAD
    wide, tall = 2 * nz, nx // 2 * ny
    hbm = pl.BlockSpec(memory_space=pltpu.HBM)
    vmem = pl.BlockSpec(memory_space=pltpu.VMEM)
    field = pltpu.VMEM((2, planes, tall_rows, nz), F32)
    dma = pltpu.SemaphoreType.DMA
    gradient, residual = pl.pallas_call(
        functools.partial(kernel, n_space, n_inj, nx, ny, nz, blocks),
        out_shape=(
            jax.ShapeDtypeStruct((nx, ny // n_inj, nz), F32),
            jax.ShapeDtypeStruct((2 * blocks, elec), F32),
        ),
        in_specs=[hbm] * 8,
        out_specs=(vmem, vmem),
        scratch_shapes=[
            pltpu.SMEM((2, 2), jnp.int32),
            pltpu.VMEM((1, blocks), jnp.int32),
            pltpu.VMEM((1, blocks), jnp.int32),
            pltpu.VMEM((2 * blocks, elec), jnp.int32),
            pltpu.VMEM((2 * blocks, elec), F32),
            pltpu.VMEM((planes, tall_rows, nz), F32),
            field, field, field, field,
            pltpu.VMEM((7, planes, ny, nz), F32),
            pltpu.VMEM((2, planes, ny, nz), F32),
            pltpu.VMEM((2, planes, ny, nz), F32),
            pltpu.VMEM((n_space, 8, elec), F32),
            pltpu.VMEM((n_space, 8, elec), F32),
            pltpu.VMEM((n_space, 4, elec), F32),
            pltpu.VMEM((n_space, 4, elec), F32),
            pltpu.VMEM((2, 2, ny, nz), F32),
            pltpu.VMEM((n_space, wide, 4 * elec), BF16),
            pltpu.VMEM((2 * tall, 2 * wide), BF16),
            pltpu.VMEM((2 * tall, wide), F32),
            pltpu.VMEM((n_inj, nx, ny // n_inj, nz), F32),
            pltpu.VMEM((n_inj, nx, ny // n_inj, nz), F32),
            dma((8,)), dma((4,)), dma((4,)), dma((2,)), dma((2,)), dma, dma,
            dma, dma, dma((2,)), dma((2,)), dma((2,)), dma((2,)), dma, dma,
        ],
        compiler_params=pltpu.CompilerParams(
            collective_id=0, has_side_effects=True, vmem_limit_bytes=60 * 1024 * 1024
        ),
    )(
        conductivity, start_potential, start_adjoint, inj_cells,
        owner_tile.reshape(1, blocks), live_count,
        dipole_cells.reshape(2 * blocks, elec), observed.reshape(2 * blocks, elec),
    )
    return gradient, residual.reshape(1, blocks, 2, elec)


def solution(mesh):
    return jax.shard_map(
        body,
        mesh=mesh,
        in_specs=(
            P("space", None, None),
            P("inj", "space", None, None),
            P("inj", "space", None, None),
            P("inj", None),
            P("inj", "space", None, None),
            P("inj", "space", None),
            P("inj", "space"),
            P("inj", "space", None, None),
        ),
        out_specs=(P("space", "inj", None), P("inj", "space", None, None)),
        check_vma=False,
    )
```

```python
import functools
import math

import jax
import jax.numpy as jnp
from jax import lax
from jax.experimental import pallas as pl
from jax.experimental.pallas import tpu as pltpu
from jax.sharding import PartitionSpec as P

MESH = pl.DeviceIdType.MESH
F32 = jnp.float32
BF16 = jnp.bfloat16
HIGHEST = lax.Precision.HIGHEST

current_amp = 4.0
sweep_weights = [
    1.0 / (1.0 + 0.9 * math.cos((2 * step_k + 1) * math.pi / 6.0)) for step_k in range(3)
]

H = 4
PAD = 8


def iota(shape, dim):
    return lax.broadcasted_iota(jnp.int32, shape, dim)


def rows_sum(values):
    return jnp.sum(values, axis=0, keepdims=True)


def kernel(
    n_space, n_inj, nx, ny, nz, blocks,
    sig_in, pot_in, adj_in, inj_in, owner_in, live_in, cells_in, observed_in,
    grad_out, res_out,
    inj_cells, owner, live, cells, observed, sigma, pa, pb, aa, ab, coef, src, asrc, send, recv, ret_send, ret_recv,
    rim, onehot, table, scat, partial, shares,
    local_sem, halo_send, halo_recv, far_send, far_recv, block_send, block_recv,
    ret_send_sem, ret_recv_sem, rim_send, rim_recv, asrc_send, asrc_recv, share_send, share_recv,
):
    me = lax.axis_index("space")
    my_inj = lax.axis_index("inj")
    left = lax.rem(me + n_space - 1, n_space)
    right = lax.rem(me + 1, n_space)
    planes = nx + 2 * H
    rows = pl.ds(PAD, ny)
    half = nx // 2
    tall = half * ny
    wide = 2 * nz
    half_cells = float(half * ny * nz)
    group = math.gcd(n_space, 8)

    barrier = pltpu.get_barrier_semaphore()

    def greet(d, carry):
        pl.semaphore_signal(barrier, inc=1, device_id=(lax.rem(me + d, n_space), my_inj), device_id_type=MESH)
        return carry

    def greet_inj(d, carry):
        pl.semaphore_signal(barrier, inc=1, device_id=(me, lax.rem(my_inj + d, n_inj)), device_id_type=MESH)
        return carry

    lax.fori_loop(1, n_space, greet, 0)
    lax.fori_loop(1, n_inj, greet_inj, 0)

    small = [
        pltpu.make_async_copy(source, target, local_sem.at[3 + k])
        for k, (source, target) in enumerate(
            ((inj_in, inj_cells), (owner_in, owner), (live_in, live), (cells_in, cells), (observed_in, observed))
        )
    ]
    locals_ = [
        pltpu.make_async_copy(sig_in, sigma.at[pl.ds(H, nx), rows], local_sem.at[0]),
        pltpu.make_async_copy(pot_in, pa.at[:, pl.ds(H, nx), rows], local_sem.at[1]),
        pltpu.make_async_copy(adj_in, aa.at[:, pl.ds(H, nx), rows], local_sem.at[2]),
    ]
    for copy in small + locals_:
        copy.start()

    for low in (0, PAD + ny):
        sigma[:, pl.ds(low, PAD), :] = jnp.zeros((planes, PAD, nz), F32)
        for buf in (pa, pb, aa, ab):
            buf[:, :, pl.ds(low, PAD), :] = jnp.zeros((2, planes, PAD, nz), F32)

    pl.semaphore_wait(barrier, n_space - 1 + n_inj - 1)

    def remote(source, target, send_sem, recv_sem, space, inj):
        return pltpu.make_async_remote_copy(
            src_ref=source, dst_ref=target, send_sem=send_sem, recv_sem=recv_sem,
            device_id=(space, inj), device_id_type=MESH,
        )

    def pair(source, target, lead, width, send_sems, recv_sems, k):
        at = (slice(None),) * lead
        return [
            remote(
                source.at[at + (pl.ds(nx - width, width),)], target.at[at + (pl.ds(H - width, width), rows)],
                send_sems.at[k], recv_sems.at[k], right, my_inj,
            ),
            remote(
                source.at[at + (pl.ds(0, width),)], target.at[at + (pl.ds(nx + H, width), rows)],
                send_sems.at[k + 1], recv_sems.at[k + 1], left, my_inj,
            ),
        ]

    early = pair(sig_in, sigma, 0, 3, halo_send, halo_recv, 0) + pair(pot_in, pa, 1, 3, halo_send, halo_recv, 2)
    late = [
        remote(sig_in.at[pl.ds(nx - H, 1)], sigma.at[pl.ds(0, 1), rows], far_send.at[0], far_recv.at[0], right, my_inj),
        remote(sig_in.at[pl.ds(H - 1, 1)], sigma.at[pl.ds(planes - 1, 1), rows], far_send.at[1], far_recv.at[1], left, my_inj),
    ] + pair(adj_in, aa, 1, H, far_send, far_recv, 2)
    for copy in early:
        copy.start()

    for copy in small:
        copy.wait()
    lanes = 4 * blocks
    lane_c = iota((blocks, lanes), 1)
    block_c = lax.rem(lane_c, 2 * blocks) // 2
    field_c = lax.rem(lane_c, 2) + 2 * (lane_c // (2 * blocks))
    row_b = iota((blocks, lanes), 0)
    owners = jnp.broadcast_to(owner[...].astype(F32), (blocks, blocks))
    owners = jnp.where(iota((blocks, blocks), 0) == iota((blocks, blocks), 1), owners, 0.0)
    owners = jnp.broadcast_to(jnp.sum(owners, axis=1, keepdims=True), (blocks, lanes))
    owner_c = rows_sum(jnp.where(row_b == block_c, owners, 0.0))
    earlier = (owners == owner_c) & (row_b < block_c)
    rank_c = rows_sum(jnp.where(earlier, 1.0, 0.0))
    slot_c = owner_c * 2.0 + rank_c
    target = slot_c * 4.0 + field_c[:1].astype(F32)
    place = jnp.where(iota((n_space * 8, lanes), 0).astype(F32) == target, 1.0, 0.0)

    row_r = iota((lanes, blocks), 0)
    block_r = lax.rem(row_r, 2 * blocks) // 2
    lives = jnp.broadcast_to(live[...].astype(F32), (lanes, blocks))
    live_r = jnp.sum(jnp.where(block_r == iota((lanes, blocks), 1), lives, 0.0), axis=1, keepdims=True)
    data = jnp.concatenate([cells[...].astype(F32) + 1.0, observed[...]], axis=0)
    elec = data.shape[1]
    data = jnp.where(iota((lanes, elec), 1).astype(F32) < live_r, data, 0.0)
    packed = jnp.dot(place, data, precision=HIGHEST, preferred_element_type=F32)
    for t in range(n_space):
        send[t] = packed[8 * t : 8 * t + 8]

    def send_block(d, carry):
        to = lax.rem(me + d, n_space)
        remote(send.at[to], recv.at[me], block_send, block_recv, to, my_inj).start()
        return carry

    lax.fori_loop(1, n_space, send_block, 0)
    recv[me] = send[me]

    cell_ids = iota((ny, nz), 0) * nz + iota((ny, nz), 1)

    for p in range(2, planes - 2):
        first = (me * nx - H + p) * (ny * nz)
        for i in range(2):
            plus = jnp.where(cell_ids == inj_cells[i, 0] - first, current_amp, 0.0)
            minus = jnp.where(cell_ids == inj_cells[i, 1] - first, current_amp, 0.0)
            src[i, p] = plus - minus

    def beyond(buf, lead, low_side, width):
        at = (slice(None),) * lead
        nothing = jnp.zeros((2,) * lead + (width, ny, nz), F32)

        @pl.when(me == (0 if low_side else n_space - 1))
        def _():
            buf[at + (pl.ds(H - width if low_side else nx + H, width), rows)] = nothing

    chunk = ny // 2

    def in_chunks(work):
        def step(q, carry):
            low = pl.multiple_of(q * chunk, 8)
            work(low, pl.ds(pl.multiple_of(low + PAD, 8), chunk))
            return carry

        lax.fori_loop(0, ny // chunk, step, 0)

    first_lane = iota((chunk, nz), 1) == 0
    last_lane = iota((chunk, nz), 1) == nz - 1

    def next_z(value):
        return jnp.where(last_lane, 0.0, pltpu.roll(value, nz - 1, 1))

    def last_z(value):
        return jnp.where(first_lane, 0.0, pltpu.roll(value, 1, 1))

    def faces(which):
        def work(low, at):
            for p in which:
                here = sigma[p, at, :]
                around = [
                    sigma[p + 1, at, :], sigma[p - 1, at, :],
                    sigma[p, pl.ds(low + PAD + 1, chunk), :], sigma[p, pl.ds(low + PAD - 1, chunk), :],
                    next_z(here), last_z(here),
                ]
                around = [0.5 * (here + value) for value in around]
                diag = around[0] + around[1] + around[2] + around[3] + around[4] + around[5]
                plane = me * nx - H + p
                inside = jnp.where((plane >= 0) & (plane < n_space * nx), 1.0, 0.0)
                inverse = inside / jnp.where(diag > 0.0, diag, 1.0)
                around[4] = jnp.where(last_lane, 0.0, around[4])
                around[5] = jnp.where(first_lane, 0.0, around[5])
                for k in range(6):
                    coef[k, p, pl.ds(low, chunk), :] = around[k] * inverse
                coef[6, p, pl.ds(low, chunk), :] = inverse

        in_chunks(work)

    def sweep(source, old, new, which, weight):
        def work(low, at):
            for p in which:
                c = [coef[k, p, pl.ds(low, chunk), :] for k in range(7)]
                for i in range(2):
                    here = old[i, p, at, :]
                    beside = c[0] * old[i, p + 1, at, :] + c[1] * old[i, p - 1, at, :]
                    beside = beside + (
                        c[2] * old[i, p, pl.ds(low + PAD + 1, chunk), :] + c[3] * old[i, p, pl.ds(low + PAD - 1, chunk), :]
                    )
                    beside = beside + (c[4] * pltpu.roll(here, nz - 1, 1) + c[5] * pltpu.roll(here, 1, 1))
                    beside = beside + c[6] * source[i, p, pl.ds(low, chunk), :]
                    new[i, p, at, :] = here + weight * (beside - here)

        in_chunks(work)

    w0, w1, w2 = sweep_weights
    end = planes - 1

    locals_[0].wait()
    faces(range(H + 1, end - H))
    locals_[1].wait()
    sweep(src, pa, pb, range(H + 1, end - H), w0)
    sweep(src, pb, pa, range(H + 2, end - H - 1), w1)

    early[0].wait()
    early[1].wait()
    beyond(sigma, 0, True, 3)
    beyond(sigma, 0, False, 3)
    faces([2, 3, 4, end - 4, end - 3, end - 2])
    early[2].wait()
    beyond(pa, 1, True, 3)
    sweep(src, pa, pb, [2, 3, 4], w0)
    sweep(src, pb, pa, [3, 4, 5], w1)
    sweep(src, pa, pb, [4, 5, 6], w2)
    early[3].wait()
    for copy in late:
        copy.start()
    beyond(pa, 1, False, 3)
    sweep(src, pa, pb, [end - 4, end - 3, end - 2], w0)
    sweep(src, pb, pa, [end - 5, end - 4, end - 3], w1)
    sweep(src, pa, pb, [end - 6, end - 5, end - 4], w2)

    rims = [
        remote(pb.at[:, H + nx - 1, rows], rim.at[0], rim_send.at[0], rim_recv.at[0], right, my_inj),
        remote(pb.at[:, H, rows], rim.at[1], rim_send.at[1], rim_recv.at[1], left, my_inj),
    ]
    for copy in rims:
        copy.start()

    for i in range(2):
        for x in range(nx):
            value = pb[i, H + x, rows, :]
            high = value.astype(BF16)
            low = (value - high.astype(F32)).astype(BF16)
            at = (pl.ds(i * tall + (x % half) * ny, ny))
            table[at, pl.ds((x // half) * nz, nz)] = high
            table[at, pl.ds(wide + (x // half) * nz, nz)] = low

    got = pltpu.make_async_copy(recv.at[pl.ds(0, n_space - 1)], recv.at[pl.ds(0, n_space - 1)], block_recv)
    got.wait()

    wide_iota = iota((wide, elec), 0).astype(F32).astype(BF16)
    tall_iota = iota((tall, elec), 0).astype(F32)
    tall_iota16 = tall_iota.astype(BF16)
    one = jnp.ones((wide, elec), BF16)
    none = jnp.zeros((wide, elec), BF16)

    def split_cells(t):
        cell = recv[t] - 1.0
        upper = cell >= half_cells
        within = jnp.where(upper, cell - half_cells, cell)
        tall_at = jnp.floor(within * (1.0 / nz))
        wide_at = within - tall_at * nz + jnp.where(upper, float(nz), 0.0)
        return tall_at, jnp.where(cell < 0.0, -1.0, wide_at)

    def mark(t, carry):
        _, wide_at = split_cells(t)
        for s in range(2):
            for f in range(2):
                row = jnp.broadcast_to(wide_at[4 * s + f : 4 * s + f + 1], (wide, elec)).astype(BF16)
                onehot[t, :, pl.ds((2 * s + f) * elec, elec)] = jnp.where(wide_iota == row, one, none)
        return carry

    lax.fori_loop(0, n_space, mark, 0)

    def fetch(u, carry):
        for k in range(group):
            t = u * group + k
            tall_at, _ = split_cells(t)
            hot = onehot[t]
            found = jnp.dot(table[...], jnp.concatenate([hot, hot], axis=0), preferred_element_type=F32)
            out = []
            for s in range(2):
                ends = [[], []]
                for f in range(2):
                    here = tall_iota == tall_at[4 * s + f : 4 * s + f + 1]
                    for i in range(2):
                        piece = found[i * tall : (i + 1) * tall, (2 * s + f) * elec : (2 * s + f + 1) * elec]
                        ends[i].append(rows_sum(jnp.where(here, piece, 0.0)))
                for i in range(2):
                    out.append(ends[i][0] - ends[i][1] - recv[t, pl.ds(4 * s + 2 + i, 1), :])
            ret_send[t] = jnp.concatenate(out, axis=0)
        return carry

    lax.fori_loop(0, n_space // group, fetch, 0)

    def send_ret(d, carry):
        to = lax.rem(me + d, n_space)
        remote(ret_send.at[to], ret_recv.at[me], ret_send_sem, ret_recv_sem, to, my_inj).start()
        return carry

    lax.fori_loop(1, n_space, send_ret, 0)
    ret_recv[me] = ret_send[me]

    scat[...] = jnp.zeros_like(scat)

    def spread(u, carry):
        amounts, hots = [], []
        for k in range(group):
            t = u * group + k
            tall_at, _ = split_cells(t)
            misfit = ret_send[t]
            high = misfit.astype(BF16).astype(F32)
            low = misfit - high
            columns = [[], []]
            for s in range(2):
                for f in range(2):
                    sign = 1.0 if f == 0 else -1.0
                    row = jnp.broadcast_to(tall_at[4 * s + f : 4 * s + f + 1], (tall, elec)).astype(BF16)
                    here = tall_iota16 == row
                    for part, value in enumerate((high, low)):
                        pieces = []
                        for i in range(2):
                            amount = jnp.broadcast_to(sign * value[2 * s + i : 2 * s + i + 1], (tall, elec)).astype(BF16)
                            pieces.append(jnp.where(here, amount, jnp.zeros((tall, elec), BF16)))
                        columns[part].append(jnp.concatenate(pieces, axis=0))
            hot = onehot[t]
            amounts += columns[0] + columns[1]
            hots += [hot, hot]
        scat[...] += lax.dot_general(
            jnp.concatenate(amounts, axis=1), jnp.concatenate(hots, axis=1), (((1,), (1,)), ((), ())),
            preferred_element_type=F32,
        )
        return carry

    lax.fori_loop(0, n_space // group, spread, 0)
    for i in range(2):
        for x in range(nx):
            asrc[i, H + x] = scat[pl.ds(i * tall + (x % half) * ny, ny), pl.ds((x // half) * nz, nz)]
    around = [
        remote(asrc.at[:, pl.ds(H + nx - 3, 3)], asrc.at[:, pl.ds(1, 3)], asrc_send.at[0], asrc_recv.at[0], right, my_inj),
        remote(asrc.at[:, pl.ds(H, 3)], asrc.at[:, pl.ds(H + nx, 3)], asrc_send.at[1], asrc_recv.at[1], left, my_inj),
    ]
    for copy in around:
        copy.start()

    locals_[2].wait()
    for copy in late:
        copy.wait()
    beyond(sigma, 0, True, H)
    beyond(sigma, 0, False, H)
    beyond(aa, 1, True, H)
    beyond(aa, 1, False, H)
    faces([1, end - 1])
    for copy in rims:
        copy.wait()
    for i in range(2):
        pb[i, H - 1, rows, :] = jnp.where(me == 0, 0.0, rim[0, i])
        pb[i, H + nx, rows, :] = jnp.where(me == n_space - 1, 0.0, rim[1, i])
    sweep(asrc, aa, ab, range(H, H + nx), w0)
    sweep(asrc, ab, aa, range(H + 1, end - H), w1)
    sweep(asrc, aa, ab, range(H + 2, end - H - 1), w2)

    def term(side):
        def work(low, at):
            for x in range(half):
                p = H + side * half + x
                total = jnp.zeros((chunk, nz), F32)
                for i in range(2):
                    here, there = pb[i, p, at, :], ab[i, p, at, :]
                    ahead, behind = pl.ds(low + PAD + 1, chunk), pl.ds(low + PAD - 1, chunk)
                    pairs = [
                        (pb[i, p + 1, at, :], ab[i, p + 1, at, :]),
                        (pb[i, p - 1, at, :], ab[i, p - 1, at, :]),
                        (pb[i, p, ahead, :], ab[i, p, ahead, :]),
                        (pb[i, p, behind, :], ab[i, p, behind, :]),
                        (next_z(here), next_z(there)),
                        (last_z(here), last_z(there)),
                    ]
                    for u, v in pairs:
                        total = total + (here - u) * (there - v)
                part = ny // n_inj
                first = low // part
                partial[side, pl.ds(first, chunk // part), x] = (-0.5 * total).reshape(chunk // part, part, nz)

        in_chunks(work)

    def send_share(side):
        def step(d, carry):
            to = lax.rem(my_inj + d, n_inj)
            remote(
                partial.at[side, to], shares.at[side, my_inj], share_send.at[side], share_recv.at[side], me, to
            ).start()
            return carry

        lax.fori_loop(1, n_inj, step, 0)
        shares[side, my_inj] = partial[side, my_inj]

    around[0].wait()
    sweep(asrc, aa, ab, [1, 2, 3], w0)
    sweep(asrc, ab, aa, [2, 3, 4], w1)
    sweep(asrc, aa, ab, [3, 4, 5], w2)
    term(0)
    send_share(0)
    around[1].wait()
    sweep(asrc, aa, ab, [end - 3, end - 2, end - 1], w0)
    sweep(asrc, ab, aa, [end - 4, end - 3, end - 2], w1)
    sweep(asrc, aa, ab, [end - 5, end - 4, end - 3], w2)
    term(1)
    send_share(1)

    ret_got = pltpu.make_async_copy(ret_recv.at[pl.ds(0, n_space - 1)], ret_recv.at[pl.ds(0, n_space - 1)], ret_recv_sem)
    ret_got.wait()
    lane_j = lax.rem(iota((1, lanes), 1), 2).astype(F32)
    back = jnp.where(iota((n_space * 4, lanes), 0).astype(F32) == slot_c * 2.0 + lane_j, 1.0, 0.0)
    back = jnp.transpose(back)[: 2 * blocks]
    returned = jnp.concatenate([ret_recv[t] for t in range(n_space)], axis=0)
    res_out[...] = jnp.dot(back, returned, precision=HIGHEST, preferred_element_type=F32)

    for side in range(2):
        window = shares.at[side, pl.ds(0, n_inj - 1)]
        pltpu.make_async_copy(window, window, share_recv.at[side]).wait()
        total = shares[side, 0]
        for k in range(1, n_inj):
            total = total + shares[side, k]
        grad_out[pl.ds(side * half, half)] = total

    pltpu.make_async_copy(send.at[pl.ds(0, n_space - 1)], send.at[pl.ds(0, n_space - 1)], block_send).wait()
    pltpu.make_async_copy(ret_send.at[pl.ds(0, n_space - 1)], ret_send.at[pl.ds(0, n_space - 1)], ret_send_sem).wait()
    for side in range(2):
        window = partial.at[side, pl.ds(0, n_inj - 1)]
        pltpu.make_async_copy(window, window, share_send.at[side]).wait()


def body(
    conductivity, start_potential, start_adjoint, inj_cells, dipole_cells, owner_tile, live_count, observed,
):
    n_space, n_inj = lax.axis_size("space"), lax.axis_size("inj")
    nx, ny, nz = conductivity.shape
    blocks, elec = observed.shape[1], observed.shape[3]
    planes, tall_rows = nx + 2 * H, ny + 2 * PAD
    wide, tall = 2 * nz, nx // 2 * ny
    hbm = pl.BlockSpec(memory_space=pltpu.HBM)
    vmem = pl.BlockSpec(memory_space=pltpu.VMEM)
    field = pltpu.VMEM((2, planes, tall_rows, nz), F32)
    dma = pltpu.SemaphoreType.DMA
    gradient, residual = pl.pallas_call(
        functools.partial(kernel, n_space, n_inj, nx, ny, nz, blocks),
        out_shape=(
            jax.ShapeDtypeStruct((nx, ny // n_inj, nz), F32),
            jax.ShapeDtypeStruct((2 * blocks, elec), F32),
        ),
        in_specs=[hbm] * 8,
        out_specs=(vmem, vmem),
        scratch_shapes=[
            pltpu.SMEM((2, 2), jnp.int32),
            pltpu.VMEM((1, blocks), jnp.int32),
            pltpu.VMEM((1, blocks), jnp.int32),
            pltpu.VMEM((2 * blocks, elec), jnp.int32),
            pltpu.VMEM((2 * blocks, elec), F32),
            pltpu.VMEM((planes, tall_rows, nz), F32),
            field, field, field, field,
            pltpu.VMEM((7, planes, ny, nz), F32),
            pltpu.VMEM((2, planes, ny, nz), F32),
            pltpu.VMEM((2, planes, ny, nz), F32),
            pltpu.VMEM((n_space, 8, elec), F32),
            pltpu.VMEM((n_space, 8, elec), F32),
            pltpu.VMEM((n_space, 4, elec), F32),
            pltpu.VMEM((n_space, 4, elec), F32),
            pltpu.VMEM((2, 2, ny, nz), F32),
            pltpu.VMEM((n_space, wide, 4 * elec), BF16),
            pltpu.VMEM((2 * tall, 2 * wide), BF16),
            pltpu.VMEM((2 * tall, wide), F32),
            pltpu.VMEM((2, n_inj, nx // 2, ny // n_inj, nz), F32),
            pltpu.VMEM((2, n_inj, nx // 2, ny // n_inj, nz), F32),
            dma((8,)), dma((4,)), dma((4,)), dma((4,)), dma((4,)), dma, dma,
            dma, dma, dma((2,)), dma((2,)), dma((2,)), dma((2,)), dma((2,)), dma((2,)),
        ],
        compiler_params=pltpu.CompilerParams(
            collective_id=0, has_side_effects=True, vmem_limit_bytes=60 * 1024 * 1024
        ),
    )(
        conductivity, start_potential, start_adjoint, inj_cells,
        owner_tile.reshape(1, blocks), live_count,
        dipole_cells.reshape(2 * blocks, elec), observed.reshape(2 * blocks, elec),
    )
    return gradient, residual.reshape(1, blocks, 2, elec)


def solution(mesh):
    return jax.shard_map(
        body,
        mesh=mesh,
        in_specs=(
            P("space", None, None),
            P("inj", "space", None, None),
            P("inj", "space", None, None),
            P("inj", None),
            P("inj", "space", None, None),
            P("inj", "space", None),
            P("inj", "space"),
            P("inj", "space", None, None),
        ),
        out_specs=(P("space", "inj", None), P("inj", "space", None, None)),
        check_vma=False,
    )
```

```python
import functools
import math

import jax
import jax.numpy as jnp
from jax import lax
from jax.experimental import pallas as pl
from jax.experimental.pallas import tpu as pltpu
from jax.sharding import PartitionSpec as P

MESH = pl.DeviceIdType.MESH
F32 = jnp.float32
BF16 = jnp.bfloat16
HIGHEST = lax.Precision.HIGHEST

current_amp = 4.0
sweep_weights = [
    1.0 / (1.0 + 0.9 * math.cos((2 * step_k + 1) * math.pi / 6.0)) for step_k in range(3)
]

H = 4
PAD = 8


def iota(shape, dim):
    return lax.broadcasted_iota(jnp.int32, shape, dim)


def rows_sum(values):
    return jnp.sum(values, axis=0, keepdims=True)


def kernel(
    n_space, n_inj, nx, ny, nz, blocks,
    sig_in, pot_in, adj_in, inj_in, owner_in, live_in, cells_in, observed_in,
    grad_out, res_out,
    inj_cells, owner, live, cells, observed, sigma, pa, pb, aa, ab, coef, src, asrc, send, recv, ret_send, ret_recv,
    rim, onehot, table, scat, partial, shares,
    local_sem, halo_send, halo_recv, far_send, far_recv, block_send, block_recv,
    ret_send_sem, ret_recv_sem, rim_send, rim_recv, asrc_send, asrc_recv, share_send, share_recv,
):
    me = lax.axis_index("space")
    my_inj = lax.axis_index("inj")
    left = lax.rem(me + n_space - 1, n_space)
    right = lax.rem(me + 1, n_space)
    planes = nx + 2 * H
    rows = pl.ds(PAD, ny)
    half = nx // 2
    tall = half * ny
    wide = 2 * nz
    half_cells = float(half * ny * nz)
    group = math.gcd(n_space, 16)

    barrier = pltpu.get_barrier_semaphore()

    def greet(to):
        pl.semaphore_signal(barrier, inc=1, device_id=to, device_id_type=MESH)

    def greet_space(d, carry):
        greet((lax.rem(me + d, n_space), my_inj))
        return carry

    def greet_inj(d, carry):
        greet((me, lax.rem(my_inj + d, n_inj)))
        return carry

    greet((left, my_inj))
    greet((right, my_inj))
    lax.fori_loop(2, n_space - 1, greet_space, 0)
    lax.fori_loop(1, n_inj, greet_inj, 0)

    small = [
        pltpu.make_async_copy(source, target, local_sem.at[3 + k])
        for k, (source, target) in enumerate(
            ((inj_in, inj_cells), (owner_in, owner), (live_in, live), (cells_in, cells), (observed_in, observed))
        )
    ]
    locals_ = [
        pltpu.make_async_copy(sig_in, sigma.at[pl.ds(H, nx), rows], local_sem.at[0]),
        pltpu.make_async_copy(pot_in, pa.at[:, pl.ds(H, nx), rows], local_sem.at[1]),
        pltpu.make_async_copy(adj_in, aa.at[:, pl.ds(H, nx), rows], local_sem.at[2]),
    ]
    for copy in small + locals_:
        copy.start()

    for low in (0, PAD + ny):
        sigma[:, pl.ds(low, PAD), :] = jnp.zeros((planes, PAD, nz), F32)
        for buf in (pa, pb, aa, ab):
            buf[:, :, pl.ds(low, PAD), :] = jnp.zeros((2, planes, PAD, nz), F32)

    pl.semaphore_wait(barrier, n_space - 1 + n_inj - 1)

    def remote(source, target, send_sem, recv_sem, space, inj):
        return pltpu.make_async_remote_copy(
            src_ref=source, dst_ref=target, send_sem=send_sem, recv_sem=recv_sem,
            device_id=(space, inj), device_id_type=MESH,
        )

    def pair(source, target, lead, width, send_sems, recv_sems, k):
        return [
            remote(
                source.at[lead + (pl.ds(nx - width, width),)], target.at[lead + (pl.ds(H - width, width), rows)],
                send_sems.at[k], recv_sems.at[k], right, my_inj,
            ),
            remote(
                source.at[lead + (pl.ds(0, width),)], target.at[lead + (pl.ds(nx + H, width), rows)],
                send_sems.at[k + 1], recv_sems.at[k + 1], left, my_inj,
            ),
        ]

    early = pair(sig_in, sigma, (), 3, halo_send, halo_recv, 0)
    near = [pair(pot_in, pa, (i,), 3, halo_send, halo_recv, 2 + 2 * i) for i in range(2)]
    late = [
        remote(sig_in.at[pl.ds(nx - H, 1)], sigma.at[pl.ds(0, 1), rows], far_send.at[0], far_recv.at[0], right, my_inj),
        remote(sig_in.at[pl.ds(H - 1, 1)], sigma.at[pl.ds(planes - 1, 1), rows], far_send.at[1], far_recv.at[1], left, my_inj),
    ] + pair(adj_in, aa, (slice(None),), H, far_send, far_recv, 2)
    for copy in early + near[0]:
        copy.start()

    for copy in small:
        copy.wait()
    lanes = 4 * blocks
    lane_c = iota((blocks, lanes), 1)
    block_c = lax.rem(lane_c, 2 * blocks) // 2
    field_c = lax.rem(lane_c, 2) + 2 * (lane_c // (2 * blocks))
    row_b = iota((blocks, lanes), 0)
    owners = jnp.broadcast_to(owner[...].astype(F32), (blocks, blocks))
    owners = jnp.where(iota((blocks, blocks), 0) == iota((blocks, blocks), 1), owners, 0.0)
    owners = jnp.broadcast_to(jnp.sum(owners, axis=1, keepdims=True), (blocks, lanes))
    owner_c = rows_sum(jnp.where(row_b == block_c, owners, 0.0))
    earlier = (owners == owner_c) & (row_b < block_c)
    rank_c = rows_sum(jnp.where(earlier, 1.0, 0.0))
    slot_c = owner_c * 2.0 + rank_c
    target = slot_c * 4.0 + field_c[:1].astype(F32)
    place = jnp.where(iota((n_space * 8, lanes), 0).astype(F32) == target, 1.0, 0.0)

    row_r = iota((lanes, blocks), 0)
    block_r = lax.rem(row_r, 2 * blocks) // 2
    lives = jnp.broadcast_to(live[...].astype(F32), (lanes, blocks))
    live_r = jnp.sum(jnp.where(block_r == iota((lanes, blocks), 1), lives, 0.0), axis=1, keepdims=True)
    data = jnp.concatenate([cells[...].astype(F32) + 1.0, observed[...]], axis=0)
    elec = data.shape[1]
    data = jnp.where(iota((lanes, elec), 1).astype(F32) < live_r, data, 0.0)
    packed = jnp.dot(place, data, precision=HIGHEST, preferred_element_type=F32)
    for t in range(n_space):
        send[t] = packed[8 * t : 8 * t + 8]

    def send_block(d, carry):
        to = lax.rem(me + d, n_space)
        remote(send.at[to], recv.at[me], block_send, block_recv, to, my_inj).start()
        return carry

    lax.fori_loop(1, n_space, send_block, 0)
    for copy in near[1]:
        copy.start()
    recv[me] = send[me]

    cell_ids = iota((ny, nz), 0) * nz + iota((ny, nz), 1)

    for p in range(2, planes - 2):
        first = (me * nx - H + p) * (ny * nz)
        for i in range(2):
            plus = jnp.where(cell_ids == inj_cells[i, 0] - first, current_amp, 0.0)
            minus = jnp.where(cell_ids == inj_cells[i, 1] - first, current_amp, 0.0)
            src[i, p] = plus - minus

    def beyond(buf, lead, low_side, width):
        nothing = jnp.zeros((width, ny, nz), F32)

        @pl.when(me == (0 if low_side else n_space - 1))
        def _():
            buf[lead + (pl.ds(H - width if low_side else nx + H, width), rows)] = nothing

    chunk = ny // 2

    def in_chunks(work):
        def step(q, carry):
            low = pl.multiple_of(q * chunk, 8)
            work(low, pl.ds(pl.multiple_of(low + PAD, 8), chunk))
            return carry

        lax.fori_loop(0, ny // chunk, step, 0)

    first_lane = iota((chunk, nz), 1) == 0
    last_lane = iota((chunk, nz), 1) == nz - 1

    def next_z(value):
        return jnp.where(last_lane, 0.0, pltpu.roll(value, nz - 1, 1))

    def last_z(value):
        return jnp.where(first_lane, 0.0, pltpu.roll(value, 1, 1))

    def faces(which):
        def work(low, at):
            for p in which:
                here = sigma[p, at, :]
                around = [
                    sigma[p + 1, at, :], sigma[p - 1, at, :],
                    sigma[p, pl.ds(low + PAD + 1, chunk), :], sigma[p, pl.ds(low + PAD - 1, chunk), :],
                    next_z(here), last_z(here),
                ]
                around = [0.5 * (here + value) for value in around]
                diag = around[0] + around[1] + around[2] + around[3] + around[4] + around[5]
                plane = me * nx - H + p
                inside = jnp.where((plane >= 0) & (plane < n_space * nx), 1.0, 0.0)
                inverse = inside / jnp.where(diag > 0.0, diag, 1.0)
                around[4] = jnp.where(last_lane, 0.0, around[4])
                around[5] = jnp.where(first_lane, 0.0, around[5])
                for k in range(6):
                    coef[k, p, pl.ds(low, chunk), :] = around[k] * inverse
                coef[6, p, pl.ds(low, chunk), :] = inverse

        in_chunks(work)

    def sweep(i, source, old, new, which, weight):
        def work(low, at):
            for p in which:
                c = [coef[k, p, pl.ds(low, chunk), :] for k in range(7)]
                here = old[i, p, at, :]
                beside = c[0] * old[i, p + 1, at, :] + c[1] * old[i, p - 1, at, :]
                beside = beside + (
                    c[2] * old[i, p, pl.ds(low + PAD + 1, chunk), :] + c[3] * old[i, p, pl.ds(low + PAD - 1, chunk), :]
                )
                beside = beside + (c[4] * pltpu.roll(here, nz - 1, 1) + c[5] * pltpu.roll(here, 1, 1))
                beside = beside + c[6] * source[i, p, pl.ds(low, chunk), :]
                new[i, p, at, :] = here + weight * (beside - here)

        in_chunks(work)

    w0, w1, w2 = sweep_weights
    end = planes - 1

    locals_[0].wait()
    faces(range(H + 1, end - H))
    locals_[1].wait()
    for i in range(2):
        sweep(i, src, pa, pb, range(H + 1, end - H), w0)
        sweep(i, src, pb, pa, range(H + 2, end - H - 1), w1)

    for copy in early:
        copy.wait()
    beyond(sigma, (), True, 3)
    beyond(sigma, (), False, 3)
    faces([2, 3, 4, end - 4, end - 3, end - 2])

    def finish_potential(i):
        for copy in near[i]:
            copy.wait()
        beyond(pa, (i,), True, 3)
        beyond(pa, (i,), False, 3)
        sweep(i, src, pa, pb, [2, 3, 4, end - 4, end - 3, end - 2], w0)
        sweep(i, src, pb, pa, [3, 4, 5, end - 5, end - 4, end - 3], w1)
        sweep(i, src, pa, pb, range(H, H + nx), w2)
        for x in range(nx):
            value = pb[i, H + x, rows, :]
            high = value.astype(BF16)
            low = (value - high.astype(F32)).astype(BF16)
            first, columns = (x % half) * ny, pl.ds((x // half) * nz, nz)
            table[i, pl.ds(first, ny), columns] = high
            table[i, pl.ds(tall + first, ny), columns] = low

    wide_iota = iota((wide, elec), 0).astype(F32).astype(BF16)
    tall_iota = iota((tall, elec), 0).astype(F32)
    tall_iota16 = tall_iota.astype(BF16)
    one = jnp.ones((wide, elec), BF16)
    none = jnp.zeros((wide, elec), BF16)

    def split_cells(t):
        cell = recv[t] - 1.0
        upper = cell >= half_cells
        within = jnp.where(upper, cell - half_cells, cell)
        tall_at = jnp.floor(within * (1.0 / nz))
        wide_at = within - tall_at * nz + jnp.where(upper, float(nz), 0.0)
        return tall_at, jnp.where(cell < 0.0, -1.0, wide_at)

    def mark(t, carry):
        _, wide_at = split_cells(t)
        for s in range(2):
            for f in range(2):
                row = jnp.broadcast_to(wide_at[4 * s + f : 4 * s + f + 1], (wide, elec)).astype(BF16)
                onehot[t, :, pl.ds((2 * s + f) * elec, elec)] = jnp.where(wide_iota == row, one, none)
        return carry

    def fetch(i):
        def step(u, carry):
            for k in range(group):
                t = u * group + k
                tall_at, _ = split_cells(t)
                found = jnp.dot(table[i], onehot[t], preferred_element_type=F32)
                for s in range(2):
                    ends = []
                    for f in range(2):
                        here = tall_iota == tall_at[4 * s + f : 4 * s + f + 1]
                        at = slice((2 * s + f) * elec, (2 * s + f + 1) * elec)
                        ends.append(rows_sum(jnp.where(here, found[:tall, at] + found[tall:, at], 0.0)))
                    ret_send[t, pl.ds(2 * s + i, 1), :] = ends[0] - ends[1] - recv[t, pl.ds(4 * s + 2 + i, 1), :]
            return carry

        lax.fori_loop(0, n_space // group, step, 0)

    def spread(i):
        scat[...] = jnp.zeros_like(scat)

        def step(u, carry):
            amounts, hots = [], []
            for k in range(group):
                t = u * group + k
                tall_at, _ = split_cells(t)
                misfit = ret_send[t]
                high = misfit.astype(BF16).astype(F32)
                for s in range(2):
                    for f in range(2):
                        sign = 1.0 if f == 0 else -1.0
                        row = jnp.broadcast_to(tall_at[4 * s + f : 4 * s + f + 1], (tall, elec)).astype(BF16)
                        here = tall_iota16 == row
                        pieces = []
                        for value in (high, misfit - high):
                            amount = jnp.broadcast_to(sign * value[2 * s + i : 2 * s + i + 1], (tall, elec)).astype(BF16)
                            pieces.append(jnp.where(here, amount, jnp.zeros((tall, elec), BF16)))
                        amounts.append(jnp.concatenate(pieces, axis=0))
                hots.append(onehot[t])
            scat[...] += lax.dot_general(
                jnp.concatenate(amounts, axis=1), jnp.concatenate(hots, axis=1), (((1,), (1,)), ((), ())),
                preferred_element_type=F32,
            )
            return carry

        lax.fori_loop(0, n_space // group, step, 0)
        for x in range(nx):
            first, columns = (x % half) * ny, pl.ds((x // half) * nz, nz)
            asrc[i, H + x] = scat[pl.ds(first, ny), columns] + scat[pl.ds(tall + first, ny), columns]

    rims = [
        [
            remote(pb.at[i, H + nx - 1, rows], rim.at[0, i], rim_send.at[2 * i], rim_recv.at[2 * i], right, my_inj),
            remote(pb.at[i, H, rows], rim.at[1, i], rim_send.at[2 * i + 1], rim_recv.at[2 * i + 1], left, my_inj),
        ]
        for i in range(2)
    ]
    around = [
        [
            remote(
                asrc.at[i, pl.ds(H + nx - 3, 3)], asrc.at[i, pl.ds(1, 3)],
                asrc_send.at[2 * i], asrc_recv.at[2 * i], right, my_inj,
            ),
            remote(
                asrc.at[i, pl.ds(H, 3)], asrc.at[i, pl.ds(H + nx, 3)],
                asrc_send.at[2 * i + 1], asrc_recv.at[2 * i + 1], left, my_inj,
            ),
        ]
        for i in range(2)
    ]

    finish_potential(0)
    for copy in rims[0]:
        copy.start()
    got = pltpu.make_async_copy(recv.at[pl.ds(0, n_space - 1)], recv.at[pl.ds(0, n_space - 1)], block_recv)
    got.wait()
    lax.fori_loop(0, n_space, mark, 0)
    fetch(0)
    finish_potential(1)
    for copy in late + rims[1]:
        copy.start()
    spread(0)
    for copy in around[0]:
        copy.start()
    fetch(1)

    def send_ret(d, carry):
        to = lax.rem(me + d, n_space)
        remote(ret_send.at[to], ret_recv.at[me], ret_send_sem, ret_recv_sem, to, my_inj).start()
        return carry

    lax.fori_loop(1, n_space, send_ret, 0)
    ret_recv[me] = ret_send[me]

    spread(1)
    for copy in around[1]:
        copy.start()

    locals_[2].wait()
    for copy in late:
        copy.wait()
    for low_side in (True, False):
        beyond(sigma, (), low_side, H)
        for i in range(2):
            beyond(aa, (i,), low_side, H)
    faces([1, end - 1])
    for i in range(2):
        for copy in rims[i]:
            copy.wait()
        pb[i, H - 1, rows, :] = jnp.where(me == 0, 0.0, rim[0, i])
        pb[i, H + nx, rows, :] = jnp.where(me == n_space - 1, 0.0, rim[1, i])

    for copy in around[0]:
        copy.wait()
    sweep(0, asrc, aa, ab, range(1, planes - 1), w0)
    sweep(0, asrc, ab, aa, range(2, planes - 2), w1)
    sweep(0, asrc, aa, ab, range(3, planes - 3), w2)
    sweep(1, asrc, aa, ab, range(H, H + nx), w0)
    sweep(1, asrc, ab, aa, range(H + 1, end - H), w1)
    sweep(1, asrc, aa, ab, range(H + 2, end - H - 1), w2)

    def term(i, side):
        def work(low, at):
            part = ny // n_inj
            where = pl.ds(low // part, chunk // part)
            for x in range(half):
                p = H + side * half + x
                here, there = pb[i, p, at, :], ab[i, p, at, :]
                ahead, behind = pl.ds(low + PAD + 1, chunk), pl.ds(low + PAD - 1, chunk)
                pairs = [
                    (pb[i, p + 1, at, :], ab[i, p + 1, at, :]),
                    (pb[i, p - 1, at, :], ab[i, p - 1, at, :]),
                    (pb[i, p, ahead, :], ab[i, p, ahead, :]),
                    (pb[i, p, behind, :], ab[i, p, behind, :]),
                    (next_z(here), next_z(there)),
                    (last_z(here), last_z(there)),
                ]
                total = jnp.zeros((chunk, nz), F32)
                for u, v in pairs:
                    total = total + (here - u) * (there - v)
                total = (-0.5 * total).reshape(chunk // part, part, nz)
                partial[side, where, x] = total if i == 0 else partial[side, where, x] + total

        in_chunks(work)

    def send_share(side):
        def step(d, carry):
            to = lax.rem(my_inj + d, n_inj)
            remote(
                partial.at[side, to], shares.at[side, my_inj], share_send.at[side], share_recv.at[side], me, to
            ).start()
            return carry

        lax.fori_loop(1, n_inj, step, 0)
        shares[side, my_inj] = partial[side, my_inj]

    term(0, 0)
    term(0, 1)
    around[1][0].wait()
    sweep(1, asrc, aa, ab, [1, 2, 3], w0)
    sweep(1, asrc, ab, aa, [2, 3, 4], w1)
    sweep(1, asrc, aa, ab, [3, 4, 5], w2)
    term(1, 0)
    send_share(0)
    around[1][1].wait()
    sweep(1, asrc, aa, ab, [end - 3, end - 2, end - 1], w0)
    sweep(1, asrc, ab, aa, [end - 4, end - 3, end - 2], w1)
    sweep(1, asrc, aa, ab, [end - 5, end - 4, end - 3], w2)
    term(1, 1)
    send_share(1)

    ret_got = pltpu.make_async_copy(ret_recv.at[pl.ds(0, n_space - 1)], ret_recv.at[pl.ds(0, n_space - 1)], ret_recv_sem)
    ret_got.wait()
    lane_j = lax.rem(iota((1, lanes), 1), 2).astype(F32)
    back = jnp.where(iota((n_space * 4, lanes), 0).astype(F32) == slot_c * 2.0 + lane_j, 1.0, 0.0)
    back = jnp.transpose(back)[: 2 * blocks]
    returned = jnp.concatenate([ret_recv[t] for t in range(n_space)], axis=0)
    res_out[...] = jnp.dot(back, returned, precision=HIGHEST, preferred_element_type=F32)

    for side in range(2):
        window = shares.at[side, pl.ds(0, n_inj - 1)]
        pltpu.make_async_copy(window, window, share_recv.at[side]).wait()
        total = shares[side, 0]
        for k in range(1, n_inj):
            total = total + shares[side, k]
        grad_out[pl.ds(side * half, half)] = total

    pltpu.make_async_copy(send.at[pl.ds(0, n_space - 1)], send.at[pl.ds(0, n_space - 1)], block_send).wait()
    pltpu.make_async_copy(ret_send.at[pl.ds(0, n_space - 1)], ret_send.at[pl.ds(0, n_space - 1)], ret_send_sem).wait()
    for side in range(2):
        window = partial.at[side, pl.ds(0, n_inj - 1)]
        pltpu.make_async_copy(window, window, share_send.at[side]).wait()


def body(
    conductivity, start_potential, start_adjoint, inj_cells, dipole_cells, owner_tile, live_count, observed,
):
    n_space, n_inj = lax.axis_size("space"), lax.axis_size("inj")
    nx, ny, nz = conductivity.shape
    blocks, elec = observed.shape[1], observed.shape[3]
    planes, tall_rows = nx + 2 * H, ny + 2 * PAD
    wide, tall = 2 * nz, nx // 2 * ny
    hbm = pl.BlockSpec(memory_space=pltpu.HBM)
    vmem = pl.BlockSpec(memory_space=pltpu.VMEM)
    field = pltpu.VMEM((2, planes, tall_rows, nz), F32)
    dma = pltpu.SemaphoreType.DMA
    gradient, residual = pl.pallas_call(
        functools.partial(kernel, n_space, n_inj, nx, ny, nz, blocks),
        out_shape=(
            jax.ShapeDtypeStruct((nx, ny // n_inj, nz), F32),
            jax.ShapeDtypeStruct((2 * blocks, elec), F32),
        ),
        in_specs=[hbm] * 8,
        out_specs=(vmem, vmem),
        scratch_shapes=[
            pltpu.SMEM((2, 2), jnp.int32),
            pltpu.VMEM((1, blocks), jnp.int32),
            pltpu.VMEM((1, blocks), jnp.int32),
            pltpu.VMEM((2 * blocks, elec), jnp.int32),
            pltpu.VMEM((2 * blocks, elec), F32),
            pltpu.VMEM((planes, tall_rows, nz), F32),
            field, field, field, field,
            pltpu.VMEM((7, planes, ny, nz), F32),
            pltpu.VMEM((2, planes, ny, nz), F32),
            pltpu.VMEM((2, planes, ny, nz), F32),
            pltpu.VMEM((n_space, 8, elec), F32),
            pltpu.VMEM((n_space, 8, elec), F32),
            pltpu.VMEM((n_space, 4, elec), F32),
            pltpu.VMEM((n_space, 4, elec), F32),
            pltpu.VMEM((2, 2, ny, nz), F32),
            pltpu.VMEM((n_space, wide, 4 * elec), BF16),
            pltpu.VMEM((2, 2 * tall, wide), BF16),
            pltpu.VMEM((2 * tall, wide), F32),
            pltpu.VMEM((2, n_inj, nx // 2, ny // n_inj, nz), F32),
            pltpu.VMEM((2, n_inj, nx // 2, ny // n_inj, nz), F32),
            dma((8,)), dma((6,)), dma((6,)), dma((4,)), dma((4,)), dma, dma,
            dma, dma, dma((4,)), dma((4,)), dma((4,)), dma((4,)), dma((2,)), dma((2,)),
        ],
        compiler_params=pltpu.CompilerParams(
            collective_id=0, has_side_effects=True, vmem_limit_bytes=60 * 1024 * 1024
        ),
    )(
        conductivity, start_potential, start_adjoint, inj_cells,
        owner_tile.reshape(1, blocks), live_count,
        dipole_cells.reshape(2 * blocks, elec), observed.reshape(2 * blocks, elec),
    )
    return gradient, residual.reshape(1, blocks, 2, elec)


def solution(mesh):
    return jax.shard_map(
        body,
        mesh=mesh,
        in_specs=(
            P("space", None, None),
            P("inj", "space", None, None),
            P("inj", "space", None, None),
            P("inj", None),
            P("inj", "space", None, None),
            P("inj", "space", None),
            P("inj", "space"),
            P("inj", "space", None, None),
        ),
        out_specs=(P("space", "inj", None), P("inj", "space", None, None)),
        check_vma=False,
    )
```

```python
import functools
import math

import jax
import jax.numpy as jnp
from jax import lax
from jax.experimental import pallas as pl
from jax.experimental.pallas import tpu as pltpu
from jax.sharding import PartitionSpec as P

MESH = pl.DeviceIdType.MESH
F32 = jnp.float32
BF16 = jnp.bfloat16
HIGHEST = lax.Precision.HIGHEST

current_amp = 4.0
sweep_weights = [
    1.0 / (1.0 + 0.9 * math.cos((2 * step_k + 1) * math.pi / 6.0)) for step_k in range(3)
]

H = 4
PAD = 8


def iota(shape, dim):
    return lax.broadcasted_iota(jnp.int32, shape, dim)


def rows_sum(values):
    return jnp.sum(values, axis=0, keepdims=True)


def kernel(
    n_space, n_inj, nx, ny, nz, blocks,
    sig_in, pot_in, adj_in, inj_in, owner_in, live_in, cells_in, observed_in,
    shares, res_out,
    inj_cells, owner, live, cells, observed, sigma, pa, pb, aa, ab, coef, src, asrc, send, recv, ret_send, ret_recv,
    rim, onehot, table, scat, partial, res,
    local_sem, halo_send, halo_recv, far_send, far_recv, block_send, block_recv,
    ret_send_sem, ret_recv_sem, rim_send, rim_recv, asrc_send, asrc_recv, share_send, share_recv,
):
    me = lax.axis_index("space")
    my_inj = lax.axis_index("inj")
    left = lax.rem(me + n_space - 1, n_space)
    right = lax.rem(me + 1, n_space)
    planes = nx + 2 * H
    rows = pl.ds(PAD, ny)
    half = nx // 2
    tall = half * ny
    wide = 2 * nz
    half_cells = float(half * ny * nz)
    group = math.gcd(n_space, 16)

    barrier = pltpu.get_barrier_semaphore()

    def greet(to):
        pl.semaphore_signal(barrier, inc=1, device_id=to, device_id_type=MESH)

    def greet_space(d, carry):
        greet((lax.rem(me + d, n_space), my_inj))
        return carry

    def greet_inj(d, carry):
        greet((me, lax.rem(my_inj + d, n_inj)))
        return carry

    greet((left, my_inj))
    greet((right, my_inj))
    lax.fori_loop(2, n_space - 1, greet_space, 0)
    lax.fori_loop(1, n_inj, greet_inj, 0)

    small = [
        pltpu.make_async_copy(source, target, local_sem.at[3 + k])
        for k, (source, target) in enumerate(
            ((inj_in, inj_cells), (owner_in, owner), (live_in, live), (cells_in, cells), (observed_in, observed))
        )
    ]
    locals_ = [
        pltpu.make_async_copy(sig_in, sigma.at[pl.ds(H, nx), rows], local_sem.at[0]),
        pltpu.make_async_copy(pot_in, pa.at[:, pl.ds(H, nx), rows], local_sem.at[1]),
        pltpu.make_async_copy(adj_in, aa.at[:, pl.ds(H, nx), rows], local_sem.at[2]),
    ]
    for copy in small + locals_:
        copy.start()

    for low in (0, PAD + ny):
        sigma[:, pl.ds(low, PAD), :] = jnp.zeros((planes, PAD, nz), F32)
        for buf in (pa, pb, aa, ab):
            buf[:, :, pl.ds(low, PAD), :] = jnp.zeros((2, planes, PAD, nz), F32)

    pl.semaphore_wait(barrier, n_space - 1 + n_inj - 1)

    def remote(source, target, send_sem, recv_sem, space, inj):
        return pltpu.make_async_remote_copy(
            src_ref=source, dst_ref=target, send_sem=send_sem, recv_sem=recv_sem,
            device_id=(space, inj), device_id_type=MESH,
        )

    def pair(source, target, lead, width, send_sems, recv_sems, k):
        return [
            remote(
                source.at[lead + (pl.ds(nx - width, width),)], target.at[lead + (pl.ds(H - width, width), rows)],
                send_sems.at[k], recv_sems.at[k], right, my_inj,
            ),
            remote(
                source.at[lead + (pl.ds(0, width),)], target.at[lead + (pl.ds(nx + H, width), rows)],
                send_sems.at[k + 1], recv_sems.at[k + 1], left, my_inj,
            ),
        ]

    early = pair(sig_in, sigma, (), 3, halo_send, halo_recv, 0)
    near = [pair(pot_in, pa, (i,), 3, halo_send, halo_recv, 2 + 2 * i) for i in range(2)]
    late = [
        remote(sig_in.at[pl.ds(nx - H, 1)], sigma.at[pl.ds(0, 1), rows], far_send.at[0], far_recv.at[0], right, my_inj),
        remote(sig_in.at[pl.ds(H - 1, 1)], sigma.at[pl.ds(planes - 1, 1), rows], far_send.at[1], far_recv.at[1], left, my_inj),
    ] + pair(adj_in, aa, (slice(None),), H, far_send, far_recv, 2)
    for copy in early + near[0]:
        copy.start()

    for copy in small:
        copy.wait()
    lanes = 4 * blocks
    lane_c = iota((blocks, lanes), 1)
    block_c = lax.rem(lane_c, 2 * blocks) // 2
    field_c = lax.rem(lane_c, 2) + 2 * (lane_c // (2 * blocks))
    row_b = iota((blocks, lanes), 0)
    owners = jnp.broadcast_to(owner[...].astype(F32), (blocks, blocks))
    owners = jnp.where(iota((blocks, blocks), 0) == iota((blocks, blocks), 1), owners, 0.0)
    owners = jnp.broadcast_to(jnp.sum(owners, axis=1, keepdims=True), (blocks, lanes))
    owner_c = rows_sum(jnp.where(row_b == block_c, owners, 0.0))
    earlier = (owners == owner_c) & (row_b < block_c)
    rank_c = rows_sum(jnp.where(earlier, 1.0, 0.0))
    slot_c = owner_c * 2.0 + rank_c
    target = slot_c * 4.0 + field_c[:1].astype(F32)
    place = jnp.where(iota((n_space * 8, lanes), 0).astype(F32) == target, 1.0, 0.0)

    row_r = iota((lanes, blocks), 0)
    block_r = lax.rem(row_r, 2 * blocks) // 2
    lives = jnp.broadcast_to(live[...].astype(F32), (lanes, blocks))
    live_r = jnp.sum(jnp.where(block_r == iota((lanes, blocks), 1), lives, 0.0), axis=1, keepdims=True)
    data = jnp.concatenate([cells[...].astype(F32) + 1.0, observed[...]], axis=0)
    elec = data.shape[1]
    data = jnp.where(iota((lanes, elec), 1).astype(F32) < live_r, data, 0.0)
    packed = jnp.dot(place, data, precision=HIGHEST, preferred_element_type=F32)
    for t in range(n_space):
        send[t] = packed[8 * t : 8 * t + 8]

    def send_block(d, carry):
        to = lax.rem(me + d, n_space)
        remote(send.at[to], recv.at[me], block_send, block_recv, to, my_inj).start()
        return carry

    lax.fori_loop(1, n_space, send_block, 0)
    for copy in near[1]:
        copy.start()
    recv[me] = send[me]

    cell_ids = iota((ny, nz), 0) * nz + iota((ny, nz), 1)

    for p in range(2, planes - 2):
        first = (me * nx - H + p) * (ny * nz)
        for i in range(2):
            plus = jnp.where(cell_ids == inj_cells[i, 0] - first, current_amp, 0.0)
            minus = jnp.where(cell_ids == inj_cells[i, 1] - first, current_amp, 0.0)
            src[i, p] = plus - minus

    def beyond(buf, lead, low_side, width):
        nothing = jnp.zeros((width, ny, nz), F32)

        @pl.when(me == (0 if low_side else n_space - 1))
        def _():
            buf[lead + (pl.ds(H - width if low_side else nx + H, width), rows)] = nothing

    chunk = ny // 2

    def in_chunks(work):
        def step(q, carry):
            low = pl.multiple_of(q * chunk, 8)
            work(low, pl.ds(pl.multiple_of(low + PAD, 8), chunk))
            return carry

        lax.fori_loop(0, ny // chunk, step, 0)

    first_lane = iota((chunk, nz), 1) == 0
    last_lane = iota((chunk, nz), 1) == nz - 1

    def next_z(value):
        return jnp.where(last_lane, 0.0, pltpu.roll(value, nz - 1, 1))

    def last_z(value):
        return jnp.where(first_lane, 0.0, pltpu.roll(value, 1, 1))

    def faces(which):
        def work(low, at):
            for p in which:
                here = sigma[p, at, :]
                around = [
                    sigma[p + 1, at, :], sigma[p - 1, at, :],
                    sigma[p, pl.ds(low + PAD + 1, chunk), :], sigma[p, pl.ds(low + PAD - 1, chunk), :],
                    next_z(here), last_z(here),
                ]
                around = [0.5 * (here + value) for value in around]
                diag = around[0] + around[1] + around[2] + around[3] + around[4] + around[5]
                plane = me * nx - H + p
                inside = jnp.where((plane >= 0) & (plane < n_space * nx), 1.0, 0.0)
                inverse = inside / jnp.where(diag > 0.0, diag, 1.0)
                around[4] = jnp.where(last_lane, 0.0, around[4])
                around[5] = jnp.where(first_lane, 0.0, around[5])
                for k in range(6):
                    coef[k, p, pl.ds(low, chunk), :] = around[k] * inverse
                coef[6, p, pl.ds(low, chunk), :] = inverse

        in_chunks(work)

    def sweep(i, source, old, new, which, weight):
        def work(low, at):
            for p in which:
                c = [coef[k, p, pl.ds(low, chunk), :] for k in range(7)]
                here = old[i, p, at, :]
                beside = c[0] * old[i, p + 1, at, :] + c[1] * old[i, p - 1, at, :]
                beside = beside + (
                    c[2] * old[i, p, pl.ds(low + PAD + 1, chunk), :] + c[3] * old[i, p, pl.ds(low + PAD - 1, chunk), :]
                )
                beside = beside + (c[4] * pltpu.roll(here, nz - 1, 1) + c[5] * pltpu.roll(here, 1, 1))
                beside = beside + c[6] * source[i, p, pl.ds(low, chunk), :]
                new[i, p, at, :] = here + weight * (beside - here)

        in_chunks(work)

    w0, w1, w2 = sweep_weights
    end = planes - 1

    locals_[0].wait()
    faces(range(H + 1, end - H))
    locals_[1].wait()
    for i in range(2):
        sweep(i, src, pa, pb, range(H + 1, end - H), w0)
        sweep(i, src, pb, pa, range(H + 2, end - H - 1), w1)

    for copy in early:
        copy.wait()
    beyond(sigma, (), True, 3)
    beyond(sigma, (), False, 3)
    faces([2, 3, 4, end - 4, end - 3, end - 2])

    def finish_potential(i):
        for copy in near[i]:
            copy.wait()
        beyond(pa, (i,), True, 3)
        beyond(pa, (i,), False, 3)
        sweep(i, src, pa, pb, [2, 3, 4, end - 4, end - 3, end - 2], w0)
        sweep(i, src, pb, pa, [3, 4, 5, end - 5, end - 4, end - 3], w1)
        sweep(i, src, pa, pb, range(H, H + nx), w2)
        for x in range(nx):
            value = pb[i, H + x, rows, :]
            high = value.astype(BF16)
            low = (value - high.astype(F32)).astype(BF16)
            first, columns = (x % half) * ny, pl.ds((x // half) * nz, nz)
            table[i, pl.ds(first, ny), columns] = high
            table[i, pl.ds(tall + first, ny), columns] = low

    wide_iota = iota((wide, elec), 0).astype(F32).astype(BF16)
    tall_iota = iota((tall, elec), 0).astype(F32)
    tall_iota16 = tall_iota.astype(BF16)
    one = jnp.ones((wide, elec), BF16)
    none = jnp.zeros((wide, elec), BF16)

    def split_cells(t):
        cell = recv[t] - 1.0
        upper = cell >= half_cells
        within = jnp.where(upper, cell - half_cells, cell)
        tall_at = jnp.floor(within * (1.0 / nz))
        wide_at = within - tall_at * nz + jnp.where(upper, float(nz), 0.0)
        return tall_at, jnp.where(cell < 0.0, -1.0, wide_at)

    def mark(t, carry):
        _, wide_at = split_cells(t)
        for s in range(2):
            for f in range(2):
                row = jnp.broadcast_to(wide_at[4 * s + f : 4 * s + f + 1], (wide, elec)).astype(BF16)
                onehot[t, :, pl.ds((2 * s + f) * elec, elec)] = jnp.where(wide_iota == row, one, none)
        return carry

    def fetch(i):
        def step(u, carry):
            for k in range(group):
                t = u * group + k
                tall_at, _ = split_cells(t)
                found = jnp.dot(table[i], onehot[t], preferred_element_type=F32)
                for s in range(2):
                    ends = []
                    for f in range(2):
                        here = tall_iota == tall_at[4 * s + f : 4 * s + f + 1]
                        at = slice((2 * s + f) * elec, (2 * s + f + 1) * elec)
                        ends.append(rows_sum(jnp.where(here, found[:tall, at] + found[tall:, at], 0.0)))
                    ret_send[t, pl.ds(2 * s + i, 1), :] = ends[0] - ends[1] - recv[t, pl.ds(4 * s + 2 + i, 1), :]
            return carry

        lax.fori_loop(0, n_space // group, step, 0)

    def spread(i):
        scat[...] = jnp.zeros_like(scat)

        def step(u, carry):
            amounts, hots = [], []
            for k in range(group):
                t = u * group + k
                tall_at, _ = split_cells(t)
                misfit = ret_send[t]
                high = misfit.astype(BF16).astype(F32)
                for s in range(2):
                    for f in range(2):
                        sign = 1.0 if f == 0 else -1.0
                        row = jnp.broadcast_to(tall_at[4 * s + f : 4 * s + f + 1], (tall, elec)).astype(BF16)
                        here = tall_iota16 == row
                        pieces = []
                        for value in (high, misfit - high):
                            amount = jnp.broadcast_to(sign * value[2 * s + i : 2 * s + i + 1], (tall, elec)).astype(BF16)
                            pieces.append(jnp.where(here, amount, jnp.zeros((tall, elec), BF16)))
                        amounts.append(jnp.concatenate(pieces, axis=0))
                hots.append(onehot[t])
            scat[...] += lax.dot_general(
                jnp.concatenate(amounts, axis=1), jnp.concatenate(hots, axis=1), (((1,), (1,)), ((), ())),
                preferred_element_type=F32,
            )
            return carry

        lax.fori_loop(0, n_space // group, step, 0)
        for x in range(nx):
            first, columns = (x % half) * ny, pl.ds((x // half) * nz, nz)
            asrc[i, H + x] = scat[pl.ds(first, ny), columns] + scat[pl.ds(tall + first, ny), columns]

    rims = [
        [
            remote(pb.at[i, H + nx - 1, rows], rim.at[0, i], rim_send.at[2 * i], rim_recv.at[2 * i], right, my_inj),
            remote(pb.at[i, H, rows], rim.at[1, i], rim_send.at[2 * i + 1], rim_recv.at[2 * i + 1], left, my_inj),
        ]
        for i in range(2)
    ]
    around = [
        [
            remote(
                asrc.at[i, pl.ds(H + nx - 3, 3)], asrc.at[i, pl.ds(1, 3)],
                asrc_send.at[2 * i], asrc_recv.at[2 * i], right, my_inj,
            ),
            remote(
                asrc.at[i, pl.ds(H, 3)], asrc.at[i, pl.ds(H + nx, 3)],
                asrc_send.at[2 * i + 1], asrc_recv.at[2 * i + 1], left, my_inj,
            ),
        ]
        for i in range(2)
    ]

    finish_potential(0)
    for copy in rims[0]:
        copy.start()
    got = pltpu.make_async_copy(recv.at[pl.ds(0, n_space - 1)], recv.at[pl.ds(0, n_space - 1)], block_recv)
    got.wait()
    lax.fori_loop(0, n_space, mark, 0)
    fetch(0)
    finish_potential(1)
    for copy in late + rims[1]:
        copy.start()
    spread(0)
    for copy in around[0]:
        copy.start()
    fetch(1)

    def send_ret(d, carry):
        to = lax.rem(me + d, n_space)
        remote(ret_send.at[to], ret_recv.at[me], ret_send_sem, ret_recv_sem, to, my_inj).start()
        return carry

    lax.fori_loop(1, n_space, send_ret, 0)
    ret_recv[me] = ret_send[me]

    spread(1)
    for copy in around[1]:
        copy.start()

    locals_[2].wait()
    for copy in late:
        copy.wait()
    for low_side in (True, False):
        beyond(sigma, (), low_side, H)
        for i in range(2):
            beyond(aa, (i,), low_side, H)
    faces([1, end - 1])
    for i in range(2):
        for copy in rims[i]:
            copy.wait()
        pb[i, H - 1, rows, :] = jnp.where(me == 0, 0.0, rim[0, i])
        pb[i, H + nx, rows, :] = jnp.where(me == n_space - 1, 0.0, rim[1, i])

    for copy in around[0]:
        copy.wait()
    sweep(0, asrc, aa, ab, range(1, planes - 1), w0)
    sweep(0, asrc, ab, aa, range(2, planes - 2), w1)
    sweep(0, asrc, aa, ab, range(3, planes - 3), w2)
    sweep(1, asrc, aa, ab, range(H, H + nx), w0)
    sweep(1, asrc, ab, aa, range(H + 1, end - H), w1)
    sweep(1, asrc, aa, ab, range(H + 2, end - H - 1), w2)

    def term(i, side):
        def work(low, at):
            part = ny // n_inj
            where = pl.ds(low // part, chunk // part)
            for x in range(half):
                p = H + side * half + x
                here, there = pb[i, p, at, :], ab[i, p, at, :]
                ahead, behind = pl.ds(low + PAD + 1, chunk), pl.ds(low + PAD - 1, chunk)
                pairs = [
                    (pb[i, p + 1, at, :], ab[i, p + 1, at, :]),
                    (pb[i, p - 1, at, :], ab[i, p - 1, at, :]),
                    (pb[i, p, ahead, :], ab[i, p, ahead, :]),
                    (pb[i, p, behind, :], ab[i, p, behind, :]),
                    (next_z(here), next_z(there)),
                    (last_z(here), last_z(there)),
                ]
                total = jnp.zeros((chunk, nz), F32)
                for u, v in pairs:
                    total = total + (here - u) * (there - v)
                total = (-0.5 * total).reshape(chunk // part, part, nz)
                partial[side, where, x] = total if i == 0 else partial[side, where, x] + total

        in_chunks(work)

    def own_share(side):
        return pltpu.make_async_copy(partial.at[side, my_inj], shares.at[side, my_inj], local_sem.at[8 + side])

    def send_share(side):
        def step(d, carry):
            to = lax.rem(my_inj + d, n_inj)
            remote(
                partial.at[side, to], shares.at[side, my_inj], share_send.at[side], share_recv.at[side], me, to
            ).start()
            return carry

        lax.fori_loop(1, n_inj, step, 0)
        own_share(side).start()

    term(0, 0)
    term(0, 1)
    around[1][0].wait()
    sweep(1, asrc, aa, ab, [1, 2, 3], w0)
    sweep(1, asrc, ab, aa, [2, 3, 4], w1)
    sweep(1, asrc, aa, ab, [3, 4, 5], w2)
    term(1, 0)
    send_share(0)
    around[1][1].wait()
    sweep(1, asrc, aa, ab, [end - 3, end - 2, end - 1], w0)
    sweep(1, asrc, ab, aa, [end - 4, end - 3, end - 2], w1)
    sweep(1, asrc, aa, ab, [end - 5, end - 4, end - 3], w2)
    term(1, 1)
    send_share(1)

    ret_got = pltpu.make_async_copy(ret_recv.at[pl.ds(0, n_space - 1)], ret_recv.at[pl.ds(0, n_space - 1)], ret_recv_sem)
    ret_got.wait()
    lane_j = lax.rem(iota((1, lanes), 1), 2).astype(F32)
    back = jnp.where(iota((n_space * 4, lanes), 0).astype(F32) == slot_c * 2.0 + lane_j, 1.0, 0.0)
    back = jnp.transpose(back)[: 2 * blocks]
    returned = jnp.concatenate([ret_recv[t] for t in range(n_space)], axis=0)
    res[...] = jnp.dot(back, returned, precision=HIGHEST, preferred_element_type=F32)
    res_copy = pltpu.make_async_copy(res, res_out, local_sem.at[10])
    res_copy.start()

    pltpu.make_async_copy(send.at[pl.ds(0, n_space - 1)], send.at[pl.ds(0, n_space - 1)], block_send).wait()
    pltpu.make_async_copy(ret_send.at[pl.ds(0, n_space - 1)], ret_send.at[pl.ds(0, n_space - 1)], ret_send_sem).wait()
    for side in range(2):
        window = partial.at[side, pl.ds(0, n_inj - 1)]
        pltpu.make_async_copy(window, window, share_send.at[side]).wait()
        own_share(side).wait()
    res_copy.wait()
    for side in range(2):
        window = shares.at[side, pl.ds(0, n_inj - 1)]
        pltpu.make_async_copy(window, window, share_recv.at[side]).wait()


def gather_up(shares, res_in, gradient, res_out, sem):
    copy = pltpu.make_async_copy(res_in, res_out, sem)
    copy.start()
    n_inj, half = shares.shape[1], shares.shape[2]
    for side in range(2):
        total = shares[side, 0]
        for k in range(1, n_inj):
            total = total + shares[side, k]
        gradient[pl.ds(side * half, half)] = total
    copy.wait()


def body(
    conductivity, start_potential, start_adjoint, inj_cells, dipole_cells, owner_tile, live_count, observed,
):
    n_space, n_inj = lax.axis_size("space"), lax.axis_size("inj")
    nx, ny, nz = conductivity.shape
    blocks, elec = observed.shape[1], observed.shape[3]
    planes, tall_rows = nx + 2 * H, ny + 2 * PAD
    wide, tall = 2 * nz, nx // 2 * ny
    hbm = pl.BlockSpec(memory_space=pltpu.HBM)
    vmem = pl.BlockSpec(memory_space=pltpu.VMEM)
    field = pltpu.VMEM((2, planes, tall_rows, nz), F32)
    dma = pltpu.SemaphoreType.DMA
    shares, residual = pl.pallas_call(
        functools.partial(kernel, n_space, n_inj, nx, ny, nz, blocks),
        out_shape=(
            jax.ShapeDtypeStruct((2, n_inj, nx // 2, ny // n_inj, nz), F32),
            jax.ShapeDtypeStruct((2 * blocks, elec), F32),
        ),
        in_specs=[hbm] * 8,
        out_specs=(hbm, hbm),
        scratch_shapes=[
            pltpu.SMEM((2, 2), jnp.int32),
            pltpu.VMEM((1, blocks), jnp.int32),
            pltpu.VMEM((1, blocks), jnp.int32),
            pltpu.VMEM((2 * blocks, elec), jnp.int32),
            pltpu.VMEM((2 * blocks, elec), F32),
            pltpu.VMEM((planes, tall_rows, nz), F32),
            field, field, field, field,
            pltpu.VMEM((7, planes, ny, nz), F32),
            pltpu.VMEM((2, planes, ny, nz), F32),
            pltpu.VMEM((2, planes, ny, nz), F32),
            pltpu.VMEM((n_space, 8, elec), F32),
            pltpu.VMEM((n_space, 8, elec), F32),
            pltpu.VMEM((n_space, 4, elec), F32),
            pltpu.VMEM((n_space, 4, elec), F32),
            pltpu.VMEM((2, 2, ny, nz), F32),
            pltpu.VMEM((n_space, wide, 4 * elec), BF16),
            pltpu.VMEM((2, 2 * tall, wide), BF16),
            pltpu.VMEM((2 * tall, wide), F32),
            pltpu.VMEM((2, n_inj, nx // 2, ny // n_inj, nz), F32),
            pltpu.VMEM((2 * blocks, elec), F32),
            dma((11,)), dma((6,)), dma((6,)), dma((4,)), dma((4,)), dma, dma,
            dma, dma, dma((4,)), dma((4,)), dma((4,)), dma((4,)), dma((2,)), dma((2,)),
        ],
        compiler_params=pltpu.CompilerParams(
            collective_id=0, has_side_effects=True, vmem_limit_bytes=60 * 1024 * 1024
        ),
    )(
        conductivity, start_potential, start_adjoint, inj_cells,
        owner_tile.reshape(1, blocks), live_count,
        dipole_cells.reshape(2 * blocks, elec), observed.reshape(2 * blocks, elec),
    )
    gradient, residual = pl.pallas_call(
        gather_up,
        out_shape=(
            jax.ShapeDtypeStruct((nx, ny // n_inj, nz), F32),
            jax.ShapeDtypeStruct((2 * blocks, elec), F32),
        ),
        in_specs=[vmem, hbm],
        out_specs=(vmem, hbm),
        scratch_shapes=[dma],
        compiler_params=pltpu.CompilerParams(vmem_limit_bytes=60 * 1024 * 1024),
    )(shares, residual)
    return gradient, residual.reshape(1, blocks, 2, elec)


def solution(mesh):
    return jax.shard_map(
        body,
        mesh=mesh,
        in_specs=(
            P("space", None, None),
            P("inj", "space", None, None),
            P("inj", "space", None, None),
            P("inj", None),
            P("inj", "space", None, None),
            P("inj", "space", None),
            P("inj", "space"),
            P("inj", "space", None, None),
        ),
        out_specs=(P("space", "inj", None), P("inj", "space", None, None)),
        check_vma=False,
    )
```

```python
import functools
import math

import jax
import jax.numpy as jnp
from jax import lax
from jax.experimental import pallas as pl
from jax.experimental.pallas import tpu as pltpu
from jax.sharding import PartitionSpec as P

MESH = pl.DeviceIdType.MESH
F32 = jnp.float32
BF16 = jnp.bfloat16
HIGHEST = lax.Precision.HIGHEST

current_amp = 4.0
sweep_weights = [
    1.0 / (1.0 + 0.9 * math.cos((2 * step_k + 1) * math.pi / 6.0)) for step_k in range(3)
]

H = 4
PAD = 8


def iota(shape, dim):
    return lax.broadcasted_iota(jnp.int32, shape, dim)


def rows_sum(values):
    return jnp.sum(values, axis=0, keepdims=True)


def kernel(
    n_space, n_inj, nx, ny, nz, blocks,
    sig_in, pot_in, adj_in, inj_in, owner_in, live_in, cells_in, observed_in,
    grad_out, res_out,
    inj_cells, owner, live, cells, observed, sigma, pa, pb, aa, ab, coef, src, asrc, send, recv, ret_send, ret_recv,
    rim, onehot, table, scat, partial, shares,
    local_sem, halo_send, halo_recv, far_send, far_recv, block_send, block_recv,
    ret_send_sem, ret_recv_sem, rim_send, rim_recv, asrc_send, asrc_recv, share_send, share_recv,
):
    me = lax.axis_index("space")
    my_inj = lax.axis_index("inj")
    left = lax.rem(me + n_space - 1, n_space)
    right = lax.rem(me + 1, n_space)
    planes = nx + 2 * H
    rows = pl.ds(PAD, ny)
    half = nx // 2
    tall = half * ny
    wide = 2 * nz
    half_cells = float(half * ny * nz)
    group = math.gcd(n_space, 16)

    barrier = pltpu.get_barrier_semaphore()

    def greet(to):
        pl.semaphore_signal(barrier, inc=1, device_id=to, device_id_type=MESH)

    def greet_space(d, carry):
        greet((lax.rem(me + d, n_space), my_inj))
        return carry

    def greet_inj(d, carry):
        greet((me, lax.rem(my_inj + d, n_inj)))
        return carry

    greet((left, my_inj))
    greet((right, my_inj))
    lax.fori_loop(2, n_space - 1, greet_space, 0)
    lax.fori_loop(1, n_inj, greet_inj, 0)

    small = [
        pltpu.make_async_copy(source, target, local_sem.at[3 + k])
        for k, (source, target) in enumerate(
            ((inj_in, inj_cells), (owner_in, owner), (live_in, live), (cells_in, cells), (observed_in, observed))
        )
    ]
    locals_ = [
        pltpu.make_async_copy(sig_in, sigma.at[pl.ds(H, nx), rows], local_sem.at[0]),
        pltpu.make_async_copy(pot_in, pa.at[:, pl.ds(H, nx), rows], local_sem.at[1]),
        pltpu.make_async_copy(adj_in, aa.at[:, pl.ds(H, nx), rows], local_sem.at[2]),
    ]
    for copy in small + locals_:
        copy.start()

    for low in (0, PAD + ny):
        sigma[:, pl.ds(low, PAD), :] = jnp.zeros((planes, PAD, nz), F32)
        for buf in (pa, pb, aa, ab):
            buf[:, :, pl.ds(low, PAD), :] = jnp.zeros((2, planes, PAD, nz), F32)

    pl.semaphore_wait(barrier, n_space - 1 + n_inj - 1)

    def remote(source, target, send_sem, recv_sem, space, inj):
        return pltpu.make_async_remote_copy(
            src_ref=source, dst_ref=target, send_sem=send_sem, recv_sem=recv_sem,
            device_id=(space, inj), device_id_type=MESH,
        )

    def pair(source, target, lead, width, send_sems, recv_sems, k):
        return [
            remote(
                source.at[lead + (pl.ds(nx - width, width),)], target.at[lead + (pl.ds(H - width, width), rows)],
                send_sems.at[k], recv_sems.at[k], right, my_inj,
            ),
            remote(
                source.at[lead + (pl.ds(0, width),)], target.at[lead + (pl.ds(nx + H, width), rows)],
                send_sems.at[k + 1], recv_sems.at[k + 1], left, my_inj,
            ),
        ]

    early = pair(sig_in, sigma, (), 3, halo_send, halo_recv, 0)
    near = [pair(pot_in, pa, (i,), 3, halo_send, halo_recv, 2 + 2 * i) for i in range(2)]
    late = [
        remote(sig_in.at[pl.ds(nx - H, 1)], sigma.at[pl.ds(0, 1), rows], far_send.at[0], far_recv.at[0], right, my_inj),
        remote(sig_in.at[pl.ds(H - 1, 1)], sigma.at[pl.ds(planes - 1, 1), rows], far_send.at[1], far_recv.at[1], left, my_inj),
    ] + pair(adj_in, aa, (slice(None),), H, far_send, far_recv, 2)
    for copy in early + near[0]:
        copy.start()

    for copy in small:
        copy.wait()
    lanes = 4 * blocks
    lane_c = iota((blocks, lanes), 1)
    block_c = lax.rem(lane_c, 2 * blocks) // 2
    field_c = lax.rem(lane_c, 2) + 2 * (lane_c // (2 * blocks))
    row_b = iota((blocks, lanes), 0)
    owners = jnp.broadcast_to(owner[...].astype(F32), (blocks, blocks))
    owners = jnp.where(iota((blocks, blocks), 0) == iota((blocks, blocks), 1), owners, 0.0)
    owners = jnp.broadcast_to(jnp.sum(owners, axis=1, keepdims=True), (blocks, lanes))
    owner_c = rows_sum(jnp.where(row_b == block_c, owners, 0.0))
    earlier = (owners == owner_c) & (row_b < block_c)
    rank_c = rows_sum(jnp.where(earlier, 1.0, 0.0))
    slot_c = owner_c * 2.0 + rank_c
    target = slot_c * 4.0 + field_c[:1].astype(F32)
    place = jnp.where(iota((n_space * 8, lanes), 0).astype(F32) == target, 1.0, 0.0)

    row_r = iota((lanes, blocks), 0)
    block_r = lax.rem(row_r, 2 * blocks) // 2
    lives = jnp.broadcast_to(live[...].astype(F32), (lanes, blocks))
    live_r = jnp.sum(jnp.where(block_r == iota((lanes, blocks), 1), lives, 0.0), axis=1, keepdims=True)
    data = jnp.concatenate([cells[...].astype(F32) + 1.0, observed[...]], axis=0)
    elec = data.shape[1]
    data = jnp.where(iota((lanes, elec), 1).astype(F32) < live_r, data, 0.0)
    packed = jnp.dot(place, data, precision=HIGHEST, preferred_element_type=F32)
    for t in range(n_space):
        send[t] = packed[8 * t : 8 * t + 8]

    def send_block(d, carry):
        to = lax.rem(me + d, n_space)
        remote(send.at[to], recv.at[me], block_send, block_recv, to, my_inj).start()
        return carry

    lax.fori_loop(1, n_space, send_block, 0)
    for copy in near[1]:
        copy.start()
    recv[me] = send[me]

    cell_ids = iota((ny, nz), 0) * nz + iota((ny, nz), 1)

    for p in range(2, planes - 2):
        first = (me * nx - H + p) * (ny * nz)
        for i in range(2):
            plus = jnp.where(cell_ids == inj_cells[i, 0] - first, current_amp, 0.0)
            minus = jnp.where(cell_ids == inj_cells[i, 1] - first, current_amp, 0.0)
            src[i, p] = plus - minus

    def beyond(buf, lead, low_side, width):
        nothing = jnp.zeros((width, ny, nz), F32)

        @pl.when(me == (0 if low_side else n_space - 1))
        def _():
            buf[lead + (pl.ds(H - width if low_side else nx + H, width), rows)] = nothing

    chunk = ny

    def in_chunks(work):
        work(0, pl.ds(PAD, ny))

    first_lane = iota((chunk, nz), 1) == 0
    last_lane = iota((chunk, nz), 1) == nz - 1

    def next_z(value):
        return jnp.where(last_lane, 0.0, pltpu.roll(value, nz - 1, 1))

    def last_z(value):
        return jnp.where(first_lane, 0.0, pltpu.roll(value, 1, 1))

    def faces(which):
        def work(low, at):
            for p in which:
                here = sigma[p, at, :]
                around = [
                    sigma[p + 1, at, :], sigma[p - 1, at, :],
                    sigma[p, pl.ds(low + PAD + 1, chunk), :], sigma[p, pl.ds(low + PAD - 1, chunk), :],
                    next_z(here), last_z(here),
                ]
                around = [0.5 * (here + value) for value in around]
                diag = around[0] + around[1] + around[2] + around[3] + around[4] + around[5]
                plane = me * nx - H + p
                inside = jnp.where((plane >= 0) & (plane < n_space * nx), 1.0, 0.0)
                inverse = inside / jnp.where(diag > 0.0, diag, 1.0)
                around[4] = jnp.where(last_lane, 0.0, around[4])
                around[5] = jnp.where(first_lane, 0.0, around[5])
                for k in range(6):
                    coef[k, p, pl.ds(low, chunk), :] = around[k] * inverse
                coef[6, p, pl.ds(low, chunk), :] = inverse

        in_chunks(work)

    def sweep(i, source, old, new, which, weight):
        def work(low, at):
            for p in which:
                c = [coef[k, p, pl.ds(low, chunk), :] for k in range(7)]
                here = old[i, p, at, :]
                beside = c[0] * old[i, p + 1, at, :] + c[1] * old[i, p - 1, at, :]
                beside = beside + (
                    c[2] * old[i, p, pl.ds(low + PAD + 1, chunk), :] + c[3] * old[i, p, pl.ds(low + PAD - 1, chunk), :]
                )
                beside = beside + (c[4] * pltpu.roll(here, nz - 1, 1) + c[5] * pltpu.roll(here, 1, 1))
                beside = beside + c[6] * source[i, p, pl.ds(low, chunk), :]
                new[i, p, at, :] = here + weight * (beside - here)

        in_chunks(work)

    w0, w1, w2 = sweep_weights
    end = planes - 1

    locals_[0].wait()
    faces(range(H + 1, end - H))
    locals_[1].wait()
    for i in range(2):
        sweep(i, src, pa, pb, range(H + 1, end - H), w0)
        sweep(i, src, pb, pa, range(H + 2, end - H - 1), w1)

    for copy in early:
        copy.wait()
    beyond(sigma, (), True, 3)
    beyond(sigma, (), False, 3)
    faces([2, 3, 4, end - 4, end - 3, end - 2])

    def finish_potential(i):
        for copy in near[i]:
            copy.wait()
        beyond(pa, (i,), True, 3)
        beyond(pa, (i,), False, 3)
        sweep(i, src, pa, pb, [2, 3, 4, end - 4, end - 3, end - 2], w0)
        sweep(i, src, pb, pa, [3, 4, 5, end - 5, end - 4, end - 3], w1)
        sweep(i, src, pa, pb, range(H, H + nx), w2)
        for x in range(nx):
            value = pb[i, H + x, rows, :]
            high = value.astype(BF16)
            low = (value - high.astype(F32)).astype(BF16)
            first, columns = (x % half) * ny, pl.ds((x // half) * nz, nz)
            table[i, pl.ds(first, ny), columns] = high
            table[i, pl.ds(tall + first, ny), columns] = low

    wide_iota = iota((wide, elec), 0).astype(F32).astype(BF16)
    tall_iota = iota((tall, elec), 0).astype(F32)
    tall_iota16 = tall_iota.astype(BF16)
    one = jnp.ones((wide, elec), BF16)
    none = jnp.zeros((wide, elec), BF16)

    def split_cells(t):
        cell = recv[t] - 1.0
        upper = cell >= half_cells
        within = jnp.where(upper, cell - half_cells, cell)
        tall_at = jnp.floor(within * (1.0 / nz))
        wide_at = within - tall_at * nz + jnp.where(upper, float(nz), 0.0)
        return tall_at, jnp.where(cell < 0.0, -1.0, wide_at)

    def mark(t, carry):
        _, wide_at = split_cells(t)
        for s in range(2):
            for f in range(2):
                row = jnp.broadcast_to(wide_at[4 * s + f : 4 * s + f + 1], (wide, elec)).astype(BF16)
                onehot[t, :, pl.ds((2 * s + f) * elec, elec)] = jnp.where(wide_iota == row, one, none)
        return carry

    def fetch(i):
        def step(u, carry):
            for k in range(group):
                t = u * group + k
                tall_at, _ = split_cells(t)
                found = jnp.dot(table[i], onehot[t], preferred_element_type=F32)
                for s in range(2):
                    ends = []
                    for f in range(2):
                        here = tall_iota == tall_at[4 * s + f : 4 * s + f + 1]
                        at = slice((2 * s + f) * elec, (2 * s + f + 1) * elec)
                        ends.append(rows_sum(jnp.where(here, found[:tall, at] + found[tall:, at], 0.0)))
                    ret_send[t, pl.ds(2 * s + i, 1), :] = ends[0] - ends[1] - recv[t, pl.ds(4 * s + 2 + i, 1), :]
            return carry

        lax.fori_loop(0, n_space // group, step, 0)

    def spread(i):
        scat[...] = jnp.zeros_like(scat)

        def step(u, carry):
            amounts, hots = [], []
            for k in range(group):
                t = u * group + k
                tall_at, _ = split_cells(t)
                misfit = ret_send[t]
                high = misfit.astype(BF16).astype(F32)
                for s in range(2):
                    for f in range(2):
                        sign = 1.0 if f == 0 else -1.0
                        row = jnp.broadcast_to(tall_at[4 * s + f : 4 * s + f + 1], (tall, elec)).astype(BF16)
                        here = tall_iota16 == row
                        pieces = []
                        for value in (high, misfit - high):
                            amount = jnp.broadcast_to(sign * value[2 * s + i : 2 * s + i + 1], (tall, elec)).astype(BF16)
                            pieces.append(jnp.where(here, amount, jnp.zeros((tall, elec), BF16)))
                        amounts.append(jnp.concatenate(pieces, axis=0))
                hots.append(onehot[t])
            scat[...] += lax.dot_general(
                jnp.concatenate(amounts, axis=1), jnp.concatenate(hots, axis=1), (((1,), (1,)), ((), ())),
                preferred_element_type=F32,
            )
            return carry

        lax.fori_loop(0, n_space // group, step, 0)
        for x in range(nx):
            first, columns = (x % half) * ny, pl.ds((x // half) * nz, nz)
            asrc[i, H + x] = scat[pl.ds(first, ny), columns] + scat[pl.ds(tall + first, ny), columns]

    rims = [
        [
            remote(pb.at[i, H + nx - 1, rows], rim.at[0, i], rim_send.at[2 * i], rim_recv.at[2 * i], right, my_inj),
            remote(pb.at[i, H, rows], rim.at[1, i], rim_send.at[2 * i + 1], rim_recv.at[2 * i + 1], left, my_inj),
        ]
        for i in range(2)
    ]
    around = [
        [
            remote(
                asrc.at[i, pl.ds(H + nx - 3, 3)], asrc.at[i, pl.ds(1, 3)],
                asrc_send.at[2 * i], asrc_recv.at[2 * i], right, my_inj,
            ),
            remote(
                asrc.at[i, pl.ds(H, 3)], asrc.at[i, pl.ds(H + nx, 3)],
                asrc_send.at[2 * i + 1], asrc_recv.at[2 * i + 1], left, my_inj,
            ),
        ]
        for i in range(2)
    ]

    finish_potential(0)
    for copy in rims[0]:
        copy.start()
    got = pltpu.make_async_copy(recv.at[pl.ds(0, n_space - 1)], recv.at[pl.ds(0, n_space - 1)], block_recv)
    got.wait()
    lax.fori_loop(0, n_space, mark, 0)
    fetch(0)
    finish_potential(1)
    for copy in late + rims[1]:
        copy.start()
    spread(0)
    for copy in around[0]:
        copy.start()
    fetch(1)

    def send_ret(d, carry):
        to = lax.rem(me + d, n_space)
        remote(ret_send.at[to], ret_recv.at[me], ret_send_sem, ret_recv_sem, to, my_inj).start()
        return carry

    lax.fori_loop(1, n_space, send_ret, 0)
    ret_recv[me] = ret_send[me]

    spread(1)
    for copy in around[1]:
        copy.start()

    locals_[2].wait()
    for copy in late:
        copy.wait()
    for low_side in (True, False):
        beyond(sigma, (), low_side, H)
        for i in range(2):
            beyond(aa, (i,), low_side, H)
    faces([1, end - 1])
    for i in range(2):
        for copy in rims[i]:
            copy.wait()
        pb[i, H - 1, rows, :] = jnp.where(me == 0, 0.0, rim[0, i])
        pb[i, H + nx, rows, :] = jnp.where(me == n_space - 1, 0.0, rim[1, i])

    for copy in around[0]:
        copy.wait()
    sweep(0, asrc, aa, ab, range(1, planes - 1), w0)
    sweep(0, asrc, ab, aa, range(2, planes - 2), w1)
    sweep(0, asrc, aa, ab, range(3, planes - 3), w2)
    sweep(1, asrc, aa, ab, range(H, H + nx), w0)
    sweep(1, asrc, ab, aa, range(H + 1, end - H), w1)
    sweep(1, asrc, aa, ab, range(H + 2, end - H - 1), w2)

    def term(i, side):
        def work(low, at):
            part = ny // n_inj
            where = pl.ds(low // part, chunk // part)
            for x in range(half):
                p = H + side * half + x
                here, there = pb[i, p, at, :], ab[i, p, at, :]
                ahead, behind = pl.ds(low + PAD + 1, chunk), pl.ds(low + PAD - 1, chunk)
                pairs = [
                    (pb[i, p + 1, at, :], ab[i, p + 1, at, :]),
                    (pb[i, p - 1, at, :], ab[i, p - 1, at, :]),
                    (pb[i, p, ahead, :], ab[i, p, ahead, :]),
                    (pb[i, p, behind, :], ab[i, p, behind, :]),
                    (next_z(here), next_z(there)),
                    (last_z(here), last_z(there)),
                ]
                total = jnp.zeros((chunk, nz), F32)
                for u, v in pairs:
                    total = total + (here - u) * (there - v)
                total = (-0.5 * total).reshape(chunk // part, part, nz)
                partial[side, where, x] = total if i == 0 else partial[side, where, x] + total

        in_chunks(work)

    def send_share(side):
        def step(d, carry):
            to = lax.rem(my_inj + d, n_inj)
            remote(
                partial.at[side, to], shares.at[side, my_inj], share_send.at[side], share_recv.at[side], me, to
            ).start()
            return carry

        lax.fori_loop(1, n_inj, step, 0)
        shares[side, my_inj] = partial[side, my_inj]

    term(0, 0)
    term(0, 1)
    around[1][0].wait()
    sweep(1, asrc, aa, ab, [1, 2, 3], w0)
    sweep(1, asrc, ab, aa, [2, 3, 4], w1)
    sweep(1, asrc, aa, ab, [3, 4, 5], w2)
    term(1, 0)
    send_share(0)
    around[1][1].wait()
    sweep(1, asrc, aa, ab, [end - 3, end - 2, end - 1], w0)
    sweep(1, asrc, ab, aa, [end - 4, end - 3, end - 2], w1)
    sweep(1, asrc, aa, ab, [end - 5, end - 4, end - 3], w2)
    term(1, 1)
    send_share(1)

    ret_got = pltpu.make_async_copy(ret_recv.at[pl.ds(0, n_space - 1)], ret_recv.at[pl.ds(0, n_space - 1)], ret_recv_sem)
    ret_got.wait()
    lane_j = lax.rem(iota((1, lanes), 1), 2).astype(F32)
    back = jnp.where(iota((n_space * 4, lanes), 0).astype(F32) == slot_c * 2.0 + lane_j, 1.0, 0.0)
    back = jnp.transpose(back)[: 2 * blocks]
    returned = jnp.concatenate([ret_recv[t] for t in range(n_space)], axis=0)
    res_out[...] = jnp.dot(back, returned, precision=HIGHEST, preferred_element_type=F32)

    for side in range(2):
        window = shares.at[side, pl.ds(0, n_inj - 1)]
        pltpu.make_async_copy(window, window, share_recv.at[side]).wait()
        total = shares[side, 0]
        for k in range(1, n_inj):
            total = total + shares[side, k]
        grad_out[pl.ds(side * half, half)] = total

    pltpu.make_async_copy(send.at[pl.ds(0, n_space - 1)], send.at[pl.ds(0, n_space - 1)], block_send).wait()
    pltpu.make_async_copy(ret_send.at[pl.ds(0, n_space - 1)], ret_send.at[pl.ds(0, n_space - 1)], ret_send_sem).wait()
    for side in range(2):
        window = partial.at[side, pl.ds(0, n_inj - 1)]
        pltpu.make_async_copy(window, window, share_send.at[side]).wait()


def body(
    conductivity, start_potential, start_adjoint, inj_cells, dipole_cells, owner_tile, live_count, observed,
):
    n_space, n_inj = lax.axis_size("space"), lax.axis_size("inj")
    nx, ny, nz = conductivity.shape
    blocks, elec = observed.shape[1], observed.shape[3]
    planes, tall_rows = nx + 2 * H, ny + 2 * PAD
    wide, tall = 2 * nz, nx // 2 * ny
    hbm = pl.BlockSpec(memory_space=pltpu.HBM)
    vmem = pl.BlockSpec(memory_space=pltpu.VMEM)
    field = pltpu.VMEM((2, planes, tall_rows, nz), F32)
    dma = pltpu.SemaphoreType.DMA
    gradient, residual = pl.pallas_call(
        functools.partial(kernel, n_space, n_inj, nx, ny, nz, blocks),
        out_shape=(
            pltpu.VMEM((nx, ny // n_inj, nz), F32),
            pltpu.VMEM((2 * blocks, elec), F32),
        ),
        in_specs=[hbm] * 8,
        out_specs=(vmem, vmem),
        scratch_shapes=[
            pltpu.SMEM((2, 2), jnp.int32),
            pltpu.VMEM((1, blocks), jnp.int32),
            pltpu.VMEM((1, blocks), jnp.int32),
            pltpu.VMEM((2 * blocks, elec), jnp.int32),
            pltpu.VMEM((2 * blocks, elec), F32),
            pltpu.VMEM((planes, tall_rows, nz), F32),
            field, field, field, field,
            pltpu.VMEM((7, planes, ny, nz), F32),
            pltpu.VMEM((2, planes, ny, nz), F32),
            pltpu.VMEM((2, planes, ny, nz), F32),
            pltpu.VMEM((n_space, 8, elec), F32),
            pltpu.VMEM((n_space, 8, elec), F32),
            pltpu.VMEM((n_space, 4, elec), F32),
            pltpu.VMEM((n_space, 4, elec), F32),
            pltpu.VMEM((2, 2, ny, nz), F32),
            pltpu.VMEM((n_space, wide, 4 * elec), BF16),
            pltpu.VMEM((2, 2 * tall, wide), BF16),
            pltpu.VMEM((2 * tall, wide), F32),
            pltpu.VMEM((2, n_inj, nx // 2, ny // n_inj, nz), F32),
            pltpu.VMEM((2, n_inj, nx // 2, ny // n_inj, nz), F32),
            dma((8,)), dma((6,)), dma((6,)), dma((4,)), dma((4,)), dma, dma,
            dma, dma, dma((4,)), dma((4,)), dma((4,)), dma((4,)), dma((2,)), dma((2,)),
        ],
        compiler_params=pltpu.CompilerParams(
            collective_id=0, has_side_effects=True, vmem_limit_bytes=60 * 1024 * 1024
        ),
    )(
        conductivity, start_potential, start_adjoint, inj_cells,
        owner_tile.reshape(1, blocks), live_count,
        dipole_cells.reshape(2 * blocks, elec), observed.reshape(2 * blocks, elec),
    )
    return gradient, residual.reshape(1, blocks, 2, elec)


def solution(mesh):
    return jax.shard_map(
        body,
        mesh=mesh,
        in_specs=(
            P("space", None, None),
            P("inj", "space", None, None),
            P("inj", "space", None, None),
            P("inj", None),
            P("inj", "space", None, None),
            P("inj", "space", None),
            P("inj", "space"),
            P("inj", "space", None, None),
        ),
        out_specs=(P("space", "inj", None), P("inj", "space", None, None)),
        check_vma=False,
    )
```

```python
import functools
import math

import jax
import jax.numpy as jnp
from jax import lax
from jax.experimental import pallas as pl
from jax.experimental.pallas import tpu as pltpu
from jax.sharding import PartitionSpec as P

MESH = pl.DeviceIdType.MESH
F32 = jnp.float32
BF16 = jnp.bfloat16
HIGHEST = lax.Precision.HIGHEST

current_amp = 4.0
sweep_weights = [
    1.0 / (1.0 + 0.9 * math.cos((2 * step_k + 1) * math.pi / 6.0)) for step_k in range(3)
]

H = 4
PAD = 8


def iota(shape, dim):
    return lax.broadcasted_iota(jnp.int32, shape, dim)


def rows_sum(values):
    return jnp.sum(values, axis=0, keepdims=True)


def kernel(
    n_space, n_inj, nx, ny, nz, blocks,
    sig_in, pot_in, adj_in, inj_in, owner_in, live_in, cells_in, observed_in,
    grad_out, res_out,
    inj_cells, owner, live, cells, observed, sigma, pa, pb, aa, ab, coef, src, asrc, send, recv, ret_send, ret_recv,
    rim, onehot, table, scat, partial, shares,
    local_sem, halo_send, halo_recv, far_send, far_recv, block_send, block_recv,
    ret_send_sem, ret_recv_sem, rim_send, rim_recv, asrc_send, asrc_recv, share_send, share_recv,
):
    me = lax.axis_index("space")
    my_inj = lax.axis_index("inj")
    left = lax.rem(me + n_space - 1, n_space)
    right = lax.rem(me + 1, n_space)
    planes = nx + 2 * H
    rows = pl.ds(PAD, ny)
    half = nx // 2
    tall = half * ny
    wide = 2 * nz
    half_cells = float(half * ny * nz)
    group = math.gcd(n_space, 16)

    barrier = pltpu.get_barrier_semaphore()

    def greet(to):
        pl.semaphore_signal(barrier, inc=1, device_id=to, device_id_type=MESH)

    def greet_space(d, carry):
        greet((lax.rem(me + d, n_space), my_inj))
        return carry

    def greet_inj(d, carry):
        greet((me, lax.rem(my_inj + d, n_inj)))
        return carry

    greet((left, my_inj))
    greet((right, my_inj))
    lax.fori_loop(2, n_space - 1, greet_space, 0)
    lax.fori_loop(1, n_inj, greet_inj, 0)

    small = [
        pltpu.make_async_copy(source, target, local_sem.at[3 + k])
        for k, (source, target) in enumerate(
            ((inj_in, inj_cells), (owner_in, owner), (live_in, live), (cells_in, cells), (observed_in, observed))
        )
    ]
    locals_ = [
        pltpu.make_async_copy(sig_in, sigma.at[pl.ds(H, nx), rows], local_sem.at[0]),
        pltpu.make_async_copy(pot_in, pa.at[:, pl.ds(H, nx), rows], local_sem.at[1]),
        pltpu.make_async_copy(adj_in, aa.at[:, pl.ds(H, nx), rows], local_sem.at[2]),
    ]
    for copy in small + locals_:
        copy.start()

    for low in (0, PAD + ny):
        sigma[:, pl.ds(low, PAD), :] = jnp.zeros((planes, PAD, nz), F32)
        for buf in (pa, pb, aa, ab):
            buf[:, :, pl.ds(low, PAD), :] = jnp.zeros((2, planes, PAD, nz), F32)

    for copy in small:
        copy.wait()
    lanes = 4 * blocks
    lane_c = iota((blocks, lanes), 1)
    block_c = lax.rem(lane_c, 2 * blocks) // 2
    field_c = lax.rem(lane_c, 2) + 2 * (lane_c // (2 * blocks))
    row_b = iota((blocks, lanes), 0)
    owners = jnp.broadcast_to(owner[...].astype(F32), (blocks, blocks))
    owners = jnp.where(iota((blocks, blocks), 0) == iota((blocks, blocks), 1), owners, 0.0)
    owners = jnp.broadcast_to(jnp.sum(owners, axis=1, keepdims=True), (blocks, lanes))
    owner_c = rows_sum(jnp.where(row_b == block_c, owners, 0.0))
    earlier = (owners == owner_c) & (row_b < block_c)
    rank_c = rows_sum(jnp.where(earlier, 1.0, 0.0))
    slot_c = owner_c * 2.0 + rank_c
    target = slot_c * 4.0 + field_c[:1].astype(F32)
    place = jnp.where(iota((n_space * 8, lanes), 0).astype(F32) == target, 1.0, 0.0)

    row_r = iota((lanes, blocks), 0)
    block_r = lax.rem(row_r, 2 * blocks) // 2
    lives = jnp.broadcast_to(live[...].astype(F32), (lanes, blocks))
    live_r = jnp.sum(jnp.where(block_r == iota((lanes, blocks), 1), lives, 0.0), axis=1, keepdims=True)
    data = jnp.concatenate([cells[...].astype(F32) + 1.0, observed[...]], axis=0)
    elec = data.shape[1]
    data = jnp.where(iota((lanes, elec), 1).astype(F32) < live_r, data, 0.0)
    packed = jnp.dot(place, data, precision=HIGHEST, preferred_element_type=F32)
    for t in range(n_space):
        send[t] = packed[8 * t : 8 * t + 8]

    pl.semaphore_wait(barrier, n_space - 1 + n_inj - 1)

    def remote(source, target, send_sem, recv_sem, space, inj):
        return pltpu.make_async_remote_copy(
            src_ref=source, dst_ref=target, send_sem=send_sem, recv_sem=recv_sem,
            device_id=(space, inj), device_id_type=MESH,
        )

    def pair(source, target, lead, width, send_sems, recv_sems, k):
        return [
            remote(
                source.at[lead + (pl.ds(nx - width, width),)], target.at[lead + (pl.ds(H - width, width), rows)],
                send_sems.at[k], recv_sems.at[k], right, my_inj,
            ),
            remote(
                source.at[lead + (pl.ds(0, width),)], target.at[lead + (pl.ds(nx + H, width), rows)],
                send_sems.at[k + 1], recv_sems.at[k + 1], left, my_inj,
            ),
        ]

    early = pair(sig_in, sigma, (), 3, halo_send, halo_recv, 0)
    near = [pair(pot_in, pa, (i,), 3, halo_send, halo_recv, 2 + 2 * i) for i in range(2)]
    late = [
        remote(sig_in.at[pl.ds(nx - H, 1)], sigma.at[pl.ds(0, 1), rows], far_send.at[0], far_recv.at[0], right, my_inj),
        remote(sig_in.at[pl.ds(H - 1, 1)], sigma.at[pl.ds(planes - 1, 1), rows], far_send.at[1], far_recv.at[1], left, my_inj),
    ] + pair(adj_in, aa, (slice(None),), H, far_send, far_recv, 2)
    for copy in early + near[0]:
        copy.start()

    def send_block(d, carry):
        to = lax.rem(me + d, n_space)
        remote(send.at[to], recv.at[me], block_send, block_recv, to, my_inj).start()
        return carry

    lax.fori_loop(1, n_space, send_block, 0)
    recv[me] = send[me]

    cell_ids = iota((ny, nz), 0) * nz + iota((ny, nz), 1)

    for p in range(2, planes - 2):
        first = (me * nx - H + p) * (ny * nz)
        for i in range(2):
            plus = jnp.where(cell_ids == inj_cells[i, 0] - first, current_amp, 0.0)
            minus = jnp.where(cell_ids == inj_cells[i, 1] - first, current_amp, 0.0)
            src[i, p] = plus - minus

    def beyond(buf, lead, low_side, width):
        nothing = jnp.zeros((width, ny, nz), F32)

        @pl.when(me == (0 if low_side else n_space - 1))
        def _():
            buf[lead + (pl.ds(H - width if low_side else nx + H, width), rows)] = nothing

    chunk = ny

    def in_chunks(work):
        work(0, pl.ds(PAD, ny))

    first_lane = iota((chunk, nz), 1) == 0
    last_lane = iota((chunk, nz), 1) == nz - 1

    def next_z(value):
        return jnp.where(last_lane, 0.0, pltpu.roll(value, nz - 1, 1))

    def last_z(value):
        return jnp.where(first_lane, 0.0, pltpu.roll(value, 1, 1))

    def faces(which):
        def work(low, at):
            for p in which:
                here = sigma[p, at, :]
                around = [
                    sigma[p + 1, at, :], sigma[p - 1, at, :],
                    sigma[p, pl.ds(low + PAD + 1, chunk), :], sigma[p, pl.ds(low + PAD - 1, chunk), :],
                    next_z(here), last_z(here),
                ]
                around = [0.5 * (here + value) for value in around]
                diag = around[0] + around[1] + around[2] + around[3] + around[4] + around[5]
                plane = me * nx - H + p
                inside = jnp.where((plane >= 0) & (plane < n_space * nx), 1.0, 0.0)
                inverse = inside / jnp.where(diag > 0.0, diag, 1.0)
                around[4] = jnp.where(last_lane, 0.0, around[4])
                around[5] = jnp.where(first_lane, 0.0, around[5])
                for k in range(6):
                    coef[k, p, pl.ds(low, chunk), :] = around[k] * inverse
                coef[6, p, pl.ds(low, chunk), :] = inverse

        in_chunks(work)

    def sweep(i, source, old, new, which, weight):
        def work(low, at):
            for p in which:
                c = [coef[k, p, pl.ds(low, chunk), :] for k in range(7)]
                here = old[i, p, at, :]
                beside = c[0] * old[i, p + 1, at, :] + c[1] * old[i, p - 1, at, :]
                beside = beside + (
                    c[2] * old[i, p, pl.ds(low + PAD + 1, chunk), :] + c[3] * old[i, p, pl.ds(low + PAD - 1, chunk), :]
                )
                beside = beside + (c[4] * pltpu.roll(here, nz - 1, 1) + c[5] * pltpu.roll(here, 1, 1))
                beside = beside + c[6] * source[i, p, pl.ds(low, chunk), :]
                new[i, p, at, :] = here + weight * (beside - here)

        in_chunks(work)

    w0, w1, w2 = sweep_weights
    end = planes - 1

    locals_[0].wait()
    faces(range(H + 1, end - H))
    locals_[1].wait()
    for i in range(2):
        sweep(i, src, pa, pb, range(H + 1, end - H), w0)
        sweep(i, src, pb, pa, range(H + 2, end - H - 1), w1)

    for copy in early:
        copy.wait()
    beyond(sigma, (), True, 3)
    beyond(sigma, (), False, 3)
    faces([2, 3, 4, end - 4, end - 3, end - 2])

    def finish_potential(i):
        for copy in near[i]:
            copy.wait()
        if i == 0:
            for copy in near[1]:
                copy.start()
        beyond(pa, (i,), True, 3)
        beyond(pa, (i,), False, 3)
        sweep(i, src, pa, pb, [2, 3, 4, end - 4, end - 3, end - 2], w0)
        sweep(i, src, pb, pa, [3, 4, 5, end - 5, end - 4, end - 3], w1)
        sweep(i, src, pa, pb, range(H, H + nx), w2)
        for x in range(nx):
            value = pb[i, H + x, rows, :]
            high = value.astype(BF16)
            low = (value - high.astype(F32)).astype(BF16)
            first, columns = (x % half) * ny, pl.ds((x // half) * nz, nz)
            table[i, pl.ds(first, ny), columns] = high
            table[i, pl.ds(tall + first, ny), columns] = low

    wide_iota = iota((wide, elec), 0).astype(F32).astype(BF16)
    tall_iota = iota((tall, elec), 0).astype(F32)
    tall_iota16 = tall_iota.astype(BF16)
    one = jnp.ones((wide, elec), BF16)
    none = jnp.zeros((wide, elec), BF16)

    def split_cells(t):
        cell = recv[t] - 1.0
        upper = cell >= half_cells
        within = jnp.where(upper, cell - half_cells, cell)
        tall_at = jnp.floor(within * (1.0 / nz))
        wide_at = within - tall_at * nz + jnp.where(upper, float(nz), 0.0)
        return tall_at, jnp.where(cell < 0.0, -1.0, wide_at)

    def mark(t, carry):
        _, wide_at = split_cells(t)
        for s in range(2):
            for f in range(2):
                row = jnp.broadcast_to(wide_at[4 * s + f : 4 * s + f + 1], (wide, elec)).astype(BF16)
                onehot[t, :, pl.ds((2 * s + f) * elec, elec)] = jnp.where(wide_iota == row, one, none)
        return carry

    def fetch(i):
        def step(u, carry):
            for k in range(group):
                t = u * group + k
                tall_at, _ = split_cells(t)
                found = jnp.dot(table[i], onehot[t], preferred_element_type=F32)
                for s in range(2):
                    ends = []
                    for f in range(2):
                        here = tall_iota == tall_at[4 * s + f : 4 * s + f + 1]
                        at = slice((2 * s + f) * elec, (2 * s + f + 1) * elec)
                        ends.append(rows_sum(jnp.where(here, found[:tall, at] + found[tall:, at], 0.0)))
                    ret_send[t, pl.ds(2 * s + i, 1), :] = ends[0] - ends[1] - recv[t, pl.ds(4 * s + 2 + i, 1), :]
            return carry

        lax.fori_loop(0, n_space // group, step, 0)

    def spread(i):
        scat[...] = jnp.zeros_like(scat)

        def step(u, carry):
            amounts, hots = [], []
            for k in range(group):
                t = u * group + k
                tall_at, _ = split_cells(t)
                misfit = ret_send[t]
                high = misfit.astype(BF16).astype(F32)
                for s in range(2):
                    for f in range(2):
                        sign = 1.0 if f == 0 else -1.0
                        row = jnp.broadcast_to(tall_at[4 * s + f : 4 * s + f + 1], (tall, elec)).astype(BF16)
                        here = tall_iota16 == row
                        pieces = []
                        for value in (high, misfit - high):
                            amount = jnp.broadcast_to(sign * value[2 * s + i : 2 * s + i + 1], (tall, elec)).astype(BF16)
                            pieces.append(jnp.where(here, amount, jnp.zeros((tall, elec), BF16)))
                        amounts.append(jnp.concatenate(pieces, axis=0))
                hots.append(onehot[t])
            scat[...] += lax.dot_general(
                jnp.concatenate(amounts, axis=1), jnp.concatenate(hots, axis=1), (((1,), (1,)), ((), ())),
                preferred_element_type=F32,
            )
            return carry

        lax.fori_loop(0, n_space // group, step, 0)
        for x in range(nx):
            first, columns = (x % half) * ny, pl.ds((x // half) * nz, nz)
            asrc[i, H + x] = scat[pl.ds(first, ny), columns] + scat[pl.ds(tall + first, ny), columns]

    rims = [
        [
            remote(pb.at[i, H + nx - 1, rows], rim.at[0, i], rim_send.at[2 * i], rim_recv.at[2 * i], right, my_inj),
            remote(pb.at[i, H, rows], rim.at[1, i], rim_send.at[2 * i + 1], rim_recv.at[2 * i + 1], left, my_inj),
        ]
        for i in range(2)
    ]
    around = [
        [
            remote(
                asrc.at[i, pl.ds(H + nx - 3, 3)], asrc.at[i, pl.ds(1, 3)],
                asrc_send.at[2 * i], asrc_recv.at[2 * i], right, my_inj,
            ),
            remote(
                asrc.at[i, pl.ds(H, 3)], asrc.at[i, pl.ds(H + nx, 3)],
                asrc_send.at[2 * i + 1], asrc_recv.at[2 * i + 1], left, my_inj,
            ),
        ]
        for i in range(2)
    ]

    finish_potential(0)
    for copy in rims[0]:
        copy.start()
    got = pltpu.make_async_copy(recv.at[pl.ds(0, n_space - 1)], recv.at[pl.ds(0, n_space - 1)], block_recv)
    got.wait()
    lax.fori_loop(0, n_space, mark, 0)
    fetch(0)
    finish_potential(1)
    for copy in late + rims[1]:
        copy.start()
    spread(0)
    for copy in around[0]:
        copy.start()
    fetch(1)

    def send_ret(d, carry):
        to = lax.rem(me + d, n_space)
        remote(ret_send.at[to], ret_recv.at[me], ret_send_sem, ret_recv_sem, to, my_inj).start()
        return carry

    lax.fori_loop(1, n_space, send_ret, 0)
    ret_recv[me] = ret_send[me]

    spread(1)
    for copy in around[1]:
        copy.start()

    locals_[2].wait()
    for copy in late:
        copy.wait()
    for low_side in (True, False):
        beyond(sigma, (), low_side, H)
        for i in range(2):
            beyond(aa, (i,), low_side, H)
    faces([1, end - 1])
    for i in range(2):
        for copy in rims[i]:
            copy.wait()
        pb[i, H - 1, rows, :] = jnp.where(me == 0, 0.0, rim[0, i])
        pb[i, H + nx, rows, :] = jnp.where(me == n_space - 1, 0.0, rim[1, i])

    for copy in around[0]:
        copy.wait()
    sweep(0, asrc, aa, ab, range(1, planes - 1), w0)
    sweep(0, asrc, ab, aa, range(2, planes - 2), w1)
    sweep(0, asrc, aa, ab, range(3, planes - 3), w2)
    sweep(1, asrc, aa, ab, range(H, H + nx), w0)
    sweep(1, asrc, ab, aa, range(H + 1, end - H), w1)
    sweep(1, asrc, aa, ab, range(H + 2, end - H - 1), w2)

    def term(i, side):
        def work(low, at):
            part = ny // n_inj
            where = pl.ds(low // part, chunk // part)
            for x in range(half):
                p = H + side * half + x
                here, there = pb[i, p, at, :], ab[i, p, at, :]
                ahead, behind = pl.ds(low + PAD + 1, chunk), pl.ds(low + PAD - 1, chunk)
                pairs = [
                    (pb[i, p + 1, at, :], ab[i, p + 1, at, :]),
                    (pb[i, p - 1, at, :], ab[i, p - 1, at, :]),
                    (pb[i, p, ahead, :], ab[i, p, ahead, :]),
                    (pb[i, p, behind, :], ab[i, p, behind, :]),
                    (next_z(here), next_z(there)),
                    (last_z(here), last_z(there)),
                ]
                total = jnp.zeros((chunk, nz), F32)
                for u, v in pairs:
                    total = total + (here - u) * (there - v)
                total = (-0.5 * total).reshape(chunk // part, part, nz)
                partial[side, where, x] = total if i == 0 else partial[side, where, x] + total

        in_chunks(work)

    def send_share(side):
        def step(d, carry):
            to = lax.rem(my_inj + d, n_inj)
            remote(
                partial.at[side, to], shares.at[side, my_inj], share_send.at[side], share_recv.at[side], me, to
            ).start()
            return carry

        lax.fori_loop(1, n_inj, step, 0)
        shares[side, my_inj] = partial[side, my_inj]

    term(0, 0)
    term(0, 1)
    around[1][0].wait()
    sweep(1, asrc, aa, ab, [1, 2, 3], w0)
    sweep(1, asrc, ab, aa, [2, 3, 4], w1)
    sweep(1, asrc, aa, ab, [3, 4, 5], w2)
    term(1, 0)
    send_share(0)
    around[1][1].wait()
    sweep(1, asrc, aa, ab, [end - 3, end - 2, end - 1], w0)
    sweep(1, asrc, ab, aa, [end - 4, end - 3, end - 2], w1)
    sweep(1, asrc, aa, ab, [end - 5, end - 4, end - 3], w2)
    term(1, 1)
    send_share(1)

    ret_got = pltpu.make_async_copy(ret_recv.at[pl.ds(0, n_space - 1)], ret_recv.at[pl.ds(0, n_space - 1)], ret_recv_sem)
    ret_got.wait()
    lane_j = lax.rem(iota((1, lanes), 1), 2).astype(F32)
    back = jnp.where(iota((n_space * 4, lanes), 0).astype(F32) == slot_c * 2.0 + lane_j, 1.0, 0.0)
    back = jnp.transpose(back)[: 2 * blocks]
    returned = jnp.concatenate([ret_recv[t] for t in range(n_space)], axis=0)
    res_out[...] = jnp.dot(back, returned, precision=HIGHEST, preferred_element_type=F32)

    for side in range(2):
        window = shares.at[side, pl.ds(0, n_inj - 1)]
        pltpu.make_async_copy(window, window, share_recv.at[side]).wait()
        total = shares[side, 0]
        for k in range(1, n_inj):
            total = total + shares[side, k]
        grad_out[pl.ds(side * half, half)] = total

    pltpu.make_async_copy(send.at[pl.ds(0, n_space - 1)], send.at[pl.ds(0, n_space - 1)], block_send).wait()
    pltpu.make_async_copy(ret_send.at[pl.ds(0, n_space - 1)], ret_send.at[pl.ds(0, n_space - 1)], ret_send_sem).wait()
    for side in range(2):
        window = partial.at[side, pl.ds(0, n_inj - 1)]
        pltpu.make_async_copy(window, window, share_send.at[side]).wait()


def body(
    conductivity, start_potential, start_adjoint, inj_cells, dipole_cells, owner_tile, live_count, observed,
):
    n_space, n_inj = lax.axis_size("space"), lax.axis_size("inj")
    nx, ny, nz = conductivity.shape
    blocks, elec = observed.shape[1], observed.shape[3]
    planes, tall_rows = nx + 2 * H, ny + 2 * PAD
    wide, tall = 2 * nz, nx // 2 * ny
    hbm = pl.BlockSpec(memory_space=pltpu.HBM)
    vmem = pl.BlockSpec(memory_space=pltpu.VMEM)
    field = pltpu.VMEM((2, planes, tall_rows, nz), F32)
    dma = pltpu.SemaphoreType.DMA
    gradient, residual = pl.pallas_call(
        functools.partial(kernel, n_space, n_inj, nx, ny, nz, blocks),
        out_shape=(
            pltpu.VMEM((nx, ny // n_inj, nz), F32),
            pltpu.VMEM((2 * blocks, elec), F32),
        ),
        in_specs=[hbm] * 8,
        out_specs=(vmem, vmem),
        scratch_shapes=[
            pltpu.SMEM((2, 2), jnp.int32),
            pltpu.VMEM((1, blocks), jnp.int32),
            pltpu.VMEM((1, blocks), jnp.int32),
            pltpu.VMEM((2 * blocks, elec), jnp.int32),
            pltpu.VMEM((2 * blocks, elec), F32),
            pltpu.VMEM((planes, tall_rows, nz), F32),
            field, field, field, field,
            pltpu.VMEM((7, planes, ny, nz), F32),
            pltpu.VMEM((2, planes, ny, nz), F32),
            pltpu.VMEM((2, planes, ny, nz), F32),
            pltpu.VMEM((n_space, 8, elec), F32),
            pltpu.VMEM((n_space, 8, elec), F32),
            pltpu.VMEM((n_space, 4, elec), F32),
            pltpu.VMEM((n_space, 4, elec), F32),
            pltpu.VMEM((2, 2, ny, nz), F32),
            pltpu.VMEM((n_space, wide, 4 * elec), BF16),
            pltpu.VMEM((2, 2 * tall, wide), BF16),
            pltpu.VMEM((2 * tall, wide), F32),
            pltpu.VMEM((2, n_inj, nx // 2, ny // n_inj, nz), F32),
            pltpu.VMEM((2, n_inj, nx // 2, ny // n_inj, nz), F32),
            dma((8,)), dma((6,)), dma((6,)), dma((4,)), dma((4,)), dma, dma,
            dma, dma, dma((4,)), dma((4,)), dma((4,)), dma((4,)), dma((2,)), dma((2,)),
        ],
        compiler_params=pltpu.CompilerParams(
            collective_id=0, has_side_effects=True, vmem_limit_bytes=60 * 1024 * 1024
        ),
    )(
        conductivity, start_potential, start_adjoint, inj_cells,
        owner_tile.reshape(1, blocks), live_count,
        dipole_cells.reshape(2 * blocks, elec), observed.reshape(2 * blocks, elec),
    )
    return gradient, residual.reshape(1, blocks, 2, elec)


def solution(mesh):
    return jax.shard_map(
        body,
        mesh=mesh,
        in_specs=(
            P("space", None, None),
            P("inj", "space", None, None),
            P("inj", "space", None, None),
            P("inj", None),
            P("inj", "space", None, None),
            P("inj", "space", None),
            P("inj", "space"),
            P("inj", "space", None, None),
        ),
        out_specs=(P("space", "inj", None), P("inj", "space", None, None)),
        check_vma=False,
    )
```

```python
import functools
import math

import jax
import jax.numpy as jnp
from jax import lax
from jax.experimental import pallas as pl
from jax.experimental.pallas import tpu as pltpu
from jax.sharding import PartitionSpec as P

MESH = pl.DeviceIdType.MESH
F32 = jnp.float32
BF16 = jnp.bfloat16
HIGHEST = lax.Precision.HIGHEST

current_amp = 4.0
sweep_weights = [
    1.0 / (1.0 + 0.9 * math.cos((2 * step_k + 1) * math.pi / 6.0)) for step_k in range(3)
]

H = 4
PAD = 8


def iota(shape, dim):
    return lax.broadcasted_iota(jnp.int32, shape, dim)


def rows_sum(values):
    return jnp.sum(values, axis=0, keepdims=True)


def kernel(
    n_space, n_inj, nx, ny, nz, blocks,
    sig_in, pot_in, adj_in, inj_in, owner_in, live_in, cells_in, observed_in,
    grad_out, res_out,
    inj_cells, owner, live, cells, observed, sigma, pa, pb, aa, ab, coef, src, asrc, send, recv, ret_send, ret_recv,
    rim, onehot, table, scat, partial, shares,
    local_sem, halo_send, halo_recv, far_send, far_recv, block_send, block_recv,
    ret_send_sem, ret_recv_sem, rim_send, rim_recv, asrc_send, asrc_recv, share_send, share_recv,
):
    me = lax.axis_index("space")
    my_inj = lax.axis_index("inj")
    left = lax.rem(me + n_space - 1, n_space)
    right = lax.rem(me + 1, n_space)
    planes = nx + 2 * H
    rows = pl.ds(PAD, ny)
    half = nx // 2
    tall = half * ny
    wide = 2 * nz
    half_cells = float(half * ny * nz)
    group = math.gcd(n_space, 16)

    barrier = pltpu.get_barrier_semaphore()

    def greet(to):
        pl.semaphore_signal(barrier, inc=1, device_id=to, device_id_type=MESH)

    def greet_space(d, carry):
        greet((lax.rem(me + d, n_space), my_inj))
        return carry

    def greet_inj(d, carry):
        greet((me, lax.rem(my_inj + d, n_inj)))
        return carry

    greet((left, my_inj))
    greet((right, my_inj))
    lax.fori_loop(2, n_space - 1, greet_space, 0)
    lax.fori_loop(1, n_inj, greet_inj, 0)

    small = [
        pltpu.make_async_copy(source, target, local_sem.at[3 + k])
        for k, (source, target) in enumerate(
            ((inj_in, inj_cells), (owner_in, owner), (live_in, live), (cells_in, cells), (observed_in, observed))
        )
    ]
    locals_ = [
        pltpu.make_async_copy(sig_in, sigma.at[pl.ds(H, nx), rows], local_sem.at[0]),
        pltpu.make_async_copy(pot_in, pa.at[:, pl.ds(H, nx), rows], local_sem.at[1]),
        pltpu.make_async_copy(adj_in, aa.at[:, pl.ds(H, nx), rows], local_sem.at[2]),
    ]
    for copy in small + locals_:
        copy.start()

    for low in (0, PAD + ny):
        sigma[:, pl.ds(low, PAD), :] = jnp.zeros((planes, PAD, nz), F32)
        for buf in (pa, pb, aa, ab):
            buf[:, :, pl.ds(low, PAD), :] = jnp.zeros((2, planes, PAD, nz), F32)

    for copy in small:
        copy.wait()
    lanes = 4 * blocks
    lane_c = iota((blocks, lanes), 1)
    block_c = lax.rem(lane_c, 2 * blocks) // 2
    field_c = lax.rem(lane_c, 2) + 2 * (lane_c // (2 * blocks))
    row_b = iota((blocks, lanes), 0)
    owners = jnp.broadcast_to(owner[...].astype(F32), (blocks, blocks))
    owners = jnp.where(iota((blocks, blocks), 0) == iota((blocks, blocks), 1), owners, 0.0)
    owners = jnp.broadcast_to(jnp.sum(owners, axis=1, keepdims=True), (blocks, lanes))
    owner_c = rows_sum(jnp.where(row_b == block_c, owners, 0.0))
    earlier = (owners == owner_c) & (row_b < block_c)
    rank_c = rows_sum(jnp.where(earlier, 1.0, 0.0))
    slot_c = owner_c * 2.0 + rank_c
    target = slot_c * 4.0 + field_c[:1].astype(F32)
    place = jnp.where(iota((n_space * 8, lanes), 0).astype(F32) == target, 1.0, 0.0)

    row_r = iota((lanes, blocks), 0)
    block_r = lax.rem(row_r, 2 * blocks) // 2
    lives = jnp.broadcast_to(live[...].astype(F32), (lanes, blocks))
    live_r = jnp.sum(jnp.where(block_r == iota((lanes, blocks), 1), lives, 0.0), axis=1, keepdims=True)
    data = jnp.concatenate([cells[...].astype(F32) + 1.0, observed[...]], axis=0)
    elec = data.shape[1]
    data = jnp.where(iota((lanes, elec), 1).astype(F32) < live_r, data, 0.0)
    packed = jnp.dot(place, data, precision=HIGHEST, preferred_element_type=F32)
    for t in range(n_space):
        send[t] = packed[8 * t : 8 * t + 8]

    pl.semaphore_wait(barrier, n_space - 1 + n_inj - 1)

    def remote(source, target, send_sem, recv_sem, space, inj):
        return pltpu.make_async_remote_copy(
            src_ref=source, dst_ref=target, send_sem=send_sem, recv_sem=recv_sem,
            device_id=(space, inj), device_id_type=MESH,
        )

    def pair(source, target, lead, width, send_sems, recv_sems, k):
        return [
            remote(
                source.at[lead + (pl.ds(nx - width, width),)], target.at[lead + (pl.ds(H - width, width), rows)],
                send_sems.at[k], recv_sems.at[k], right, my_inj,
            ),
            remote(
                source.at[lead + (pl.ds(0, width),)], target.at[lead + (pl.ds(nx + H, width), rows)],
                send_sems.at[k + 1], recv_sems.at[k + 1], left, my_inj,
            ),
        ]

    early = pair(sig_in, sigma, (), 3, halo_send, halo_recv, 0)
    near = [pair(pot_in, pa, (i,), 3, halo_send, halo_recv, 2 + 2 * i) for i in range(2)]
    late = [
        remote(sig_in.at[pl.ds(nx - H, 1)], sigma.at[pl.ds(0, 1), rows], far_send.at[0], far_recv.at[0], right, my_inj),
        remote(sig_in.at[pl.ds(H - 1, 1)], sigma.at[pl.ds(planes - 1, 1), rows], far_send.at[1], far_recv.at[1], left, my_inj),
    ] + pair(adj_in, aa, (slice(None),), H, far_send, far_recv, 2)
    for copy in early:
        copy.start()

    def send_block(d, carry):
        to = lax.rem(me + d, n_space)
        remote(send.at[to], recv.at[me], block_send, block_recv, to, my_inj).start()
        return carry

    lax.fori_loop(1, n_space, send_block, 0)
    for copy in near[0]:
        copy.start()
    recv[me] = send[me]

    cell_ids = iota((ny, nz), 0) * nz + iota((ny, nz), 1)

    for p in range(2, planes - 2):
        first = (me * nx - H + p) * (ny * nz)
        for i in range(2):
            plus = jnp.where(cell_ids == inj_cells[i, 0] - first, current_amp, 0.0)
            minus = jnp.where(cell_ids == inj_cells[i, 1] - first, current_amp, 0.0)
            src[i, p] = plus - minus

    def beyond(buf, lead, low_side, width):
        nothing = jnp.zeros((width, ny, nz), F32)

        @pl.when(me == (0 if low_side else n_space - 1))
        def _():
            buf[lead + (pl.ds(H - width if low_side else nx + H, width), rows)] = nothing

    chunk = ny

    def in_chunks(work):
        work(0, pl.ds(PAD, ny))

    first_lane = iota((chunk, nz), 1) == 0
    last_lane = iota((chunk, nz), 1) == nz - 1

    def next_z(value):
        return jnp.where(last_lane, 0.0, pltpu.roll(value, nz - 1, 1))

    def last_z(value):
        return jnp.where(first_lane, 0.0, pltpu.roll(value, 1, 1))

    def faces(which):
        def work(low, at):
            for p in which:
                here = sigma[p, at, :]
                around = [
                    sigma[p + 1, at, :], sigma[p - 1, at, :],
                    sigma[p, pl.ds(low + PAD + 1, chunk), :], sigma[p, pl.ds(low + PAD - 1, chunk), :],
                    next_z(here), last_z(here),
                ]
                around = [0.5 * (here + value) for value in around]
                diag = around[0] + around[1] + around[2] + around[3] + around[4] + around[5]
                plane = me * nx - H + p
                inside = jnp.where((plane >= 0) & (plane < n_space * nx), 1.0, 0.0)
                inverse = inside / jnp.where(diag > 0.0, diag, 1.0)
                around[4] = jnp.where(last_lane, 0.0, around[4])
                around[5] = jnp.where(first_lane, 0.0, around[5])
                for k in range(6):
                    coef[k, p, pl.ds(low, chunk), :] = around[k] * inverse
                coef[6, p, pl.ds(low, chunk), :] = inverse

        in_chunks(work)

    def sweep(i, source, old, new, which, weight):
        def work(low, at):
            for p in which:
                c = [coef[k, p, pl.ds(low, chunk), :] for k in range(7)]
                here = old[i, p, at, :]
                beside = c[0] * old[i, p + 1, at, :] + c[1] * old[i, p - 1, at, :]
                beside = beside + (
                    c[2] * old[i, p, pl.ds(low + PAD + 1, chunk), :] + c[3] * old[i, p, pl.ds(low + PAD - 1, chunk), :]
                )
                beside = beside + (c[4] * pltpu.roll(here, nz - 1, 1) + c[5] * pltpu.roll(here, 1, 1))
                beside = beside + c[6] * source[i, p, pl.ds(low, chunk), :]
                new[i, p, at, :] = here + weight * (beside - here)

        in_chunks(work)

    w0, w1, w2 = sweep_weights
    end = planes - 1

    locals_[0].wait()
    faces(range(H + 1, end - H))
    locals_[1].wait()
    for i in range(2):
        sweep(i, src, pa, pb, range(H + 1, end - H), w0)
        sweep(i, src, pb, pa, range(H + 2, end - H - 1), w1)

    for copy in early:
        copy.wait()
    beyond(sigma, (), True, 3)
    beyond(sigma, (), False, 3)
    faces([2, 3, 4, end - 4, end - 3, end - 2])

    def finish_potential(i):
        for copy in near[i]:
            copy.wait()
        if i == 0:
            for copy in near[1]:
                copy.start()
        beyond(pa, (i,), True, 3)
        beyond(pa, (i,), False, 3)
        sweep(i, src, pa, pb, [2, 3, 4, end - 4, end - 3, end - 2], w0)
        sweep(i, src, pb, pa, [3, 4, 5, end - 5, end - 4, end - 3], w1)
        sweep(i, src, pa, pb, range(H, H + nx), w2)
        for x in range(nx):
            value = pb[i, H + x, rows, :]
            high = value.astype(BF16)
            low = (value - high.astype(F32)).astype(BF16)
            first, columns = (x % half) * ny, pl.ds((x // half) * nz, nz)
            table[i, pl.ds(first, ny), columns] = high
            table[i, pl.ds(tall + first, ny), columns] = low

    wide_iota = iota((wide, elec), 0).astype(F32).astype(BF16)
    tall_iota = iota((tall, elec), 0).astype(F32)
    tall_iota16 = tall_iota.astype(BF16)
    one = jnp.ones((wide, elec), BF16)
    none = jnp.zeros((wide, elec), BF16)

    def split_cells(t):
        cell = recv[t] - 1.0
        upper = cell >= half_cells
        within = jnp.where(upper, cell - half_cells, cell)
        tall_at = jnp.floor(within * (1.0 / nz))
        wide_at = within - tall_at * nz + jnp.where(upper, float(nz), 0.0)
        return tall_at, jnp.where(cell < 0.0, -1.0, wide_at)

    def mark(t, carry):
        _, wide_at = split_cells(t)
        for s in range(2):
            for f in range(2):
                row = jnp.broadcast_to(wide_at[4 * s + f : 4 * s + f + 1], (wide, elec)).astype(BF16)
                onehot[t, :, pl.ds((2 * s + f) * elec, elec)] = jnp.where(wide_iota == row, one, none)
        return carry

    def fetch(i):
        def step(u, carry):
            for k in range(group):
                t = u * group + k
                tall_at, _ = split_cells(t)
                found = jnp.dot(table[i], onehot[t], preferred_element_type=F32)
                for s in range(2):
                    ends = []
                    for f in range(2):
                        here = tall_iota == tall_at[4 * s + f : 4 * s + f + 1]
                        at = slice((2 * s + f) * elec, (2 * s + f + 1) * elec)
                        ends.append(rows_sum(jnp.where(here, found[:tall, at] + found[tall:, at], 0.0)))
                    ret_send[t, pl.ds(2 * s + i, 1), :] = ends[0] - ends[1] - recv[t, pl.ds(4 * s + 2 + i, 1), :]
            return carry

        lax.fori_loop(0, n_space // group, step, 0)

    def spread(i):
        scat[...] = jnp.zeros_like(scat)

        def step(u, carry):
            amounts, hots = [], []
            for k in range(group):
                t = u * group + k
                tall_at, _ = split_cells(t)
                misfit = ret_send[t]
                high = misfit.astype(BF16).astype(F32)
                for s in range(2):
                    for f in range(2):
                        sign = 1.0 if f == 0 else -1.0
                        row = jnp.broadcast_to(tall_at[4 * s + f : 4 * s + f + 1], (tall, elec)).astype(BF16)
                        here = tall_iota16 == row
                        pieces = []
                        for value in (high, misfit - high):
                            amount = jnp.broadcast_to(sign * value[2 * s + i : 2 * s + i + 1], (tall, elec)).astype(BF16)
                            pieces.append(jnp.where(here, amount, jnp.zeros((tall, elec), BF16)))
                        amounts.append(jnp.concatenate(pieces, axis=0))
                hots.append(onehot[t])
            scat[...] += lax.dot_general(
                jnp.concatenate(amounts, axis=1), jnp.concatenate(hots, axis=1), (((1,), (1,)), ((), ())),
                preferred_element_type=F32,
            )
            return carry

        lax.fori_loop(0, n_space // group, step, 0)
        for x in range(nx):
            first, columns = (x % half) * ny, pl.ds((x // half) * nz, nz)
            asrc[i, H + x] = scat[pl.ds(first, ny), columns] + scat[pl.ds(tall + first, ny), columns]

    rims = [
        [
            remote(pb.at[i, H + nx - 1, rows], rim.at[0, i], rim_send.at[2 * i], rim_recv.at[2 * i], right, my_inj),
            remote(pb.at[i, H, rows], rim.at[1, i], rim_send.at[2 * i + 1], rim_recv.at[2 * i + 1], left, my_inj),
        ]
        for i in range(2)
    ]
    around = [
        [
            remote(
                asrc.at[i, pl.ds(H + nx - 3, 3)], asrc.at[i, pl.ds(1, 3)],
                asrc_send.at[2 * i], asrc_recv.at[2 * i], right, my_inj,
            ),
            remote(
                asrc.at[i, pl.ds(H, 3)], asrc.at[i, pl.ds(H + nx, 3)],
                asrc_send.at[2 * i + 1], asrc_recv.at[2 * i + 1], left, my_inj,
            ),
        ]
        for i in range(2)
    ]

    finish_potential(0)
    for copy in rims[0]:
        copy.start()
    got = pltpu.make_async_copy(recv.at[pl.ds(0, n_space - 1)], recv.at[pl.ds(0, n_space - 1)], block_recv)
    got.wait()
    lax.fori_loop(0, n_space, mark, 0)
    fetch(0)
    finish_potential(1)
    for copy in late + rims[1]:
        copy.start()
    spread(0)
    for copy in around[0]:
        copy.start()
    fetch(1)

    def send_ret(d, carry):
        to = lax.rem(me + d, n_space)
        remote(ret_send.at[to], ret_recv.at[me], ret_send_sem, ret_recv_sem, to, my_inj).start()
        return carry

    lax.fori_loop(1, n_space, send_ret, 0)
    ret_recv[me] = ret_send[me]

    spread(1)
    for copy in around[1]:
        copy.start()

    locals_[2].wait()
    for copy in late:
        copy.wait()
    for low_side in (True, False):
        beyond(sigma, (), low_side, H)
        for i in range(2):
            beyond(aa, (i,), low_side, H)
    faces([1, end - 1])
    for i in range(2):
        for copy in rims[i]:
            copy.wait()
        pb[i, H - 1, rows, :] = jnp.where(me == 0, 0.0, rim[0, i])
        pb[i, H + nx, rows, :] = jnp.where(me == n_space - 1, 0.0, rim[1, i])

    for copy in around[0]:
        copy.wait()
    sweep(0, asrc, aa, ab, range(1, planes - 1), w0)
    sweep(0, asrc, ab, aa, range(2, planes - 2), w1)
    sweep(0, asrc, aa, ab, range(3, planes - 3), w2)
    sweep(1, asrc, aa, ab, range(H, H + nx), w0)
    sweep(1, asrc, ab, aa, range(H + 1, end - H), w1)
    sweep(1, asrc, aa, ab, range(H + 2, end - H - 1), w2)

    def term(i, side):
        def work(low, at):
            part = ny // n_inj
            where = pl.ds(low // part, chunk // part)
            for x in range(half):
                p = H + side * half + x
                here, there = pb[i, p, at, :], ab[i, p, at, :]
                ahead, behind = pl.ds(low + PAD + 1, chunk), pl.ds(low + PAD - 1, chunk)
                pairs = [
                    (pb[i, p + 1, at, :], ab[i, p + 1, at, :]),
                    (pb[i, p - 1, at, :], ab[i, p - 1, at, :]),
                    (pb[i, p, ahead, :], ab[i, p, ahead, :]),
                    (pb[i, p, behind, :], ab[i, p, behind, :]),
                    (next_z(here), next_z(there)),
                    (last_z(here), last_z(there)),
                ]
                total = jnp.zeros((chunk, nz), F32)
                for u, v in pairs:
                    total = total + (here - u) * (there - v)
                total = (-0.5 * total).reshape(chunk // part, part, nz)
                partial[side, where, x] = total if i == 0 else partial[side, where, x] + total

        in_chunks(work)

    def send_share(side):
        def step(d, carry):
            to = lax.rem(my_inj + d, n_inj)
            remote(
                partial.at[side, to], shares.at[side, my_inj], share_send.at[side], share_recv.at[side], me, to
            ).start()
            return carry

        lax.fori_loop(1, n_inj, step, 0)
        shares[side, my_inj] = partial[side, my_inj]

    term(0, 0)
    term(0, 1)
    around[1][0].wait()
    sweep(1, asrc, aa, ab, [1, 2, 3], w0)
    sweep(1, asrc, ab, aa, [2, 3, 4], w1)
    sweep(1, asrc, aa, ab, [3, 4, 5], w2)
    term(1, 0)
    send_share(0)
    around[1][1].wait()
    sweep(1, asrc, aa, ab, [end - 3, end - 2, end - 1], w0)
    sweep(1, asrc, ab, aa, [end - 4, end - 3, end - 2], w1)
    sweep(1, asrc, aa, ab, [end - 5, end - 4, end - 3], w2)
    term(1, 1)
    send_share(1)

    ret_got = pltpu.make_async_copy(ret_recv.at[pl.ds(0, n_space - 1)], ret_recv.at[pl.ds(0, n_space - 1)], ret_recv_sem)
    ret_got.wait()
    lane_j = lax.rem(iota((1, lanes), 1), 2).astype(F32)
    back = jnp.where(iota((n_space * 4, lanes), 0).astype(F32) == slot_c * 2.0 + lane_j, 1.0, 0.0)
    back = jnp.transpose(back)[: 2 * blocks]
    returned = jnp.concatenate([ret_recv[t] for t in range(n_space)], axis=0)
    res_out[...] = jnp.dot(back, returned, precision=HIGHEST, preferred_element_type=F32)

    for side in range(2):
        window = shares.at[side, pl.ds(0, n_inj - 1)]
        pltpu.make_async_copy(window, window, share_recv.at[side]).wait()
        total = shares[side, 0]
        for k in range(1, n_inj):
            total = total + shares[side, k]
        grad_out[pl.ds(side * half, half)] = total

    pltpu.make_async_copy(send.at[pl.ds(0, n_space - 1)], send.at[pl.ds(0, n_space - 1)], block_send).wait()
    pltpu.make_async_copy(ret_send.at[pl.ds(0, n_space - 1)], ret_send.at[pl.ds(0, n_space - 1)], ret_send_sem).wait()
    for side in range(2):
        window = partial.at[side, pl.ds(0, n_inj - 1)]
        pltpu.make_async_copy(window, window, share_send.at[side]).wait()


def body(
    conductivity, start_potential, start_adjoint, inj_cells, dipole_cells, owner_tile, live_count, observed,
):
    n_space, n_inj = lax.axis_size("space"), lax.axis_size("inj")
    nx, ny, nz = conductivity.shape
    blocks, elec = observed.shape[1], observed.shape[3]
    planes, tall_rows = nx + 2 * H, ny + 2 * PAD
    wide, tall = 2 * nz, nx // 2 * ny
    hbm = pl.BlockSpec(memory_space=pltpu.HBM)
    vmem = pl.BlockSpec(memory_space=pltpu.VMEM)
    field = pltpu.VMEM((2, planes, tall_rows, nz), F32)
    dma = pltpu.SemaphoreType.DMA
    gradient, residual = pl.pallas_call(
        functools.partial(kernel, n_space, n_inj, nx, ny, nz, blocks),
        out_shape=(
            pltpu.VMEM((nx, ny // n_inj, nz), F32),
            pltpu.VMEM((2 * blocks, elec), F32),
        ),
        in_specs=[hbm] * 8,
        out_specs=(vmem, vmem),
        scratch_shapes=[
            pltpu.SMEM((2, 2), jnp.int32),
            pltpu.VMEM((1, blocks), jnp.int32),
            pltpu.VMEM((1, blocks), jnp.int32),
            pltpu.VMEM((2 * blocks, elec), jnp.int32),
            pltpu.VMEM((2 * blocks, elec), F32),
            pltpu.VMEM((planes, tall_rows, nz), F32),
            field, field, field, field,
            pltpu.VMEM((7, planes, ny, nz), F32),
            pltpu.VMEM((2, planes, ny, nz), F32),
            pltpu.VMEM((2, planes, ny, nz), F32),
            pltpu.VMEM((n_space, 8, elec), F32),
            pltpu.VMEM((n_space, 8, elec), F32),
            pltpu.VMEM((n_space, 4, elec), F32),
            pltpu.VMEM((n_space, 4, elec), F32),
            pltpu.VMEM((2, 2, ny, nz), F32),
            pltpu.VMEM((n_space, wide, 4 * elec), BF16),
            pltpu.VMEM((2, 2 * tall, wide), BF16),
            pltpu.VMEM((2 * tall, wide), F32),
            pltpu.VMEM((2, n_inj, nx // 2, ny // n_inj, nz), F32),
            pltpu.VMEM((2, n_inj, nx // 2, ny // n_inj, nz), F32),
            dma((8,)), dma((6,)), dma((6,)), dma((4,)), dma((4,)), dma, dma,
            dma, dma, dma((4,)), dma((4,)), dma((4,)), dma((4,)), dma((2,)), dma((2,)),
        ],
        compiler_params=pltpu.CompilerParams(
            collective_id=0, has_side_effects=True, vmem_limit_bytes=60 * 1024 * 1024
        ),
    )(
        conductivity, start_potential, start_adjoint, inj_cells,
        owner_tile.reshape(1, blocks), live_count,
        dipole_cells.reshape(2 * blocks, elec), observed.reshape(2 * blocks, elec),
    )
    return gradient, residual.reshape(1, blocks, 2, elec)


def solution(mesh):
    return jax.shard_map(
        body,
        mesh=mesh,
        in_specs=(
            P("space", None, None),
            P("inj", "space", None, None),
            P("inj", "space", None, None),
            P("inj", None),
            P("inj", "space", None, None),
            P("inj", "space", None),
            P("inj", "space"),
            P("inj", "space", None, None),
        ),
        out_specs=(P("space", "inj", None), P("inj", "space", None, None)),
        check_vma=False,
    )
```
